32 devices in a mesh: seq: 8 (over z, y), head: 4 (over x, core).
Axes of the slice: x: 2, y: 2, z: 4, core: 2. Of those that a mesh axis runs over, the one named last changes fastest.
Arguments:
- query: bfloat16 [4096, 2048], P('seq', 'head'), may hold values from -6 to 6
- keys: bfloat16 [4096, 2048], P('seq', 'head'), may hold values from -6 to 6
- values: bfloat16 [4096, 4096], P('seq', 'head'), may hold values from -6 to 6
- gate_logit: float32 [4096, 32], P('seq', 'head'), may hold values from -17 to 1.5
- beta_logit: float32 [4096, 32], P('seq', 'head'), may hold values from -9 to 6
- decay_rate: float32 [32], P('head'), may hold values from 0.5 to 8
- norm_gain: float32 [128], replicated, may hold values from 0.1 to 1.9
- gate_z: bfloat16 [4096, 4096], P('seq', 'head'), may hold values from -6 to 6
- out_weight: bfloat16 [4096, 2048], P('head'), may hold values from -0.09375 to 0.09375
Outputs:
- mixed: bfloat16 [4096, 2048], P(('seq', 'head'))
The draws below stay inside these ranges and needn't reach their ends.
All inputs are finite; a program needn't handle non-finite values.
Results may differ from the reference program's by a relative error of at most 0.014.
Values may be sent and summed in bfloat16 or wider, within the bound.
No kernel may reach another device: no remote copies, remote signals or barrier semaphores. Data moves between devices by JAX's collectives and lax.ppermute only.
A program may use at most 128 MiB of HBM per device.

```python
import math
import jax
import jax.numpy as jnp
from jax import lax

D = 2048
VALUE_HEADS = 32
DK = 128
DV = 128
SPAN = 64
HK = 16
SEQUENCE_TOKENS = 4096


def head_plan(key):
    chosen = jax.random.uniform(jax.random.fold_in(key, 101), (VALUE_HEADS,), jnp.float32)
    slow_heads = chosen < 0.5
    head_rates = jnp.exp(jax.random.uniform(jax.random.fold_in(key, 102), (VALUE_HEADS,), jnp.float32, math.log(0.5), math.log(8.0)))
    return (slow_heads, head_rates)


def jitter(key):
    return jnp.clip(0.6 * jax.random.normal(key, (SEQUENCE_TOKENS, VALUE_HEADS), jnp.float32), -1.5, 1.5)


def draw_decay_rate(key, part):
    slow_heads, head_rates = head_plan(key)
    return head_rates


def draw_gate_logit(key, part):
    slow_heads, head_rates = head_plan(key)
    spread_part = jitter(jax.random.fold_in(key, 103))
    phases = jax.random.uniform(jax.random.fold_in(key, 104), (VALUE_HEADS,), jnp.float32, 0.0, 2.0 * math.pi)
    position = jnp.arange(SEQUENCE_TOKENS, dtype=jnp.float32)[:, None] / SEQUENCE_TOKENS
    drift = 0.7 * jnp.sin(2.0 * math.pi * 3.0 * position + phases[None, :])
    base_amount = jnp.where(slow_heads, 0.3 / SEQUENCE_TOKENS, 1.0 / 40.0)
    shift_amount = base_amount[None, :] * jnp.exp(spread_part + drift)
    spike_position = jax.random.randint(jax.random.fold_in(key, 105), (2, VALUE_HEADS), 0, SEQUENCE_TOKENS, dtype=jnp.int32)
    token_positions = jnp.arange(SEQUENCE_TOKENS, dtype=jnp.int32)[:, None, None]
    spike_matches = jnp.any(token_positions == spike_position[None, :, :], axis=1)
    spike_magnitude = jax.random.uniform(jax.random.fold_in(key, 106), (SEQUENCE_TOKENS, VALUE_HEADS), jnp.float32, 0.22, 0.69)
    shift_amount = jnp.where(spike_matches, spike_magnitude, shift_amount)
    return jnp.log(jnp.expm1(shift_amount / head_rates[None, :]))


def draw_beta_logit(key, part):
    slow_heads, head_rates = head_plan(key)
    spread_part = jitter(jax.random.fold_in(key, 107))
    slow_beta = 0.4 * DK / SEQUENCE_TOKENS * jnp.exp(spread_part)
    slow_logit = jnp.log(slow_beta) - jnp.log1p(-slow_beta)
    fast_logit = jnp.clip(0.5 + 1.5 * jax.random.normal(jax.random.fold_in(key, 108), (SEQUENCE_TOKENS, VALUE_HEADS), jnp.float32), -5.0, 6.0)
    return jnp.where(slow_heads[None, :], slow_logit, fast_logit)


def block_levels(key, shape, shards, smallest, largest):
    factor_of, own = 1.0, jax.random.fold_in(key, 6)
    for axis_at, shards_of in shards:
        heights = jnp.exp(jax.random.uniform(jax.random.fold_in(own, axis_at), (shards_of,), jnp.float32, smallest / len(shards), largest / len(shards)))
        factor_of = factor_of * jnp.repeat(heights, shape[axis_at] // shards_of).reshape([-1 if axis == axis_at else 1 for axis in range(len(shape))])
    return factor_of


def noise(stream_key, shape, scale, bound, split=(), kind=jnp.bfloat16):
    array = jax.random.normal(stream_key, shape, jnp.float32) * scale
    if len(split) > 0:
        array = block_levels(stream_key, shape, split, -0.22, 0.18) * array
    return jnp.clip(array, min=-bound, max=bound).astype(kind)


def setup_inputs(seed: int = 0) -> dict:
    streams_of = jax.random.split(jax.random.key(seed), 10)
    query = noise(streams_of[0], (SEQUENCE_TOKENS, HK * DK), 1.0, 6.0, ((0, 8), (1, 4)))
    keys = noise(streams_of[1], (SEQUENCE_TOKENS, HK * DK), 1.0, 6.0, ((0, 8), (1, 4)))
    values = noise(streams_of[2], (SEQUENCE_TOKENS, VALUE_HEADS * DV), 1.0, 6.0, ((0, 8), (1, 4)))
    gate_logit = draw_gate_logit(jax.random.fold_in(streams_of[9], 71), 0)
    beta_logit = draw_beta_logit(jax.random.fold_in(streams_of[9], 71), 0)
    decay_rate = draw_decay_rate(jax.random.fold_in(streams_of[9], 71), 0)
    norm_gain = jnp.clip(1.0 + 0.18 * jax.random.normal(streams_of[6], (DV,), jnp.float32), 0.1, 1.9)
    gate_z = noise(streams_of[7], (SEQUENCE_TOKENS, VALUE_HEADS * DV), 1.0, 6.0, ((0, 8), (1, 4)))
    out_weight = noise(streams_of[8], (VALUE_HEADS * DV, D), (VALUE_HEADS * DV) ** -0.5, 0.09375, ((0, 4),))
    return {"query": query, "keys": keys, "values": values, "gate_logit": gate_logit, "beta_logit": beta_logit, "decay_rate": decay_rate, "norm_gain": norm_gain, "gate_z": gate_z, "out_weight": out_weight}


def unit_norm(values_in):
    return values_in * lax.rsqrt(lax.optimization_barrier(jnp.sum(values_in * values_in, axis=-1, keepdims=True)) + 1e-06)

def block_terms(query, keys, values, logdecay, beta):
    highest = lax.Precision.HIGHEST
    size = logdecay.shape[-1]
    width = keys.shape[-1]
    cumul = jnp.cumsum(logdecay, axis=-1)
    differ = cumul[..., :, None] - cumul[..., None, :]
    row_ids = lax.broadcasted_iota(jnp.int32, (size, size), 0)
    col_ids = lax.broadcasted_iota(jnp.int32, (size, size), 1)
    inclusive = col_ids <= row_ids
    strict = col_ids < row_ids
    ratio = jnp.where(inclusive, jnp.exp(jnp.where(inclusive, differ, 0.0)), 0.0)
    key_key = jnp.einsum('...te,...se->...ts', keys, keys, precision=highest)
    query_key = jnp.einsum('...te,...se->...ts', query, keys, precision=highest)
    lower = jnp.where(strict, beta[..., :, None] * ratio * key_key, 0.0) + jnp.eye(size, dtype=jnp.float32)
    rhs_values = beta[..., None] * values
    rhs_keys = (beta * jnp.exp(cumul))[..., None] * keys
    update = lax.linalg.triangular_solve(lower, rhs_values, left_side=True, lower=True, unit_diagonal=True)
    weights = lax.linalg.triangular_solve(lower, rhs_keys, left_side=True, lower=True, unit_diagonal=True)
    mixing = ratio * query_key
    decayed_query = jnp.exp(cumul)[..., None] * query
    key_end = jnp.exp(cumul[..., -1:] - cumul)[..., None] * keys
    transit = jnp.exp(cumul[..., -1])[..., None, None] * jnp.eye(width, dtype=jnp.float32)
    transit = transit - jnp.einsum('...se,...sf->...ef', key_end, weights, precision=highest)
    inject = jnp.einsum('...se,...sf->...ef', key_end, update, precision=highest)
    return (update, weights, mixing, decayed_query, transit, inject)

def run_blocks(terms, start):
    highest = lax.Precision.HIGHEST

    def advance(state, item):
        update, weights, mixing, decayed_query, transit, inject = item
        resid = update - jnp.einsum('...ce,...ef->...cf', weights, state, precision=highest)
        result = jnp.einsum('...ce,...ef->...cf', decayed_query, state, precision=highest)
        result = result + jnp.einsum('...ts,...sf->...tf', mixing, resid, precision=highest)
        state = jnp.einsum('...ef,...fg->...eg', transit, state, precision=highest) + inject
        return (state, result)
    return lax.scan(advance, start, terms)

def reference(query, keys, values, gate_logit, beta_logit, decay_rate, norm_gain, gate_z, out_weight):
    tokens = query.shape[0]
    blocks = tokens // SPAN
    qn = unit_norm(query.astype(jnp.float32).reshape(tokens, HK, DK))
    kn = unit_norm(keys.astype(jnp.float32).reshape(tokens, HK, DK))
    qn = jnp.repeat(qn, 2, axis=1).transpose(1, 0, 2)
    kn = jnp.repeat(kn, 2, axis=1).transpose(1, 0, 2)
    vals = values.astype(jnp.float32).reshape(tokens, VALUE_HEADS, DV).transpose(1, 0, 2)
    logdecay = (-decay_rate[None, :] * jax.nn.softplus(gate_logit)).T
    beta = jax.nn.sigmoid(beta_logit).T

    def one_head(item):
        q_head, k_head, v_head, d_head, b_head = item
        terms = block_terms(q_head.reshape(blocks, SPAN, DK), k_head.reshape(blocks, SPAN, DK), v_head.reshape(blocks, SPAN, DV), d_head.reshape(blocks, SPAN), b_head.reshape(blocks, SPAN))
        final, outs = run_blocks(terms, jnp.zeros((DK, DV), jnp.float32))
        return outs.reshape(tokens, DV)
    core = lax.map(one_head, (qn, kn, vals, logdecay, beta)).transpose(1, 0, 2)
    gate = jax.nn.silu(gate_z.astype(jnp.float32).reshape(tokens, VALUE_HEADS, DV))
    scale = lax.rsqrt(lax.optimization_barrier(jnp.mean(core * core, axis=-1, keepdims=True)) + 1e-06)
    gated = (core * scale * norm_gain * gate).astype(jnp.bfloat16).reshape(tokens, VALUE_HEADS * DV)
    return jnp.dot(gated.astype(jnp.float32), out_weight.astype(jnp.float32), preferred_element_type=jnp.float32).astype(jnp.bfloat16)
```

```python
import functools

import jax
import jax.numpy as jnp
from jax import lax
from jax.experimental import pallas as pl
from jax.experimental.pallas import tpu as pltpu
from jax.sharding import PartitionSpec as P

DK = 128
DV = 128
CHUNK = 256
F32 = jnp.float32
BF16 = jnp.bfloat16
NEG = -1e30
VMEM_BYTES = 56 * 1024 * 1024


def mm(left, right):
    return lax.dot_general(left, right, (((1,), (0,)), ((), ())), preferred_element_type=F32)


def mm_nt(left, right):
    return lax.dot_general(left, right, (((1,), (1,)), ((), ())), preferred_element_type=F32)


def iota(shape, dim):
    return lax.broadcasted_iota(jnp.int32, shape, dim)


def split3(x):
    hi = x.astype(BF16).astype(F32)
    mid = (x - hi).astype(BF16).astype(F32)
    return hi, mid, x - hi - mid


def softplus(x):
    small = jnp.exp(-jnp.abs(x))
    one = 1.0 + small
    log1p = jnp.where(one == 1.0, small, jnp.log(one) * (small / jnp.where(one == 1.0, 1.0, one - 1.0)))
    return jnp.maximum(x, 0.0) + log1p


def rows_of(pick, array):
    total = None
    for part in split3(array):
        term = mm_nt(pick, part.astype(BF16))
        total = term if total is None else total + term
    return total


def log_inverse_norm(x):
    square = x.astype(F32) * x.astype(F32)
    high = square.astype(BF16)
    low = (square - high.astype(F32)).astype(BF16)
    ones = jnp.ones((8, x.shape[1]), BF16)
    return -0.5 * jnp.log(mm_nt(ones, high) + mm_nt(ones, low) + 1e-6)


def odd_rows(x, n):
    return jnp.concatenate([x[i + n : i + 2 * n] for i in range(0, x.shape[0], 2 * n)], axis=0)


def weave(x, odd, n):
    parts = []
    for at in range(0, odd.shape[0], n):
        parts.append(x[2 * at : 2 * at + n])
        parts.append(odd[at : at + n])
    return jnp.concatenate(parts, axis=0)


def unit_lower_inverse(lower):
    size = lower.shape[0]
    half = size // 2
    row, col = iota((size, size), 0), iota((size, size), 1)
    crow, ccol = iota((half, size), 0), iota((half, size), 1)
    zeros = jnp.zeros((size, size), F32)
    pair = (row // 2 == col // 2)
    x = jnp.where(row == col, 1.0, jnp.where(pair, -lower, 0.0))
    n = 2
    while n < size:
        xb = x.astype(BF16)
        if n < 8:
            below = (row // n == col // n + 1) & (row // (2 * n) == col // (2 * n))
            b = jnp.where(below, lower, 0.0).astype(BF16)
            x = x - mm(xb, mm(b, xb).astype(BF16))
        elif n < half:
            b = jnp.where(ccol // n == 2 * (crow // n), odd_rows(lower, n), 0.0).astype(BF16)
            y = mm(b, xb)
            x_odd = odd_rows(x, n)
            z = mm(x_odd.astype(BF16), weave(zeros, y, n).astype(BF16))
            x = weave(x, x_odd - z, n)
        else:
            y = mm(lower[half:, :half].astype(BF16), xb[:half, :half])
            z = mm(xb[half:, half:], y.astype(BF16))
            low = jnp.concatenate([-z, x[half:, half:]], axis=1)
            x = jnp.concatenate([x[:half], low], axis=0)
        n *= 2
    return x


def local_kernel(first_ref, q_ref, k_ref, v_ref, gate_ref, beta_ref, rate_ref, *rest):
    ends_ref, out_ref, gain_ref = rest[-3:]
    tokens = q_ref.shape[0]
    heads = gate_ref.shape[1]
    key_head = first_ref[0] + pl.program_id(0)
    q_all, k_all = q_ref[...], k_ref[...]

    pick = iota((8, heads), 1) == 2 * key_head + iota((8, heads), 0)
    rate = jnp.sum(jnp.where(pick, rate_ref[...], 0.0), axis=1, keepdims=True)
    pick = jnp.where(pick, 1.0, 0.0).astype(BF16)
    decay = -rate * softplus(rows_of(pick, gate_ref[...]))
    log_beta = -softplus(-rows_of(pick, beta_ref[...]))
    log_k, log_q = log_inverse_norm(k_all), log_inverse_norm(q_all)

    row, col = iota((CHUNK, CHUNK), 0), iota((CHUNK, CHUNK), 1)
    upto = jnp.where(row <= col, 1.0, 0.0).astype(BF16)
    state = [None, None]
    for at in range(0, tokens, CHUNK):
        here = slice(at, at + CHUNK)
        q, k, v = q_all[here], k_all[here], v_ref[here, :]
        parts = mm(jnp.concatenate(split3(decay[:, here]), axis=0).astype(BF16), upto)
        cumul = parts[:8] + parts[8:16] + parts[16:]
        end = cumul[:, CHUNK - 1 :]
        lb, lk, lq = log_beta[:, here], log_k[:, here], log_q[:, here]
        col_log = cumul - lk
        row_lower = cumul + lb + lk
        row_mix = cumul + lq
        key_end = jnp.exp(end - cumul + lk)
        columns = jnp.concatenate(
            [row_lower, row_mix, jnp.exp(lb), jnp.exp(row_lower), jnp.exp(row_mix)], axis=0
        ).T
        turned = k.astype(F32).T
        turned_b = turned.astype(BF16)
        key_key = mm(k, turned_b)
        query_key = mm(q, turned_b)
        k32, q32 = k.astype(F32), q.astype(F32)
        for r in range(2):
            c_lower, c_mix, c_beta, c_weight, c_query = (
                columns[:, 8 * i + r : 8 * i + r + 1] for i in range(5)
            )
            b_row = col_log[r : r + 1]
            lower = jnp.exp(jnp.where(col < row, c_lower - b_row, NEG)) * key_key
            mixing = (jnp.exp(jnp.where(col <= row, c_mix - b_row, NEG)) * query_key).astype(BF16)
            inverse = unit_lower_inverse(lower).astype(BF16)
            v32 = v[:, r * DV : (r + 1) * DV].astype(F32)
            rhs = jnp.concatenate([c_beta * v32, c_weight * k32], axis=1).astype(BF16)
            solved = mm(inverse, rhs)
            update, weights = solved[:, :DV], solved[:, DV:]
            q_decayed = c_query * q32
            k_ended = (turned * key_end[r : r + 1]).astype(BF16)
            e = jnp.exp(end[r : r + 1])
            if state[r] is None:
                resid = jnp.concatenate([update, -weights], axis=1).astype(BF16)
                result = mm(mixing, resid)
                result = jnp.concatenate([result[:, :DV], result[:, DV:] + q_decayed], axis=1)
                eye = jnp.where(iota((DK, DV + DK), 1) == iota((DK, DV + DK), 0) + DV, e, 0.0)
                state[r] = eye + mm(k_ended, resid)
            else:
                held = state[r].astype(BF16)
                moved = mm(weights.astype(BF16), held)
                resid = jnp.concatenate([update - moved[:, :DV], -moved[:, DV:]], axis=1).astype(BF16)
                result = mm(q_decayed.astype(BF16), held) + mm(mixing, resid)
                state[r] = e * state[r] + mm(k_ended, resid)
            out_ref[here, r * DV : (r + 1) * DV] = result[:, :DV]
            gain_ref[here, r * DK : (r + 1) * DK] = result[:, DV:].astype(BF16)
    for r in range(2):
        ends_ref[r] = state[r].astype(BF16)


def local_part(first, groups, query, keys, values, gate_logit, beta_logit, rate, earlier):
    tokens, heads = gate_logit.shape
    whole = lambda i, first: (0, 0)
    mine = lambda i, first: (0, first[0] + i)
    in_specs = [
        pl.BlockSpec((tokens, DK), mine),
        pl.BlockSpec((tokens, DK), mine),
        pl.BlockSpec((tokens, 2 * DV), mine),
        pl.BlockSpec((tokens, heads), whole),
        pl.BlockSpec((tokens, heads), whole),
        pl.BlockSpec((1, heads), whole),
    ]
    args = [first, query, keys, values, gate_logit, beta_logit, rate]
    aliases = {}
    if earlier is not None:
        in_specs += [pl.BlockSpec(memory_space=pl.ANY)] * 2
        aliases = {len(args): 1, len(args) + 1: 2}
        args += list(earlier)
    return pl.pallas_call(
        local_kernel,
        grid_spec=pltpu.PrefetchScalarGridSpec(
            num_scalar_prefetch=1,
            grid=(groups,),
            in_specs=in_specs,
            out_specs=[
                pl.BlockSpec((2, DK, DV + DK), lambda i, first: (i, 0, 0)),
                pl.BlockSpec((tokens, 2 * DV), mine),
                pl.BlockSpec((tokens, 2 * DK), mine),
            ],
        ),
        out_shape=[
            jax.ShapeDtypeStruct((2 * groups, DK, DV + DK), BF16),
            jax.ShapeDtypeStruct((tokens, heads * DV), F32),
            jax.ShapeDtypeStruct((tokens, heads * DK), BF16),
        ],
        input_output_aliases=aliases,
        compiler_params=pltpu.CompilerParams(vmem_limit_bytes=VMEM_BYTES),
        cost_estimate=pl.CostEstimate(
            flops=groups * 4 * 14 * 2 * CHUNK**3, bytes_accessed=groups * 2**20, transcendentals=0
        ),
        name="local_part",
    )(*args)


def small_call(kernel, flag, arrays, out_shapes, flops):
    return pl.pallas_call(
        kernel,
        in_specs=[pl.BlockSpec(memory_space=pltpu.SMEM)]
        + [pl.BlockSpec(memory_space=pltpu.VMEM)] * len(arrays),
        out_specs=[pl.BlockSpec(memory_space=pltpu.VMEM)] * len(out_shapes),
        out_shape=[jax.ShapeDtypeStruct(s, BF16) for s in out_shapes],
        cost_estimate=pl.CostEstimate(flops=flops, bytes_accessed=2**18, transcendentals=0),
        name=kernel.__name__.strip("_"),
    )(flag, *arrays)


def pair_kernel(upper_ref, own_ref, other_ref, pair_ref):
    upper = upper_ref[0] == 1
    for h in range(own_ref.shape[0]):
        own, other = own_ref[h].astype(F32), other_ref[h].astype(F32)
        one = jnp.where(upper, other, own)
        two = jnp.where(upper, own, other)
        both = mm(two[:, DV:].astype(BF16), one.astype(BF16))
        pair_ref[h] = jnp.concatenate([both[:, :DV] + two[:, :DV], both[:, DV:]], axis=1).astype(BF16)


def hop_kernel(upper_ref, pair_ref, held_ref, came_ref, sum_ref, out_ref):
    for h in range(pair_ref.shape[0]):
        start = held_ref[h] + came_ref[h]
        sum_ref[h] = start
        pair = pair_ref[h]
        out_ref[h] = (mm(pair[:, DV:], start) + pair[:, :DV].astype(F32)).astype(BF16)


def middle_kernel(upper_ref, own_ref, other_ref, held_ref, came_ref, keep_ref, send_ref):
    upper = upper_ref[0] == 1
    for h in range(own_ref.shape[0]):
        start = held_ref[h] + came_ref[h]
        one = jnp.where(upper, other_ref[h].astype(F32), own_ref[h].astype(F32))
        middle = mm(one[:, DV:].astype(BF16), start) + one[:, :DV]
        start = start.astype(F32)
        keep_ref[h] = jnp.where(upper, middle, start).astype(BF16)
        send_ref[h] = jnp.where(upper, start, middle).astype(BF16)


def project_kernel(
    place_ref, out_ref, gain_ref, z_ref, keep_ref, came_ref, norm_ref, w_ref, send_ref, stay_ref, gated_ref
):
    heads = z_ref.shape[1] // DV
    half = heads // 2
    upper = place_ref[2]
    ones = jnp.full((DV, DV), 1.0 / DV, BF16)
    for h in range(heads):
        at = slice(h * DV, (h + 1) * DV)
        kept = keep_ref[h % half].astype(F32)
        came = came_ref[h % half].astype(F32)
        start = jnp.where(upper == h // half, kept, came).astype(BF16)
        core = out_ref[:, at] + mm(gain_ref[:, at], start)
        square = core * core
        high = square.astype(BF16)
        low = (square - high.astype(F32)).astype(BF16)
        mean = mm(high, ones) + mm(low, ones)
        z = z_ref[:, at].astype(F32)
        gate = z / (1.0 + jnp.exp(-z))
        gated_ref[:, at] = (core * lax.rsqrt(mean + 1e-6) * norm_ref[...] * gate).astype(BF16)
    partial = mm(gated_ref[...], w_ref[...])

    @pl.when(pl.program_id(0) == 0)
    def _():
        send_ref[...] = partial.astype(BF16)

    @pl.when(pl.program_id(0) == 1)
    def _():
        stay_ref[...] = partial


def project_part(place, rows, out, gain, z, keep, came, norm_gain, weight):
    width = z.shape[1]
    wide = weight.shape[1]
    half = keep.shape[0]

    def block(i, place):
        return (2 * place[0] + jnp.where(i == 0, 1 - place[1], place[1]), 0)

    fixed = lambda i, place: (0, 0)
    return pl.pallas_call(
        project_kernel,
        grid_spec=pltpu.PrefetchScalarGridSpec(
            num_scalar_prefetch=1,
            grid=(2,),
            in_specs=[
                pl.BlockSpec((rows, width), block),
                pl.BlockSpec((rows, width), block),
                pl.BlockSpec((rows, width), block),
                pl.BlockSpec((half, DK, DV), lambda i, place: (0, 0, 0)),
                pl.BlockSpec((half, DK, DV), lambda i, place: (0, 0, 0)),
                pl.BlockSpec((1, DV), fixed),
                pl.BlockSpec(weight.shape, fixed),
            ],
            out_specs=[pl.BlockSpec((rows, wide), fixed)] * 2,
            scratch_shapes=[pltpu.VMEM((rows, width), BF16)],
        ),
        out_shape=[
            jax.ShapeDtypeStruct((rows, wide), BF16),
            jax.ShapeDtypeStruct((rows, wide), F32),
        ],
        compiler_params=pltpu.CompilerParams(vmem_limit_bytes=VMEM_BYTES),
        cost_estimate=pl.CostEstimate(
            flops=2 * rows * 2 * width * wide, bytes_accessed=2 * weight.size, transcendentals=0
        ),
        name="project_part",
    )(place, out, gain, z, keep, came, norm_gain, weight)


def on_device(
    query, keys, values, gate_logit, beta_logit, decay_rate, norm_gain, gate_z, out_weight
):
    shards, cores = lax.axis_size("seq"), lax.axis_size("head")
    seq, head = lax.axis_index("seq"), lax.axis_index("head")
    key_heads = query.shape[1] // DK
    groups = key_heads // 2
    half = 2 * groups
    upper = lax.rem(seq, 2)
    flag = upper.reshape(1)
    rate = decay_rate.reshape(1, -1)
    arrays = (query, keys, values, gate_logit, beta_logit, rate)

    away, out, gain = local_part(((1 - upper) * groups).reshape(1), groups, *arrays, None)
    other = lax.ppermute(away, "seq", [(s, s ^ 1) for s in range(shards)])
    own, out, gain = local_part((upper * groups).reshape(1), groups, *arrays, (out, gain))

    state = (half, DK, DV)
    pair = small_call(pair_kernel, flag, (own, other), [own.shape], half * 2**23)[0]
    held = jnp.zeros(state, BF16)
    ending = pair[:, :, :DV]
    came = None
    for step in range(shards // 2 - 1):
        if step:
            held, ending = small_call(hop_kernel, flag, (pair, held, came), [state] * 2, half * 2**22)
        came = lax.ppermute(
            ending, "seq", [(2 * step + i, 2 * step + 2 + i) for i in range(2)]
        )
    keep, send = small_call(middle_kernel, flag, (own, other, held, came), [state] * 2, half * 2**22)
    back = lax.ppermute(send, "seq", [(s, s ^ 1) for s in range(shards)])

    chips = cores // 2
    chip, core = head // 2, lax.rem(head, 2)
    rows = query.shape[0] // cores
    norm_gain = norm_gain.reshape(1, -1)
    swap = [(i, i ^ 1) for i in range(cores)]
    arrived = []
    for by in list(range(1, chips)) + [0]:
        target = lax.rem(chip + by, chips)
        place = jnp.stack([target, core, upper])
        give, stay = project_part(
            place, rows, out, gain, gate_z, keep, back, norm_gain, out_weight
        )
        both = stay + lax.ppermute(give, "head", swap).astype(F32)
        if by:
            moves = [(i, (i + 2 * by) % cores) for i in range(cores)]
            arrived.append(lax.ppermute(both.astype(BF16), "head", moves))
    for part in arrived:
        both = both + part.astype(F32)
    return both.astype(BF16)


def solution(mesh):
    return jax.shard_map(
        on_device,
        mesh=mesh,
        in_specs=(
            P("seq", "head"),
            P("seq", "head"),
            P("seq", "head"),
            P("seq", "head"),
            P("seq", "head"),
            P("head"),
            P(),
            P("seq", "head"),
            P("head", None),
        ),
        out_specs=P(("seq", "head"), None),
        check_vma=False,
    )
```

```python
import functools

import jax
import jax.numpy as jnp
from jax import lax
from jax.experimental import pallas as pl
from jax.experimental.pallas import tpu as pltpu
from jax.sharding import PartitionSpec as P

DK = 128
DV = 128
CHUNK = 256
F32 = jnp.float32
BF16 = jnp.bfloat16
NEG = -1e30
LOCAL_VMEM = 60 * 1024 * 1024
PROJECT_VMEM = 32 * 1024 * 1024


def mm(left, right):
    return lax.dot_general(left, right, (((1,), (0,)), ((), ())), preferred_element_type=F32)


def mm_nt(left, right):
    return lax.dot_general(left, right, (((1,), (1,)), ((), ())), preferred_element_type=F32)


def iota(shape, dim):
    return lax.broadcasted_iota(jnp.int32, shape, dim)


def split3(x):
    hi = x.astype(BF16).astype(F32)
    mid = (x - hi).astype(BF16).astype(F32)
    return hi, mid, x - hi - mid


def softplus(x):
    small = jnp.exp(-jnp.abs(x))
    one = 1.0 + small
    log1p = jnp.where(one == 1.0, small, jnp.log(one) * (small / jnp.where(one == 1.0, 1.0, one - 1.0)))
    return jnp.maximum(x, 0.0) + log1p


def log_inverse_norm(x, rows):
    square = x.astype(F32) * x.astype(F32)
    high = square.astype(BF16)
    low = (square - high.astype(F32)).astype(BF16)
    ones = jnp.ones((rows, x.shape[1]), BF16)
    return -0.5 * jnp.log(mm_nt(ones, high) + mm_nt(ones, low) + 1e-6)


def odd_rows(x, n):
    return jnp.concatenate([x[i + n : i + 2 * n] for i in range(0, x.shape[0], 2 * n)], axis=0)


def weave(even, odd, n):
    parts = []
    for at in range(0, odd.shape[0], n):
        parts.append(even[2 * at : 2 * at + n])
        parts.append(odd[at : at + n])
    return jnp.concatenate(parts, axis=0)


def as_mask(where):
    return jnp.where(where, 1.0, 0.0).astype(BF16)


def unit_lower_inverses(lowers):
    size = lowers[0].shape[0]
    half = size // 2
    row, col = iota((size, size), 0), iota((size, size), 1)
    crow, ccol = iota((half, size), 0), iota((half, size), 1)
    zeros = jnp.zeros((size, size), BF16)
    eye, pair = as_mask(row == col), as_mask(row // 2 == col // 2)
    xs = [eye - lower * pair for lower in lowers]
    n = 2
    while n < size:
        if n < 16:
            mask = as_mask((row // n == col // n + 1) & (row // (2 * n) == col // (2 * n)))
            ys = [mm(lower * mask, x).astype(BF16) for lower, x in zip(lowers, xs)]
            zs = [mm(x, y).astype(BF16) for x, y in zip(xs, ys)]
            xs = [x - z for x, z in zip(xs, zs)]
        elif n < half:
            mask = as_mask(ccol // n == 2 * (crow // n))
            ys = [mm(odd_rows(lower, n) * mask, x).astype(BF16) for lower, x in zip(lowers, xs)]
            odds = [odd_rows(x, n) for x in xs]
            zs = [mm(odd, weave(zeros, y, n)).astype(BF16) for odd, y in zip(odds, ys)]
            xs = [weave(x, odd - z, n) for x, odd, z in zip(xs, odds, zs)]
        else:
            ys = [mm(lower[half:, :half], x[:half, :half]).astype(BF16) for lower, x in zip(lowers, xs)]
            zs = [mm(x[half:, half:], y).astype(BF16) for x, y in zip(xs, ys)]
            xs = [
                jnp.concatenate([x[:half], jnp.concatenate([-z, x[half:, half:]], axis=1)], axis=0)
                for x, z in zip(xs, zs)
            ]
        n *= 2
    return xs


def decayed(c, b, product, mask):
    h = CHUNK // 2

    def quarter(i, j):
        arg = c[i * h : (i + 1) * h] - b[:, j * h : (j + 1) * h]
        if i == j:
            arg = jnp.where(mask, arg, NEG)
        return (jnp.exp(arg) * product[i * h : (i + 1) * h, j * h : (j + 1) * h]).astype(BF16)

    top = jnp.concatenate([quarter(0, 0), jnp.zeros((h, h), BF16)], axis=1)
    return jnp.concatenate([top, jnp.concatenate([quarter(1, 0), quarter(1, 1)], axis=1)], axis=0)


def local_kernel(place_ref, q_ref, k_ref, v_ref, gate_ref, beta_ref, rate_ref, *rest):
    ends_ref, out_ref, gain_ref = rest[-3:]
    tokens = q_ref.shape[0]
    heads = gate_ref.shape[0]
    groups = q_ref.shape[1] // DK
    half = heads // 2
    second = place_ref[0] == 1
    chunks = [slice(at, at + CHUNK) for at in range(0, tokens, CHUNK)]
    members = [(g, r) for g in range(groups) for r in range(2)]

    def chosen(x):
        return jnp.where(second, jnp.concatenate([x[half:], x[:half]], axis=0), x)

    decay = -chosen(rate_ref[...]) * softplus(chosen(gate_ref[...]))
    log_beta = -softplus(-chosen(beta_ref[...]))
    head_row = iota((heads, tokens), 0)

    def per_head(ref):
        total = log_inverse_norm(ref[:, :DK], heads)
        for g in range(1, groups):
            more = log_inverse_norm(ref[:, g * DK : (g + 1) * DK], heads)
            total = jnp.where(head_row < 2 * g, total, more)
        return total

    log_k, log_q = per_head(k_ref), per_head(q_ref)

    row, col = iota((CHUNK, CHUNK), 0), iota((CHUNK, CHUNK), 1)
    upto = jnp.where(row <= col, 1.0, 0.0).astype(BF16)
    sums = mm(
        jnp.concatenate([p for here in chunks for p in split3(decay[:, here])], axis=0).astype(BF16), upto
    )
    square = CHUNK // 2
    strict = iota((square, square), 1) < iota((square, square), 0)
    inclusive = iota((square, square), 1) <= iota((square, square), 0)

    lowers, mixings, rights, queries, ended, decays = {}, {}, {}, {}, {}, {}
    for c, here in enumerate(chunks):
        parts = [sums[(3 * c + i) * heads : (3 * c + i + 1) * heads] for i in range(3)]
        cumul = parts[0] + parts[1] + parts[2]
        end = cumul[:, CHUNK - 1 :]
        lb, lk, lq = log_beta[:, here], log_k[:, here], log_q[:, here]
        col_log = cumul - lk
        row_lower = cumul + lb + lk
        row_mix = cumul + lq
        key_end = jnp.exp(end - cumul + lk)
        ends = jnp.exp(end)
        columns = jnp.concatenate(
            [row_lower, row_mix, jnp.exp(lb), jnp.exp(row_lower), jnp.exp(row_mix)], axis=0
        ).T
        for g in range(groups):
            q, k = q_ref[here, g * DK : (g + 1) * DK], k_ref[here, g * DK : (g + 1) * DK]
            q32, k32 = q.astype(F32), k.astype(F32)
            turned = k32.T
            turned_b = turned.astype(BF16)
            key_key = mm(k, turned_b)
            query_key = mm(q, turned_b)
            for r in range(2):
                at = 2 * g + r
                c_lower, c_mix, c_beta, c_weight, c_query = (
                    columns[:, heads * i + at : heads * i + at + 1] for i in range(5)
                )
                b_row = col_log[at : at + 1]
                m = (c, at)
                lowers[m] = decayed(c_lower, b_row, key_key, strict)
                mixings[m] = decayed(c_mix, b_row, query_key, inclusive)
                v32 = v_ref[here, at * DV : (at + 1) * DV].astype(F32)
                rights[m] = jnp.concatenate([c_beta * v32, c_weight * k32], axis=1).astype(BF16)
                queries[m] = c_query * q32
                ended[m] = (turned * key_end[at : at + 1]).astype(BF16)
                decays[m] = ends[at : at + 1]
    names = list(lowers)
    inverses = dict(zip(names, unit_lower_inverses([lowers[m] for m in names])))
    solved = {m: mm(inverses[m], rights[m]) for m in names}
    state = {}
    for c, here in enumerate(chunks):
        all_heads = range(2 * groups)
        if c == 0:
            resid = {a: jnp.concatenate([solved[c, a][:, :DV], -solved[c, a][:, DV:]], axis=1) for a in all_heads}
            resid = {a: resid[a].astype(BF16) for a in all_heads}
            eye = iota((DK, DV + DK), 1) == iota((DK, DV + DK), 0) + DV
            state = {a: jnp.where(eye, decays[c, a], 0.0) + mm(ended[c, a], resid[a]) for a in all_heads}
            result = {a: mm(mixings[c, a], resid[a]) for a in all_heads}
            for a in all_heads:
                out_ref[here, a * DV : (a + 1) * DV] = result[a][:, :DV]
                gain_ref[here, a * DK : (a + 1) * DK] = (result[a][:, DV:] + queries[c, a]).astype(BF16)
        else:
            held = {a: state[a].astype(BF16) for a in all_heads}
            moved = {a: mm(solved[c, a][:, DV:].astype(BF16), held[a]) for a in all_heads}
            resid = {
                a: jnp.concatenate([solved[c, a][:, :DV] - moved[a][:, :DV], -moved[a][:, DV:]], axis=1)
                for a in all_heads
            }
            resid = {a: resid[a].astype(BF16) for a in all_heads}
            state = {a: decays[c, a] * state[a] + mm(ended[c, a], resid[a]) for a in all_heads}
            result = {
                a: mm(queries[c, a].astype(BF16), held[a]) + mm(mixings[c, a], resid[a]) for a in all_heads
            }
            for a in all_heads:
                out_ref[here, a * DV : (a + 1) * DV] = result[a][:, :DV]
                gain_ref[here, a * DK : (a + 1) * DK] = result[a][:, DV:].astype(BF16)
    for a in range(2 * groups):
        ends_ref[a] = state[a].astype(BF16)


def local_part(place, groups, query, keys, values, gate_logit, beta_logit, rate, earlier):
    heads, tokens = gate_logit.shape
    whole = lambda i, place: (0, 0)
    mine = lambda i, place: (0, place[0])
    in_specs = [
        pl.BlockSpec((tokens, groups * DK), mine),
        pl.BlockSpec((tokens, groups * DK), mine),
        pl.BlockSpec((tokens, 2 * groups * DV), mine),
        pl.BlockSpec((heads, tokens), whole),
        pl.BlockSpec((heads, tokens), whole),
        pl.BlockSpec((heads, 1), whole),
    ]
    args = [place, query, keys, values, gate_logit, beta_logit, rate]
    aliases = {}
    if earlier is not None:
        in_specs += [pl.BlockSpec(memory_space=pl.ANY)] * 2
        aliases = {len(args): 1, len(args) + 1: 2}
        args += list(earlier)
    return pl.pallas_call(
        local_kernel,
        grid_spec=pltpu.PrefetchScalarGridSpec(
            num_scalar_prefetch=1,
            grid=(1,),
            in_specs=in_specs,
            out_specs=[
                pl.BlockSpec((2 * groups, DK, DV + DK), lambda i, place: (0, 0, 0)),
                pl.BlockSpec((tokens, 2 * groups * DV), mine),
                pl.BlockSpec((tokens, 2 * groups * DK), mine),
            ],
        ),
        out_shape=[
            jax.ShapeDtypeStruct((2 * groups, DK, DV + DK), BF16),
            jax.ShapeDtypeStruct((tokens, heads * DV), F32),
            jax.ShapeDtypeStruct((tokens, heads * DK), BF16),
        ],
        input_output_aliases=aliases,
        compiler_params=pltpu.CompilerParams(vmem_limit_bytes=LOCAL_VMEM),
        cost_estimate=pl.CostEstimate(
            flops=groups * 4 * 14 * 2 * CHUNK**3, bytes_accessed=groups * 2**20, transcendentals=0
        ),
        name="local_part",
    )(*args)


def small_call(kernel, flag, arrays, out_shapes, flops):
    return pl.pallas_call(
        kernel,
        in_specs=[pl.BlockSpec(memory_space=pltpu.SMEM)]
        + [pl.BlockSpec(memory_space=pltpu.VMEM)] * len(arrays),
        out_specs=[pl.BlockSpec(memory_space=pltpu.VMEM)] * len(out_shapes),
        out_shape=[pltpu.MemorySpace.VMEM(s, BF16) for s in out_shapes],
        cost_estimate=pl.CostEstimate(flops=flops, bytes_accessed=2**18, transcendentals=0),
        name=kernel.__name__.strip("_"),
    )(flag, *[pltpu.with_memory_space_constraint(a, pltpu.VMEM) for a in arrays])


def pair_kernel(upper_ref, own_ref, other_ref, pair_ref):
    upper = upper_ref[0] == 1
    for h in range(own_ref.shape[0]):
        own, other = own_ref[h].astype(F32), other_ref[h].astype(F32)
        one = jnp.where(upper, other, own)
        two = jnp.where(upper, own, other)
        both = mm(two[:, DV:].astype(BF16), one.astype(BF16))
        pair_ref[h] = jnp.concatenate([both[:, :DV] + two[:, :DV], both[:, DV:]], axis=1).astype(BF16)


def hop_kernel(upper_ref, pair_ref, held_ref, came_ref, sum_ref, out_ref):
    for h in range(pair_ref.shape[0]):
        start = held_ref[h] + came_ref[h]
        sum_ref[h] = start
        pair = pair_ref[h]
        out_ref[h] = (mm(pair[:, DV:], start) + pair[:, :DV].astype(F32)).astype(BF16)


def middle_kernel(upper_ref, own_ref, other_ref, held_ref, came_ref, keep_ref, send_ref):
    upper = upper_ref[0] == 1
    for h in range(own_ref.shape[0]):
        start = held_ref[h] + came_ref[h]
        one = jnp.where(upper, other_ref[h].astype(F32), own_ref[h].astype(F32))
        middle = mm(one[:, DV:].astype(BF16), start) + one[:, :DV]
        start = start.astype(F32)
        keep_ref[h] = jnp.where(upper, middle, start).astype(BF16)
        send_ref[h] = jnp.where(upper, start, middle).astype(BF16)


def project_kernel(
    place_ref, out_ref, gain_ref, z_ref, keep_ref, came_ref, norm_ref, w_ref, send_ref, stay_ref
):
    rows = z_ref.shape[0] // 2
    heads = z_ref.shape[1] // DV
    half = heads // 2
    core, upper = place_ref[1], place_ref[2]
    gated = []
    for h in range(heads):
        at = slice(h * DV, (h + 1) * DV)
        kept = keep_ref[h % half].astype(F32)
        came = came_ref[h % half].astype(F32)
        start = jnp.where(upper == h // half, kept, came).astype(BF16)
        core_out = out_ref[:, at] + mm(gain_ref[:, at], start)
        mean = jnp.mean(core_out * core_out, axis=1, keepdims=True)
        z = z_ref[:, at].astype(F32)
        gate = z / (1.0 + jnp.exp(-z))
        gated.append((core_out * lax.rsqrt(mean + 1e-6) * norm_ref[...] * gate).astype(BF16))
    gated = jnp.concatenate(gated, axis=1)
    wide = w_ref.shape[1]
    step = min(wide, 512)
    for at in range(0, wide, step):
        partial = mm(gated, w_ref[:, at : at + step])
        one, two = partial[:rows], partial[rows:]
        send_ref[:, at : at + step] = jnp.where(core == 0, two, one).astype(BF16)
        stay_ref[:, at : at + step] = jnp.where(core == 0, one, two)


def project_part(place, rows, out, gain, z, keep, came, norm_gain, weight):
    width = z.shape[1]
    wide = weight.shape[1]
    half = keep.shape[0]
    block = lambda i, place: (place[0], 0)
    fixed = lambda i, place: (0, 0)
    return pl.pallas_call(
        project_kernel,
        grid_spec=pltpu.PrefetchScalarGridSpec(
            num_scalar_prefetch=1,
            grid=(1,),
            in_specs=[
                pl.BlockSpec((2 * rows, width), block),
                pl.BlockSpec((2 * rows, width), block),
                pl.BlockSpec((2 * rows, width), block),
                pl.BlockSpec((half, DK, DV), lambda i, place: (0, 0, 0)),
                pl.BlockSpec((half, DK, DV), lambda i, place: (0, 0, 0)),
                pl.BlockSpec((1, DV), fixed),
                pl.BlockSpec(weight.shape, fixed),
            ],
            out_specs=[pl.BlockSpec((rows, wide), fixed)] * 2,
        ),
        out_shape=[
            jax.ShapeDtypeStruct((rows, wide), BF16),
            jax.ShapeDtypeStruct((rows, wide), F32),
        ],
        compiler_params=pltpu.CompilerParams(vmem_limit_bytes=PROJECT_VMEM),
        cost_estimate=pl.CostEstimate(
            flops=2 * rows * 2 * width * wide, bytes_accessed=2 * weight.size, transcendentals=0
        ),
        name="project_part",
    )(place, out, gain, z, keep, came, norm_gain, weight)


def on_device(
    query, keys, values, gate_logit, beta_logit, decay_rate, norm_gain, gate_z, out_weight
):
    shards, cores = lax.axis_size("seq"), lax.axis_size("head")
    seq, head = lax.axis_index("seq"), lax.axis_index("head")
    key_heads = query.shape[1] // DK
    groups = key_heads // 2
    half = 2 * groups
    upper = lax.rem(seq, 2)
    flag = upper.reshape(1)
    rate = decay_rate.reshape(-1, 1)
    arrays = (query, keys, values, gate_logit.T, beta_logit.T, rate)

    away, out, gain = local_part((1 - upper).reshape(1), groups, *arrays, None)
    other = lax.ppermute(away, "seq", [(s, s ^ 1) for s in range(shards)])
    own, out, gain = local_part(flag, groups, *arrays, (out, gain))

    state = (half, DK, DV)
    pair = small_call(pair_kernel, flag, (own, other), [own.shape], half * 2**23)[0]
    held = jnp.zeros(state, BF16)
    ending = pair[:, :, :DV]
    came = None
    for step in range(shards // 2 - 1):
        if step:
            held, ending = small_call(hop_kernel, flag, (pair, held, came), [state] * 2, half * 2**22)
        came = lax.ppermute(
            ending, "seq", [(2 * step + i, 2 * step + 2 + i) for i in range(2)]
        )
    keep, send = small_call(middle_kernel, flag, (own, other, held, came), [state] * 2, half * 2**22)
    back = lax.ppermute(send, "seq", [(s, s ^ 1) for s in range(shards)])

    chips = cores // 2
    chip, core = head // 2, lax.rem(head, 2)
    rows = query.shape[0] // cores
    norm_gain = norm_gain.reshape(1, -1)
    swap = [(i, i ^ 1) for i in range(cores)]
    arrived = []
    for by in list(range(1, chips)) + [0]:
        target = lax.rem(chip + by, chips)
        place = jnp.stack([target, core, upper])
        give, stay = project_part(
            place, rows, out, gain, gate_z, keep, back, norm_gain, out_weight
        )
        both = stay + lax.ppermute(give, "head", swap).astype(F32)
        if by:
            moves = [(i, (i + 2 * by) % cores) for i in range(cores)]
            arrived.append(lax.ppermute(both.astype(BF16), "head", moves))
    for part in arrived:
        both = both + part.astype(F32)
    return both.astype(BF16)


def solution(mesh):
    return jax.shard_map(
        on_device,
        mesh=mesh,
        in_specs=(
            P("seq", "head"),
            P("seq", "head"),
            P("seq", "head"),
            P("seq", "head"),
            P("seq", "head"),
            P("head"),
            P(),
            P("seq", "head"),
            P("head", None),
        ),
        out_specs=P(("seq", "head"), None),
        check_vma=False,
    )
```

```python
import functools

import jax
import jax.numpy as jnp
from jax import lax
from jax.experimental import pallas as pl
from jax.experimental.pallas import tpu as pltpu
from jax.sharding import PartitionSpec as P

DK = 128
DV = 128
CHUNK = 256
F32 = jnp.float32
BF16 = jnp.bfloat16
NEG = -1e30
DELTA_VMEM = 20 * 1024 * 1024
OUTPUT_VMEM = 12 * 1024 * 1024
PROJECT_VMEM = 24 * 1024 * 1024


def mm(left, right):
    return lax.dot_general(left, right, (((1,), (0,)), ((), ())), preferred_element_type=F32)


def mm_nt(left, right):
    return lax.dot_general(left, right, (((1,), (1,)), ((), ())), preferred_element_type=F32)


def iota(shape, dim):
    return lax.broadcasted_iota(jnp.int32, shape, dim)


def split3(x):
    hi = x.astype(BF16).astype(F32)
    mid = (x - hi).astype(BF16).astype(F32)
    return hi, mid, x - hi - mid


def softplus(x):
    small = jnp.exp(-jnp.abs(x))
    one = 1.0 + small
    log1p = jnp.where(one == 1.0, small, jnp.log(one) * (small / jnp.where(one == 1.0, 1.0, one - 1.0)))
    return jnp.maximum(x, 0.0) + log1p


def log_inverse_norm(x, rows):
    square = x.astype(F32) * x.astype(F32)
    high = square.astype(BF16)
    low = (square - high.astype(F32)).astype(BF16)
    ones = jnp.ones((rows, x.shape[1]), BF16)
    return -0.5 * jnp.log(mm_nt(ones, high) + mm_nt(ones, low) + 1e-6)


def odd_rows(x, n):
    return jnp.concatenate([x[i + n : i + 2 * n] for i in range(0, x.shape[0], 2 * n)], axis=0)


def weave(even, odd, n):
    parts = []
    for at in range(0, odd.shape[0], n):
        parts.append(even[2 * at : 2 * at + n])
        parts.append(odd[at : at + n])
    return jnp.concatenate(parts, axis=0)


def as_mask(where):
    return jnp.where(where, 1.0, 0.0).astype(BF16)


def unit_lower_inverses(lowers):
    size = lowers[0].shape[0]
    half = size // 2
    row, col = iota((size, size), 0), iota((size, size), 1)
    crow, ccol = iota((half, size), 0), iota((half, size), 1)
    zeros = jnp.zeros((size, size), BF16)
    eye, pair = as_mask(row == col), as_mask(row // 2 == col // 2)
    xs = [eye - lower * pair for lower in lowers]
    n = 2
    while n < size:
        if n < 16:
            mask = as_mask((row // n == col // n + 1) & (row // (2 * n) == col // (2 * n)))
            ys = [mm(lower * mask, x).astype(BF16) for lower, x in zip(lowers, xs)]
            zs = [mm(x, y).astype(BF16) for x, y in zip(xs, ys)]
            xs = [x - z for x, z in zip(xs, zs)]
        elif n < half:
            mask = as_mask(ccol // n == 2 * (crow // n))
            ys = [mm(odd_rows(lower, n) * mask, x).astype(BF16) for lower, x in zip(lowers, xs)]
            odds = [odd_rows(x, n) for x in xs]
            zs = [mm(odd, weave(zeros, y, n)).astype(BF16) for odd, y in zip(odds, ys)]
            xs = [weave(x, odd - z, n) for x, odd, z in zip(xs, odds, zs)]
        else:
            ys = [mm(lower[half:, :half], x[:half, :half]).astype(BF16) for lower, x in zip(lowers, xs)]
            zs = [mm(x[half:, half:], y).astype(BF16) for x, y in zip(xs, ys)]
            xs = [
                jnp.concatenate([x[:half], jnp.concatenate([-z, x[half:, half:]], axis=1)], axis=0)
                for x, z in zip(xs, zs)
            ]
        n *= 2
    return xs


def decayed(c, b, product, mask):
    h = CHUNK // 2

    def quarter(i, j):
        arg = c[i * h : (i + 1) * h] - b[:, j * h : (j + 1) * h]
        if i == j:
            arg = jnp.where(mask, arg, NEG)
        return (jnp.exp(arg) * product[i * h : (i + 1) * h, j * h : (j + 1) * h]).astype(BF16)

    top = jnp.concatenate([quarter(0, 0), jnp.zeros((h, h), BF16)], axis=1)
    return jnp.concatenate([top, jnp.concatenate([quarter(1, 0), quarter(1, 1)], axis=1)], axis=0)


def chosen(x, second):
    half = x.shape[0] // 2
    return jnp.where(second, jnp.concatenate([x[half:], x[:half]], axis=0), x)


def delta_kernel(rate, gate, beta, k_ref, v_ref, second, ends_ref, resid_ref, held_ref, cumul_ref, log_ref):
    tokens = k_ref.shape[0]
    heads = gate.shape[0]
    groups = k_ref.shape[1] // DK
    chunks = [slice(at, at + CHUNK) for at in range(0, tokens, CHUNK)]

    diagonal = iota((heads, heads), 0) == iota((heads, heads), 1)
    rate = jnp.sum(jnp.where(diagonal, rate, 0.0), axis=1, keepdims=True)
    decay = -chosen(rate, second) * softplus(chosen(gate, second))
    log_beta = -softplus(-chosen(beta, second))
    log_k = log_norms(k_ref, heads)

    row, col = iota((CHUNK, CHUNK), 0), iota((CHUNK, CHUNK), 1)
    upto = jnp.where(row <= col, 1.0, 0.0).astype(BF16)
    sums = mm(
        jnp.concatenate([p for here in chunks for p in split3(decay[:, here])], axis=0).astype(BF16), upto
    )
    square = CHUNK // 2
    strict = iota((square, square), 1) < iota((square, square), 0)

    lowers, rights, ended, decays = {}, {}, {}, {}
    for c, here in enumerate(chunks):
        parts = [sums[(3 * c + i) * heads : (3 * c + i + 1) * heads] for i in range(3)]
        cumul = parts[0] + parts[1] + parts[2]
        end = cumul[:, CHUNK - 1 :]
        lb, lk = log_beta[:, here], log_k[:, here]
        col_log = cumul - lk
        row_lower = cumul + lb + lk
        cumul_ref[:, here] = cumul
        log_ref[:, here] = col_log
        key_end = jnp.exp(end - cumul + lk)
        ends = jnp.exp(end)
        columns = jnp.concatenate([row_lower, jnp.exp(lb), jnp.exp(row_lower)], axis=0).T
        for g in range(groups):
            k = k_ref[here, g * DK : (g + 1) * DK]
            k32 = k.astype(F32)
            turned = k32.T
            key_key = mm(k, turned.astype(BF16))
            for r in range(2):
                at = 2 * g + r
                c_lower, c_beta, c_weight = (
                    columns[:, heads * i + at : heads * i + at + 1] for i in range(3)
                )
                m = (c, at)
                lowers[m] = decayed(c_lower, col_log[at : at + 1], key_key, strict)
                v32 = v_ref[here, at * DV : (at + 1) * DV].astype(F32)
                rights[m] = jnp.concatenate([c_beta * v32, c_weight * k32], axis=1).astype(BF16)
                ended[m] = (turned * key_end[at : at + 1]).astype(BF16)
                decays[m] = ends[at : at + 1]
    names = list(lowers)
    inverses = dict(zip(names, unit_lower_inverses([lowers[m] for m in names])))
    solved = {m: mm(inverses[m], rights[m]) for m in names}
    state = {}
    all_heads = range(2 * groups)
    for c, here in enumerate(chunks):
        if c == 0:
            resid = {a: jnp.concatenate([solved[c, a][:, :DV], -solved[c, a][:, DV:]], axis=1) for a in all_heads}
            before = iota((DK, DV + DK), 1) == iota((DK, DV + DK), 0) + DV
            before = {a: jnp.where(before, 1.0, 0.0) for a in all_heads}
        else:
            held = {a: state[a].astype(BF16) for a in all_heads}
            for a in all_heads:
                held_ref[c - 1, a] = held[a]
            moved = {a: mm(solved[c, a][:, DV:].astype(BF16), held[a]) for a in all_heads}
            resid = {
                a: jnp.concatenate([solved[c, a][:, :DV] - moved[a][:, :DV], -moved[a][:, DV:]], axis=1)
                for a in all_heads
            }
            before = state
        resid = {a: resid[a].astype(BF16) for a in all_heads}
        for a in all_heads:
            resid_ref[c, a] = resid[a]
        state = {a: decays[c, a] * before[a] + mm(ended[c, a], resid[a]) for a in all_heads}
    for a in all_heads:
        ends_ref[a] = state[a].astype(BF16)


def log_norms(ref, heads):
    tokens = ref.shape[0]
    head_row = iota((heads, tokens), 0)
    total = log_inverse_norm(ref[:, :DK], heads)
    for g in range(1, ref.shape[1] // DK):
        more = log_inverse_norm(ref[:, g * DK : (g + 1) * DK], heads)
        total = jnp.where(head_row < 2 * g, total, more)
    return total


def lanes(source, which, target):
    width = target.shape[1]
    return source.at[:, pl.ds(pl.multiple_of(which * width, 128), width)], target


def started(moves, sems):
    copies = [pltpu.make_async_copy(a, b, sems.at[i]) for i, (a, b) in enumerate(moves)]
    for copy in copies:
        copy.start()
    return copies


def waited(copies):
    for copy in copies:
        copy.wait()


def first_kernel(
    place_ref, rate_hbm, q_hbm, k_hbm, v_hbm, gate_hbm, beta_hbm, ends, resid, held, cumul, logs,
    rate, gate, beta, k_own, v_own, q_away, k_away, v_away, sems
):
    away = place_ref[0]
    moves = [(rate_hbm, rate), (gate_hbm, gate), (beta_hbm, beta)]
    moves += [lanes(k_hbm, away, k_away), lanes(v_hbm, away, v_away)]
    moves += [lanes(k_hbm, 1 - away, k_own), lanes(v_hbm, 1 - away, v_own), lanes(q_hbm, away, q_away)]
    copies = started(moves, sems)
    waited(copies[:5])
    delta_kernel(rate[...], gate[...], beta[...], k_away, v_away, away == 1, ends, resid, held, cumul, logs)
    waited(copies[5:])


def second_kernel(
    place_ref, q_hbm, rate, gate, beta, k_own, v_own, q_away, k_away, cumul_away, logs_away, resid_away, held_away,
    ends, resid, held, cumul, logs, out, gain, q_own, sems
):
    copies = started([lanes(q_hbm, 1 - place_ref[0], q_own)], sems)
    delta_kernel(rate[...], gate[...], beta[...], k_own, v_own, place_ref[0] == 0, ends, resid, held, cumul, logs)
    local_outputs(q_away, k_away, cumul_away, logs_away, resid_away, held_away, out, gain)
    waited(copies)


def in_vmem(array):
    return pltpu.with_memory_space_constraint(array, pltpu.VMEM)


def delta_shapes(tokens, heads):
    half, chunks = heads // 2, tokens // CHUNK
    return [
        pltpu.MemorySpace.VMEM((half, DK, DV + DK), BF16),
        pltpu.MemorySpace.VMEM((chunks, half, CHUNK, DV + DK), BF16),
        pltpu.MemorySpace.VMEM((chunks - 1, half, DK, DV + DK), BF16),
        pltpu.MemorySpace.VMEM((heads, tokens), F32),
        pltpu.MemorySpace.VMEM((heads, tokens), F32),
    ]


def in_hbm(array):
    return pltpu.with_memory_space_constraint(array, pltpu.HBM)


def output_shapes(tokens, heads):
    return [pltpu.MemorySpace.VMEM((tokens, heads // 2 * DV), BF16)] * 2


def first_part(place, rate, query, keys, values, gate_logit, beta_logit):
    heads, tokens = gate_logit.shape
    half = heads // 2
    vmem = pltpu.MemorySpace.VMEM
    key_part, value_part = (tokens, half // 2 * DK), (tokens, half * DV)
    shapes = delta_shapes(tokens, heads) + [
        vmem((1, heads), F32),
        vmem((heads, tokens), F32),
        vmem((heads, tokens), F32),
        vmem(key_part, BF16),
        vmem(value_part, BF16),
        vmem(key_part, BF16),
        vmem(key_part, BF16),
    ]
    return pl.pallas_call(
        first_kernel,
        in_specs=[pl.BlockSpec(memory_space=pltpu.SMEM)] + [pl.BlockSpec(memory_space=pltpu.HBM)] * 6,
        out_specs=[pl.BlockSpec(memory_space=pltpu.VMEM)] * len(shapes),
        out_shape=shapes,
        scratch_shapes=[pltpu.VMEM(value_part, BF16), pltpu.SemaphoreType.DMA((8,))],
        compiler_params=pltpu.CompilerParams(vmem_limit_bytes=DELTA_VMEM),
        cost_estimate=pl.CostEstimate(flops=4 * 10**9, bytes_accessed=2**20, transcendentals=0),
        name="first_part",
    )(place, *map(in_hbm, (rate, query, keys, values, gate_logit, beta_logit)))


def second_part(place, query, *arrays):
    heads, tokens = arrays[1].shape
    key_part = arrays[3].shape
    shapes = delta_shapes(tokens, heads) + output_shapes(tokens, heads)
    shapes += [pltpu.MemorySpace.VMEM(key_part, BF16)]
    return pl.pallas_call(
        second_kernel,
        in_specs=[pl.BlockSpec(memory_space=pltpu.SMEM), pl.BlockSpec(memory_space=pltpu.HBM)]
        + [pl.BlockSpec(memory_space=pltpu.VMEM)] * len(arrays),
        out_specs=[pl.BlockSpec(memory_space=pltpu.VMEM)] * len(shapes),
        out_shape=shapes,
        scratch_shapes=[pltpu.SemaphoreType.DMA((1,))],
        compiler_params=pltpu.CompilerParams(vmem_limit_bytes=DELTA_VMEM),
        cost_estimate=pl.CostEstimate(flops=5 * 10**9, bytes_accessed=2**20, transcendentals=0),
        name="second_part",
    )(place, in_hbm(query), *map(in_vmem, arrays))


def local_outputs(q_ref, k_ref, cumul_ref, log_ref, resid_ref, held_ref, out_ref, gain_ref):
    tokens = q_ref.shape[0]
    heads = cumul_ref.shape[0]
    groups = q_ref.shape[1] // DK
    square = CHUNK // 2
    inclusive = iota((square, square), 1) <= iota((square, square), 0)
    row_mix = cumul_ref[...] + log_norms(q_ref, heads)
    for c in range(tokens // CHUNK):
        here = slice(c * CHUNK, (c + 1) * CHUNK)
        mix = row_mix[:, here]
        columns = jnp.concatenate([mix, jnp.exp(mix)], axis=0).T
        mixings, queries = {}, {}
        for g in range(groups):
            q, k = q_ref[here, g * DK : (g + 1) * DK], k_ref[here, g * DK : (g + 1) * DK]
            query_key = mm_nt(q, k)
            q32 = q.astype(F32)
            for a in (2 * g, 2 * g + 1):
                b_row = log_ref[a : a + 1, here]
                mixings[a] = decayed(columns[:, a : a + 1], b_row, query_key, inclusive)
                queries[a] = columns[:, heads + a : heads + a + 1] * q32
        for a in range(2 * groups):
            result = mm(mixings[a], resid_ref[c, a])
            if c:
                result = result + mm(queries[a].astype(BF16), held_ref[c - 1, a])
                gain = result[:, DV:]
            else:
                gain = result[:, DV:] + queries[a]
            out_ref[here, a * DV : (a + 1) * DV] = result[:, :DV].astype(BF16)
            gain_ref[here, a * DK : (a + 1) * DK] = gain.astype(BF16)


def third_kernel(*refs):
    local_outputs(*refs[:6], *refs[-2:])


def third_part(q, k, cumul, logs, resid, held, after):
    heads, tokens = cumul.shape
    return pl.pallas_call(
        third_kernel,
        in_specs=[pl.BlockSpec(memory_space=pltpu.VMEM)] * 6 + [pl.BlockSpec(memory_space=pl.ANY)],
        out_specs=[pl.BlockSpec(memory_space=pltpu.VMEM)] * 2,
        out_shape=output_shapes(tokens, heads),
        compiler_params=pltpu.CompilerParams(vmem_limit_bytes=OUTPUT_VMEM),
        cost_estimate=pl.CostEstimate(flops=2 * 10**9, bytes_accessed=2**20, transcendentals=0),
        name="third_part",
    )(*map(in_vmem, (q, k, cumul, logs, resid, held)), after)


def small_call(kernel, flag, arrays, out_shapes, flops, after=()):
    return pl.pallas_call(
        kernel,
        in_specs=[pl.BlockSpec(memory_space=pltpu.SMEM)]
        + [pl.BlockSpec(memory_space=pltpu.VMEM)] * len(arrays)
        + [pl.BlockSpec(memory_space=pl.ANY)] * len(after),
        out_specs=[pl.BlockSpec(memory_space=pltpu.VMEM)] * len(out_shapes),
        out_shape=[pltpu.MemorySpace.VMEM(s, BF16) for s in out_shapes],
        cost_estimate=pl.CostEstimate(flops=flops, bytes_accessed=2**18, transcendentals=0),
        name="hand_over",
    )(flag, *map(in_vmem, arrays), *after)


def pair_kernel(upper_ref, own_ref, other_ref, pair_ref, *ending_refs):
    upper = upper_ref[0] == 1
    count = ending_refs[0].shape[0]
    for h in range(own_ref.shape[0]):
        own, other = own_ref[h].astype(F32), other_ref[h].astype(F32)
        one = jnp.where(upper, other, own)
        two = jnp.where(upper, own, other)
        both = mm(two[:, DV:].astype(BF16), one.astype(BF16))
        inject = (both[:, :DV] + two[:, :DV]).astype(BF16)
        ending_refs[h // count][h % count] = inject
        pair_ref[h] = jnp.concatenate([inject, both[:, DV:].astype(BF16)], axis=1)


def hop_kernel(part, came, upper_ref, pair_ref, *refs):
    sum_ref, out_ref = refs[-2:]
    count = sum_ref.shape[0]
    for h in range(count):
        start = refs[0][h]
        for came_ref in refs[1:came]:
            start = start + came_ref[h]
        sum_ref[h] = start
        pair = pair_ref[part * count + h]
        out_ref[h] = (mm(pair[:, DV:], start) + pair[:, :DV].astype(F32)).astype(BF16)


def middle_kernel(part, came, upper_ref, own_ref, other_ref, *refs):
    keep_ref, send_ref = refs[-2:]
    upper = upper_ref[0] == 1
    count = keep_ref.shape[0]
    for h in range(count):
        start = refs[0][h]
        for came_ref in refs[1:came]:
            start = start + came_ref[h]
        at = part * count + h
        one = jnp.where(upper, other_ref[at].astype(F32), own_ref[at].astype(F32))
        middle = mm(one[:, DV:].astype(BF16), start) + one[:, :DV]
        start = start.astype(F32)
        keep_ref[h] = jnp.where(upper, middle, start).astype(BF16)
        send_ref[h] = jnp.where(upper, start, middle).astype(BF16)


def gated_rows(out, gain, z, at, start_refs, norm):
    parts = []
    count = start_refs[0].shape[0]
    for h in range(count * len(start_refs)):
        cols = slice(h * DV, (h + 1) * DV)
        core = out[at, cols].astype(F32) + mm(gain[at, cols], start_refs[h // count][h % count])
        mean = jnp.mean(core * core, axis=1, keepdims=True)
        z_here = z[:, cols].astype(F32)
        gate = z_here / (1.0 + jnp.exp(-z_here))
        parts.append((core * lax.rsqrt(mean + 1e-6) * norm * gate).astype(BF16))
    return jnp.concatenate(parts, axis=1)


def chip_rows(place_ref, rows):
    return pl.ds(pl.multiple_of(place_ref[0] * rows, rows), rows)


def patch(source, row, group, target):
    height, width = target.shape
    at = (
        pl.ds(pl.multiple_of(row * height, height), height),
        pl.ds(pl.multiple_of(group * width, 128), width),
    )
    return source.at[at], target


def bands(source, group, target):
    height = target.shape[0]
    return source.at[pl.ds(pl.multiple_of(group * height, 128), height), :], target


def group_moves(place_ref, group, z_hbm, w_hbm, z, w):
    return [patch(z_hbm, place_ref[0], group, z), bands(w_hbm, group, w)]


def group_buffers(rows, width, wide, make):
    return [make((rows, width), BF16), make((width, wide), BF16)]


def keep_kernel(place_ref, z_hbm, w_hbm, norm_hbm, out, gain, *refs):
    start_refs, (sum_ref, norm, z_away, w_away, z_own, w_own, sems) = refs[:-7], refs[-7:]
    group = place_ref[2]
    moves = [(norm_hbm, norm)] + group_moves(place_ref, group, z_hbm, w_hbm, z_own, w_own)
    moves += group_moves(place_ref, 1 - group, z_hbm, w_hbm, z_away, w_away)
    copies = started(moves, sems)
    waited(copies[:2])
    gated = gated_rows(out, gain, z_own, chip_rows(place_ref, z_own.shape[0]), start_refs, norm[...])
    waited(copies[2:3])
    sum_ref[...] = mm(gated, w_own[...])
    waited(copies[3:])


def keep_part(place, rows, gate_z, weight, norm_gain, out, gain, start):
    wide = weight.shape[1]
    width = weight.shape[0] // 2
    vmem = pltpu.MemorySpace.VMEM
    shapes = [vmem((2 * rows, wide), F32), vmem((1, DV), F32)] + group_buffers(2 * rows, width, wide, vmem)
    return pl.pallas_call(
        keep_kernel,
        in_specs=[pl.BlockSpec(memory_space=pltpu.SMEM)]
        + [pl.BlockSpec(memory_space=pltpu.HBM)] * 3
        + [pl.BlockSpec(memory_space=pltpu.VMEM)] * (2 + len(start)),
        out_specs=[pl.BlockSpec(memory_space=pltpu.VMEM)] * len(shapes),
        out_shape=shapes,
        scratch_shapes=group_buffers(2 * rows, width, wide, pltpu.VMEM) + [pltpu.SemaphoreType.DMA((5,))],
        compiler_params=pltpu.CompilerParams(vmem_limit_bytes=PROJECT_VMEM),
        cost_estimate=pl.CostEstimate(
            flops=4 * rows * width * wide, bytes_accessed=2**20, transcendentals=0
        ),
        name="keep_part",
    )(place, *map(in_hbm, (gate_z, weight, norm_gain)), *map(in_vmem, (out, gain, *start)))


def send_rows(partial, core, send_refs, stay_ref):
    rows, width = send_refs[0].shape
    one, two = partial[:rows], partial[rows:]
    send = jnp.where(core == 0, two, one).astype(BF16)
    for i, ref in enumerate(send_refs):
        ref[...] = send[:, i * width : (i + 1) * width]
    stay_ref[...] = jnp.where(core == 0, one, two)


def away_kernel(place_ref, sum_ref, norm, z, w, out, gain, *refs):
    start_refs, (send_ref, stay_ref) = refs[:-2], refs[-2:]
    gated = gated_rows(out, gain, z, chip_rows(place_ref, z.shape[0]), start_refs, norm[...])
    send_rows(mm(gated, w[...]) + sum_ref[...], place_ref[1], [send_ref], stay_ref)


def away_part(place, kept, out, gain, start):
    rows, wide = kept[0].shape[0] // 2, kept[0].shape[1]
    vmem = pltpu.MemorySpace.VMEM
    arrays = (*kept, out, gain, *start)
    return pl.pallas_call(
        away_kernel,
        in_specs=[pl.BlockSpec(memory_space=pltpu.SMEM)] + [pl.BlockSpec(memory_space=pltpu.VMEM)] * len(arrays),
        out_specs=[pl.BlockSpec(memory_space=pltpu.VMEM)] * 2,
        out_shape=[vmem((rows, wide), BF16), vmem((rows, wide), F32)],
        compiler_params=pltpu.CompilerParams(vmem_limit_bytes=PROJECT_VMEM),
        cost_estimate=pl.CostEstimate(
            flops=4 * rows * kept[-1].size, bytes_accessed=2**20, transcendentals=0
        ),
        name="away_part",
    )(place, *map(in_vmem, arrays))


def whole_kernel(place_ref, z_hbm, w_hbm, norm_hbm, own_out, own_gain, away_out, away_gain, *refs):
    starts, (send_one, send_two, stay_ref, norm, z_own, w_own, z_away, w_away, sems) = refs[:-9], refs[-9:]
    group = place_ref[2]
    moves = [(norm_hbm, norm)] + group_moves(place_ref, group, z_hbm, w_hbm, z_own, w_own)
    moves += group_moves(place_ref, 1 - group, z_hbm, w_hbm, z_away, w_away)
    copies = started(moves, sems)
    waited(copies[:2])
    at = chip_rows(place_ref, z_own.shape[0])
    first = gated_rows(own_out, own_gain, z_own, at, starts[: len(starts) // 2], norm[...])
    waited(copies[2:4])
    second = gated_rows(away_out, away_gain, z_away, at, starts[len(starts) // 2 :], norm[...])
    waited(copies[4:])
    partial = mm(first, w_own[...]) + mm(second, w_away[...])
    send_rows(partial, place_ref[1], [send_one, send_two], stay_ref)


def whole_part(place, rows, gate_z, weight, norm_gain, *arrays):
    wide = weight.shape[1]
    width = weight.shape[0] // 2
    vmem = pltpu.MemorySpace.VMEM
    return pl.pallas_call(
        whole_kernel,
        in_specs=[pl.BlockSpec(memory_space=pltpu.SMEM)]
        + [pl.BlockSpec(memory_space=pltpu.HBM)] * 3
        + [pl.BlockSpec(memory_space=pltpu.VMEM)] * len(arrays),
        out_specs=[pl.BlockSpec(memory_space=pltpu.VMEM)] * 3,
        out_shape=[vmem((rows, wide // 2), BF16)] * 2 + [vmem((rows, wide), F32)],
        scratch_shapes=[pltpu.VMEM((1, DV), F32)]
        + group_buffers(2 * rows, width, wide, pltpu.VMEM) * 2
        + [pltpu.SemaphoreType.DMA((5,))],
        compiler_params=pltpu.CompilerParams(vmem_limit_bytes=PROJECT_VMEM),
        cost_estimate=pl.CostEstimate(
            flops=8 * rows * width * wide, bytes_accessed=2**22, transcendentals=0
        ),
        name="whole_part",
    )(place, *map(in_hbm, (gate_z, weight, norm_gain)), *map(in_vmem, arrays))


def on_device(
    query, keys, values, gate_logit, beta_logit, decay_rate, norm_gain, gate_z, out_weight
):
    shards, cores = lax.axis_size("seq"), lax.axis_size("head")
    seq, head = lax.axis_index("seq"), lax.axis_index("head")
    half = values.shape[1] // DV // 2
    upper = lax.rem(seq, 2)
    flag = upper.reshape(1)
    place = (1 - upper).reshape(1)

    rate, norm_gain = decay_rate.reshape(1, -1), norm_gain.reshape(1, -1)

    away, resid, held, cumul, logs, rate, gate, beta, k_own, v_own, q_away, k_away = first_part(
        place, rate, query, keys, values, gate_logit.T, beta_logit.T
    )
    other = lax.ppermute(away, "seq", [(s, s ^ 1) for s in range(shards)])
    own, resid, held, cumul, logs, out_away, gain_away, q_own = second_part(
        place, query, rate, gate, beta, k_own, v_own, q_away, k_away, cumul, logs, resid, held
    )
    parts = 2 if half % 2 == 0 else 1
    state = (half // parts, DK, DV)
    pair, *endings = small_call(
        pair_kernel, flag, (own, other), [own.shape] + [state] * parts, half * 2**23
    )
    out_own, gain_own = third_part(q_own, k_own, cumul, logs, resid, held, pair)
    came = [[] for _ in range(parts)]
    for step in range(shards // 2 - 1):
        along = [(2 * step + i, 2 * step + 2 + i) for i in range(2)]
        for p in range(parts):
            if step:
                start, endings[p] = small_call(
                    functools.partial(hop_kernel, p, len(came[p])), flag, (pair, *came[p]), [state] * 2, half * 2**22,
                    (out_own,) if step == 1 and p == parts - 1 else (),
                )
                came[p] = [start]
            came[p].append(lax.ppermute(endings[p], "seq", along))
    keep, back = [], []
    for p in range(parts):
        kept, send = small_call(
            functools.partial(middle_kernel, p, len(came[p])), flag, (own, other, *came[p]), [state] * 2, half * 2**22
        )
        keep.append(kept)
        back.append(lax.ppermute(send, "seq", [(s, s ^ 1) for s in range(shards)]))

    chips = cores // 2
    chip, core = head // 2, lax.rem(head, 2)
    rows = query.shape[0] // cores
    swap = [(i, i ^ 1) for i in range(cores)]
    arrived = []
    for by in range(1, chips):
        spot = jnp.stack([lax.rem(chip + by, chips), core, upper])
        kept = keep_part(spot, rows, gate_z, out_weight, norm_gain, out_own, gain_own, keep)
        give, stay = away_part(spot, kept, out_away, gain_away, back)
        both = (stay + lax.ppermute(give, "head", swap).astype(F32)).astype(BF16)
        moves = [(i, (i + 2 * by) % cores) for i in range(cores)]
        arrived.append(lax.ppermute(both, "head", moves))
    spot = jnp.stack([chip, core, upper])
    if arrived:
        spot, both = lax.optimization_barrier((spot, both))
    *gives, stay = whole_part(
        spot, rows, gate_z, out_weight, norm_gain, out_own, gain_own, out_away, gain_away, *keep, *back
    )
    total = stay + jnp.concatenate([lax.ppermute(g, "head", swap) for g in gives], axis=1).astype(F32)
    for part in arrived:
        total = total + part.astype(F32)
    return total.astype(BF16)


def solution(mesh):
    return jax.shard_map(
        on_device,
        mesh=mesh,
        in_specs=(
            P("seq", "head"),
            P("seq", "head"),
            P("seq", "head"),
            P("seq", "head"),
            P("seq", "head"),
            P("head"),
            P(),
            P("seq", "head"),
            P("head", None),
        ),
        out_specs=P(("seq", "head"), None),
        check_vma=False,
    )
```

```python
import jax
import jax.numpy as jnp
from jax import lax
from jax.experimental import pallas as pl
from jax.experimental.pallas import tpu as pltpu
from jax.sharding import PartitionSpec as P

DK = 128
DV = 128
CHUNK = 256
F32 = jnp.float32
BF16 = jnp.bfloat16
NEG = -1e30
SMALL_VMEM = 8 * 1024 * 1024
DELTA_VMEM = 28 * 1024 * 1024
OUTPUT_VMEM = 20 * 1024 * 1024
PROJECT_VMEM = 24 * 1024 * 1024


def mm(left, right):
    return lax.dot_general(left, right, (((1,), (0,)), ((), ())), preferred_element_type=F32)


def mm_nt(left, right):
    return lax.dot_general(left, right, (((1,), (1,)), ((), ())), preferred_element_type=F32)


def iota(shape, dim):
    return lax.broadcasted_iota(jnp.int32, shape, dim)


def split3(x):
    hi = x.astype(BF16).astype(F32)
    mid = (x - hi).astype(BF16).astype(F32)
    return hi, mid, x - hi - mid


def softplus(x):
    small = jnp.exp(-jnp.abs(x))
    one = 1.0 + small
    log1p = jnp.where(one == 1.0, small, jnp.log(one) * (small / jnp.where(one == 1.0, 1.0, one - 1.0)))
    return jnp.maximum(x, 0.0) + log1p


def log_inverse_norm(x, rows):
    square = x.astype(F32) * x.astype(F32)
    high = square.astype(BF16)
    low = (square - high.astype(F32)).astype(BF16)
    ones = jnp.ones((rows, x.shape[1]), BF16)
    return -0.5 * jnp.log(mm_nt(ones, high) + mm_nt(ones, low) + 1e-6)


def odd_rows(x, n):
    return jnp.concatenate([x[i + n : i + 2 * n] for i in range(0, x.shape[0], 2 * n)], axis=0)


def weave(even, odd, n):
    parts = []
    for at in range(0, odd.shape[0], n):
        parts.append(even[2 * at : 2 * at + n])
        parts.append(odd[at : at + n])
    return jnp.concatenate(parts, axis=0)


def as_mask(where):
    return jnp.where(where, 1.0, 0.0).astype(BF16)


def unit_lower_inverses(lowers):
    size = lowers[0].shape[0]
    half = size // 2
    row, col = iota((size, size), 0), iota((size, size), 1)
    crow, ccol = iota((half, size), 0), iota((half, size), 1)
    zeros = jnp.zeros((size, size), BF16)
    eye, pair = as_mask(row == col), as_mask(row // 2 == col // 2)
    xs = [eye - lower * pair for lower in lowers]
    n = 2
    while n < size:
        if n < 16:
            mask = as_mask((row // n == col // n + 1) & (row // (2 * n) == col // (2 * n)))
            ys = [mm(lower * mask, x).astype(BF16) for lower, x in zip(lowers, xs)]
            zs = [mm(x, y).astype(BF16) for x, y in zip(xs, ys)]
            xs = [x - z for x, z in zip(xs, zs)]
        elif n < half:
            mask = as_mask(ccol // n == 2 * (crow // n))
            ys = [mm(odd_rows(lower, n) * mask, x).astype(BF16) for lower, x in zip(lowers, xs)]
            odds = [odd_rows(x, n) for x in xs]
            zs = [mm(odd, weave(zeros, y, n)).astype(BF16) for odd, y in zip(odds, ys)]
            xs = [weave(x, odd - z, n) for x, odd, z in zip(xs, odds, zs)]
        else:
            ys = [mm(lower[half:, :half], x[:half, :half]).astype(BF16) for lower, x in zip(lowers, xs)]
            zs = [mm(x[half:, half:], y).astype(BF16) for x, y in zip(xs, ys)]
            xs = [
                jnp.concatenate([x[:half], jnp.concatenate([-z, x[half:, half:]], axis=1)], axis=0)
                for x, z in zip(xs, zs)
            ]
        n *= 2
    return xs


def decayed(c, b, product, mask):
    h = CHUNK // 2

    def quarter(i, j):
        arg = c[i * h : (i + 1) * h] - b[:, j * h : (j + 1) * h]
        if i == j:
            arg = jnp.where(mask, arg, NEG)
        return (jnp.exp(arg) * product[i * h : (i + 1) * h, j * h : (j + 1) * h]).astype(BF16)

    top = jnp.concatenate([quarter(0, 0), jnp.zeros((h, h), BF16)], axis=1)
    return jnp.concatenate([top, jnp.concatenate([quarter(1, 0), quarter(1, 1)], axis=1)], axis=0)


def reordered(x, quarters, first):
    row = iota(x.shape, 0)
    total = jnp.zeros_like(x)
    for j, quarter in enumerate(quarters, first):
        for r in range(2):
            picked = jnp.sum(jnp.where(row == 2 * quarter + r, x, 0.0), axis=0, keepdims=True)
            total = jnp.where(row == 2 * j + r, picked, total)
    return total


def log_norms(refs, heads, first=0):
    tokens = refs[0].shape[0]
    head_row = iota((heads, tokens), 0)
    total = log_inverse_norm(refs[0][...], heads)
    for j, ref in enumerate(refs[1:], first + 1):
        total = jnp.where(head_row < 2 * j, total, log_inverse_norm(ref[...], heads))
    return total


def delta_kernel(rate, gate, beta, quarters, first, k_refs, v_refs, ends_refs, resid_ref, held_ref, cumul_ref, log_ref):
    tokens = k_refs[0].shape[0]
    heads = gate.shape[0]
    chunks = [slice(at, at + CHUNK) for at in range(0, tokens, CHUNK)]

    diagonal = iota((heads, heads), 0) == iota((heads, heads), 1)
    rate = jnp.sum(jnp.where(diagonal, rate, 0.0), axis=1, keepdims=True)
    decay = reordered(-rate * softplus(gate), quarters, first)
    log_beta = reordered(-softplus(-beta), quarters, first)
    log_k = log_norms(k_refs, heads, first)

    row, col = iota((CHUNK, CHUNK), 0), iota((CHUNK, CHUNK), 1)
    upto = jnp.where(row <= col, 1.0, 0.0).astype(BF16)
    sums = mm(
        jnp.concatenate([p for here in chunks for p in split3(decay[:, here])], axis=0).astype(BF16), upto
    )
    square = CHUNK // 2
    strict = iota((square, square), 1) < iota((square, square), 0)

    lowers, rights, ended, decays = {}, {}, {}, {}
    for c, here in enumerate(chunks):
        parts = [sums[(3 * c + i) * heads : (3 * c + i + 1) * heads] for i in range(3)]
        cumul = parts[0] + parts[1] + parts[2]
        end = cumul[:, CHUNK - 1 :]
        lb, lk = log_beta[:, here], log_k[:, here]
        col_log = cumul - lk
        row_lower = cumul + lb + lk
        cumul_ref[:, here] = cumul
        log_ref[:, here] = col_log
        key_end = jnp.exp(end - cumul + lk)
        ends = jnp.exp(end)
        columns = jnp.concatenate([row_lower, jnp.exp(lb), jnp.exp(row_lower)], axis=0).T
        for j, (k_ref, v_ref) in enumerate(zip(k_refs, v_refs)):
            k = k_ref[here, :]
            k32 = k.astype(F32)
            turned = k32.T
            key_key = mm(k, turned.astype(BF16))
            for r in range(2):
                at = 2 * (first + j) + r
                c_lower, c_beta, c_weight = (
                    columns[:, heads * i + at : heads * i + at + 1] for i in range(3)
                )
                m = (c, 2 * j + r)
                lowers[m] = decayed(c_lower, col_log[at : at + 1], key_key, strict)
                v32 = v_ref[here, r * DV : (r + 1) * DV].astype(F32)
                rights[m] = jnp.concatenate([c_beta * v32, c_weight * k32], axis=1).astype(BF16)
                ended[m] = (turned * key_end[at : at + 1]).astype(BF16)
                decays[m] = ends[at : at + 1]
    names = list(lowers)
    inverses = dict(zip(names, unit_lower_inverses([lowers[m] for m in names])))
    solved = {m: mm(inverses[m], rights[m]) for m in names}
    all_heads = range(2 * len(k_refs))
    state = {}
    for c, here in enumerate(chunks):
        if c == 0:
            resid = {a: jnp.concatenate([solved[c, a][:, :DV], -solved[c, a][:, DV:]], axis=1) for a in all_heads}
            before = iota((DK, DV + DK), 1) == iota((DK, DV + DK), 0) + DV
            before = {a: jnp.where(before, 1.0, 0.0) for a in all_heads}
            for a in all_heads:
                held_ref[a // 2, c, a % 2] = before[a].astype(BF16)
        else:
            held = {a: state[a].astype(BF16) for a in all_heads}
            for a in all_heads:
                held_ref[a // 2, c, a % 2] = held[a]
            moved = {a: mm(solved[c, a][:, DV:].astype(BF16), held[a]) for a in all_heads}
            resid = {
                a: jnp.concatenate([solved[c, a][:, :DV] - moved[a][:, :DV], -moved[a][:, DV:]], axis=1)
                for a in all_heads
            }
            before = state
        resid = {a: resid[a].astype(BF16) for a in all_heads}
        for a in all_heads:
            resid_ref[a // 2, c, a % 2] = resid[a]
        state = {a: decays[c, a] * before[a] + mm(ended[c, a], resid[a]) for a in all_heads}
    for a in all_heads:
        ends_refs[a // 2][a % 2] = state[a].astype(BF16)


def local_outputs(q_refs, k_refs, cumul, logs, waits, resid, held, out_ref, gain_ref):
    tokens = q_refs[0].shape[0]
    heads = cumul.shape[0]
    square = CHUNK // 2
    inclusive = iota((square, square), 1) <= iota((square, square), 0)
    row_mix = cumul + log_norms(q_refs, heads)
    mixings, queries = {}, {}
    for c in range(tokens // CHUNK):
        here = slice(c * CHUNK, (c + 1) * CHUNK)
        mix = row_mix[:, here]
        columns = jnp.concatenate([mix, jnp.exp(mix)], axis=0).T
        for j, (q_ref, k_ref) in enumerate(zip(q_refs, k_refs)):
            q, k = q_ref[here, :], k_ref[here, :]
            query_key = mm_nt(q, k)
            q32 = q.astype(F32)
            for a in (2 * j, 2 * j + 1):
                b_row = logs[a : a + 1, here]
                mixings[c, a] = decayed(columns[:, a : a + 1], b_row, query_key, inclusive)
                queries[c, a] = (columns[:, heads + a : heads + a + 1] * q32).astype(BF16)
    waited(waits)
    for c, a in mixings:
        here = slice(c * CHUNK, (c + 1) * CHUNK)
        result = mm(queries[c, a], held(c, a)) + mm(mixings[c, a], resid(c, a))
        out_ref[here, a * DV : (a + 1) * DV] = result[:, :DV].astype(BF16)
        gain_ref[here, a * DK : (a + 1) * DK] = result[:, DV:].astype(BF16)


def lanes(source, which, target):
    width = target.shape[1]
    return source.at[:, pl.ds(pl.multiple_of(which * width, 128), width)], target


def started(moves, sems, first=0):
    copies = [pltpu.make_async_copy(a, b, sems.at[first + i]) for i, (a, b) in enumerate(moves)]
    for copy in copies:
        copy.start()
    return copies


def waited(copies):
    for copy in copies:
        copy.wait()


def in_vmem(array):
    return pltpu.with_memory_space_constraint(array, pltpu.VMEM)


def in_hbm(array):
    return pltpu.with_memory_space_constraint(array, pltpu.HBM)


def call(kernel, name, groups, outs, scratch, vmem_bytes, flops):
    specs, args = [], []
    for space, arrays in groups:
        specs += [pl.BlockSpec(memory_space=space)] * len(arrays)
        if space is pltpu.VMEM or space is pltpu.HBM:
            arrays = [pltpu.with_memory_space_constraint(a, space) for a in arrays]
        args += arrays
    return pl.pallas_call(
        kernel,
        in_specs=specs,
        out_specs=[pl.BlockSpec(memory_space=space) for space, _, _ in outs],
        out_shape=[space(shape, kind) for space, shape, kind in outs],
        scratch_shapes=scratch,
        compiler_params=pltpu.CompilerParams(vmem_limit_bytes=vmem_bytes),
        cost_estimate=pl.CostEstimate(flops=flops, bytes_accessed=2**20, transcendentals=0),
        name=name,
    )(*args)


def local_shapes(count, tokens, heads):
    chunks = tokens // CHUNK
    return [
        ((count, chunks, 2, CHUNK, DV + DK), BF16),
        ((count, chunks, 2, DK, DV + DK), BF16),
        ((heads, tokens), F32),
        ((heads, tokens), F32),
    ]


def first_part(member, turns, rate, keys, values, gate_logit, beta_logit):
    heads, tokens = gate_logit.shape
    count = len(turns)
    key_part, value_part = (tokens, DK), (tokens, 2 * DV)

    def kernel(member_ref, rate_hbm, k_hbm, v_hbm, gate_hbm, beta_hbm, *refs):
        ends, (resid, held, cumul, logs, rate, gate, beta, k_own, v_own), refs = (
            refs[:count], refs[count : count + 9], refs[count + 9 :]
        )
        k_refs, v_refs, sems = refs[:count], refs[count : 2 * count], refs[-1]
        quarters = [jnp.bitwise_xor(member_ref[0], turn) for turn in turns]
        moves = [(rate_hbm, rate), (gate_hbm, gate), (beta_hbm, beta)]
        moves += [lanes(k_hbm, q, ref) for q, ref in zip(quarters, k_refs)]
        moves += [lanes(v_hbm, q, ref) for q, ref in zip(quarters, v_refs)]
        moves += [lanes(k_hbm, member_ref[0], k_own), lanes(v_hbm, member_ref[0], v_own)]
        copies = started(moves, sems)
        waited(copies[:-2])
        delta_kernel(
            rate[...], gate[...], beta[...], quarters, 0, k_refs, v_refs, ends, resid, held, cumul, logs
        )
        waited(copies[-2:])

    vmem = pltpu.VMEM
    outs = [(vmem, (2, DK, DV + DK), BF16)] * count
    outs += [(vmem, *shape) for shape in local_shapes(count, tokens, heads)]
    outs += [(vmem, (1, heads), F32), (vmem, (heads, tokens), F32), (vmem, (heads, tokens), F32)]
    outs += [(vmem, key_part, BF16), (vmem, value_part, BF16)]
    outs = [(pltpu.MemorySpace.VMEM, *rest) for _, *rest in outs]
    scratch = [vmem(key_part, BF16)] * count + [vmem(value_part, BF16)] * count
    scratch += [pltpu.SemaphoreType.DMA((5 + 2 * count,))]
    groups = [(pltpu.SMEM, [member]), (pltpu.HBM, [rate, keys, values, gate_logit, beta_logit])]
    result = call(kernel, "first_part", groups, outs, scratch, DELTA_VMEM, 6 * 10**9)
    return result[:count], result[count : count + 4], result[count + 4 :]


def second_part(member, operands, earlier):
    heads, tokens = operands[1].shape

    def kernel(member_ref, rate, gate, beta, k_own, v_own, *refs):
        earlier_refs, (ends,), out_hbm, local, sems = refs[:4], refs[4:5], refs[5:13], refs[13:17], refs[17]
        copies = started(zip(earlier_refs, out_hbm[:4]), sems)
        delta_kernel(
            rate[...], gate[...], beta[...], [member_ref[0]], heads // 2 - 1, [k_own], [v_own], [ends], *local
        )
        copies += started(zip(local, out_hbm[4:]), sems, 4)
        waited(copies)

    shapes = local_shapes(1, tokens, heads)
    outs = [(pltpu.MemorySpace.VMEM, (2, DK, DV + DK), BF16)]
    outs += [(pltpu.MemorySpace.HBM, a.shape, a.dtype) for a in earlier]
    outs += [(pltpu.MemorySpace.HBM, *shape) for shape in shapes]
    scratch = [pltpu.VMEM(*shape) for shape in shapes] + [pltpu.SemaphoreType.DMA((8,))]
    groups = [(pltpu.SMEM, [member]), (pltpu.VMEM, [*operands, *earlier])]
    ends, *rest = call(kernel, "second_part", groups, outs, scratch, DELTA_VMEM, 2 * 10**9)
    return ends, rest[:4], rest[4:]


def third_part(place, turns, chunks, query, keys, earlier, own, after):
    count = len(turns) + 1
    tokens = chunks * CHUNK
    heads = 2 * count

    def kernel(place_ref, q_hbm, k_hbm, *refs):
        sources, (_, out, gain), refs = refs[:8], refs[8:11], refs[11:]
        q_refs, k_refs, local, sems = refs[:count], refs[count : 2 * count], refs[2 * count : -1], refs[-1]
        first = place_ref[0] * chunks
        rows = pl.ds(pl.multiple_of(first * CHUNK, CHUNK), tokens)
        quarters = [jnp.bitwise_xor(place_ref[2], turn) for turn in (*turns, 0)]
        moves = []
        for hbm, targets in ((q_hbm, q_refs), (k_hbm, k_refs)):
            for quarter, ref in zip(quarters, targets):
                moves.append((hbm.at[rows, pl.ds(pl.multiple_of(quarter * DK, DK), DK)], ref))
        for i in (2, 3, 6, 7):
            moves.append((sources[i].at[:, rows], local[i]))
        for i in (0, 1, 4, 5):
            moves.append((sources[i].at[:, pl.ds(first, chunks)], local[i]))
        copies = started(moves, sems)
        waited(copies[:-4])
        theirs = iota((heads, tokens), 0) < heads - 2
        cumul = jnp.where(theirs, local[2][...], local[6][...])
        logs = jnp.where(theirs, local[3][...], local[7][...])

        def read(which):
            return lambda c, a: local[which][a // 2, c, a % 2] if a < heads - 2 else local[which + 4][0, c, a % 2]

        local_outputs(q_refs, k_refs, cumul, logs, copies[-4:], read(0), read(1), out, gain)

    outs = [(pltpu.MemorySpace.VMEM, (tokens, heads * DV), BF16)] * 2
    scratch = [pltpu.VMEM((tokens, DK), BF16)] * (2 * count)
    for pairs in (count - 1, 1):
        scratch += [pltpu.VMEM(*shape) for shape in local_shapes(pairs, tokens, heads)]
    scratch += [pltpu.SemaphoreType.DMA((2 * count + 8,))]
    groups = [(pltpu.SMEM, [place]), (pltpu.HBM, [query, keys, *earlier, *own, after])]
    return call(kernel, "third_part", groups, outs, scratch, OUTPUT_VMEM, 3 * 10**9)


def in_order(member_ref, turns, own_ref, other_refs, order_ref):
    order_ref[member_ref[0]] = own_ref[...]
    for turn, ref in zip(turns, other_refs):
        order_ref[jnp.bitwise_xor(member_ref[0], turn)] = ref[...]


def after_shard(ends, state):
    return mm(ends[:, DV:], state.astype(BF16)) + ends[:, :DV].astype(F32)


def group_part(member, turns, own, others, chained):
    count = len(turns) + 1

    def kernel(member_ref, own_ref, *refs):
        other_refs, (order, ending_ref, *total_refs) = refs[: count - 1], refs[count - 1 :]
        in_order(member_ref, turns, own_ref, other_refs, order)
        states = [order[0, h][:, :DV].astype(F32) for h in range(2)]
        for i in range(1, count):
            states = [after_shard(order[i, h], states[h]) for h in range(2)]
        for h in range(2):
            ending_ref[h] = states[h].astype(BF16)
        for total_ref in total_refs:
            for h in range(2):
                transit = order[0, h][:, DV:]
                for i in range(1, count):
                    transit = mm(order[i, h][:, DV:], transit).astype(BF16)
                total_ref[h] = jnp.concatenate([states[h].astype(BF16), transit], axis=1)

    vmem = pltpu.MemorySpace.VMEM
    outs = [(vmem, (count, *own.shape), BF16), (vmem, (2, DK, DV), BF16)]
    if chained:
        outs.append((vmem, own.shape, BF16))
    groups = [(pltpu.SMEM, [member]), (pltpu.VMEM, [own, *others])]
    return call(kernel, "group_part", groups, outs, [], SMALL_VMEM, 10**8)


def hop_part(total, came):
    def kernel(total_ref, *refs):
        sum_ref, out_ref = refs[-2:]
        for h in range(2):
            start = refs[0][h]
            for ref in refs[1:-2]:
                start = start + ref[h]
            sum_ref[h] = start
            out_ref[h] = after_shard(total_ref[h], start).astype(BF16)

    outs = [(pltpu.MemorySpace.VMEM, (2, DK, DV), BF16)] * 2
    return call(kernel, "hop_part", [(pltpu.VMEM, [total, *came])], outs, [], SMALL_VMEM, 10**7)


def starts_part(member, turns, order, came, after):
    count = len(turns) + 1

    def kernel(member_ref, order_ref, *refs):
        came_refs, outs, states_ref = refs[: len(came)], refs[len(came) + 1 : -1], refs[-1]
        states = [came_refs[0][h] for h in range(2)]
        for ref in came_refs[1:]:
            states = [states[h] + ref[h] for h in range(2)]
        for i in range(count):
            for h in range(2):
                states_ref[i, h] = states[h].astype(BF16)
            if i < count - 1:
                states = [after_shard(order_ref[i, h], states[h]) for h in range(2)]
        for turn, ref in zip((0, *turns), outs):
            ref[...] = states_ref[jnp.bitwise_xor(member_ref[0], turn)]

    state = (2, DK, DV)
    outs = [(pltpu.MemorySpace.VMEM, state, BF16)] * count
    groups = [(pltpu.SMEM, [member]), (pltpu.VMEM, [order, *came]), (pltpu.VMEM, [after])]
    return call(kernel, "starts_part", groups, outs, [pltpu.VMEM((count, *state), BF16)], SMALL_VMEM, 10**8)


def gated_rows(out, gain, z, at, first, start_refs, norm):
    parts = []
    for h in range(2 * len(start_refs)):
        cols = slice(h * DV, (h + 1) * DV)
        local = slice((2 * first + h) * DV, (2 * first + h + 1) * DV)
        core = out[at, local].astype(F32) + mm(gain[at, local], start_refs[h // 2][h % 2])
        mean = jnp.mean(core * core, axis=1, keepdims=True)
        z_here = z[:, cols].astype(F32)
        gate = z_here / (1.0 + jnp.exp(-z_here))
        parts.append((core * lax.rsqrt(mean + 1e-6) * norm * gate).astype(BF16))
    return jnp.concatenate(parts, axis=1)


def pair_moves(place_ref, turns, z_hbm, w_hbm, z, w):
    rows, width = z.shape[0], 2 * DV
    here = pl.ds(pl.multiple_of(place_ref[0] * rows, rows), rows)
    gates, bands = [], []
    for j, turn in enumerate(turns):
        at = pl.ds(pl.multiple_of(jnp.bitwise_xor(place_ref[2], turn) * width, width), width)
        part = slice(j * width, (j + 1) * width)
        gates.append((z_hbm.at[here, at], z.at[:, part]))
        bands.append((w_hbm.at[at, :], w.at[part, :]))
    return gates + bands


def pair_buffers(count, rows, wide):
    width = 2 * count * DV
    return [((rows, width), BF16), ((width, wide), BF16)]


def local_rows(place_ref, rows, out):
    return slice(None) if out.shape[0] == rows else pl.ds(pl.multiple_of(place_ref[0] * rows, rows), rows)


def keep_part(place, turns, rows, gate_z, weight, norm_gain, out, gain, start):
    wide = weight.shape[1]
    count = len(turns)

    def kernel(place_ref, z_hbm, w_hbm, norm_hbm, out, gain, start_ref, sum_ref, norm, *refs):
        away, own, sems = refs[:2], refs[2:4], refs[4]
        moves = [(norm_hbm, norm)] + pair_moves(place_ref, [0], z_hbm, w_hbm, *own)
        copies = started(moves + pair_moves(place_ref, turns, z_hbm, w_hbm, *away), sems)
        waited(copies[:2])
        gated = gated_rows(out, gain, own[0], local_rows(place_ref, rows, out), count, [start_ref], norm[...])
        waited(copies[2:3])
        sum_ref[...] = mm(gated, own[1][...])
        waited(copies[3:])

    vmem = pltpu.MemorySpace.VMEM
    outs = [(vmem, (rows, wide), F32), (vmem, (1, DV), F32)]
    outs += [(vmem, *shape) for shape in pair_buffers(count, rows, wide)]
    scratch = [pltpu.VMEM(*shape) for shape in pair_buffers(1, rows, wide)]
    scratch += [pltpu.SemaphoreType.DMA((3 + 2 * count,))]
    groups = [(pltpu.SMEM, [place]), (pltpu.HBM, [gate_z, weight, norm_gain]), (pltpu.VMEM, [out, gain, start])]
    return call(kernel, "keep_part", groups, outs, scratch, PROJECT_VMEM, 4 * rows * DV * wide)


def send_rows(partial, core, send_refs, stay_ref):
    rows, width = send_refs[0].shape
    one, two = partial[:rows], partial[rows:]
    send = jnp.where(core == 0, two, one).astype(BF16)
    for i, ref in enumerate(send_refs):
        ref[...] = send[:, i * width : (i + 1) * width]
    stay_ref[...] = jnp.where(core == 0, one, two)


def away_part(place, kept, out, gain, starts):
    rows, wide = kept[0].shape

    def kernel(place_ref, sum_ref, norm, z, w, out, gain, *refs):
        start_refs, (send_ref, stay_ref) = refs[:-2], refs[-2:]
        gated = gated_rows(out, gain, z, local_rows(place_ref, rows, out), 0, start_refs, norm[...])
        send_rows(mm(gated, w[...]) + sum_ref[...], place_ref[1], [send_ref], stay_ref)

    vmem = pltpu.MemorySpace.VMEM
    outs = [(vmem, (rows // 2, wide), BF16), (vmem, (rows // 2, wide), F32)]
    groups = [(pltpu.SMEM, [place]), (pltpu.VMEM, [*kept, out, gain, *starts])]
    return call(kernel, "away_part", groups, outs, [], PROJECT_VMEM, 2 * rows * kept[-1].size)


def whole_part(place, turns, rows, gate_z, weight, norm_gain, out, gain, starts):
    wide = weight.shape[1]
    count = len(turns) + 1

    def kernel(place_ref, z_hbm, w_hbm, norm_hbm, out, gain, *refs):
        start_refs, sends, (stay_ref, norm, z, w, sems) = refs[:count], refs[count : count + 2], refs[count + 2 :]
        moves = [(norm_hbm, norm)] + pair_moves(place_ref, (*turns, 0), z_hbm, w_hbm, z, w)
        copies = started(moves, sems)
        waited(copies[: 1 + count])
        gated = gated_rows(out, gain, z, local_rows(place_ref, rows, out), 0, start_refs, norm[...])
        waited(copies[1 + count :])
        send_rows(mm(gated, w[...]), place_ref[1], sends, stay_ref)

    vmem = pltpu.MemorySpace.VMEM
    outs = [(vmem, (rows // 2, wide // 2), BF16)] * 2 + [(vmem, (rows // 2, wide), F32)]
    scratch = [pltpu.VMEM((1, DV), F32)] + [pltpu.VMEM(*shape) for shape in pair_buffers(count, rows, wide)]
    scratch += [pltpu.SemaphoreType.DMA((1 + 2 * count,))]
    groups = [(pltpu.SMEM, [place]), (pltpu.HBM, [gate_z, weight, norm_gain]), (pltpu.VMEM, [out, gain, *starts])]
    return call(kernel, "whole_part", groups, outs, scratch, PROJECT_VMEM, 2 * rows * weight.size)


def on_device(
    query, keys, values, gate_logit, beta_logit, decay_rate, norm_gain, gate_z, out_weight
):
    shards, cores = lax.axis_size("seq"), lax.axis_size("head")
    seq, head = lax.axis_index("seq"), lax.axis_index("head")
    members = query.shape[1] // DK
    turns = sorted(range(1, members), key=lambda turn: (-bin(turn).count("1"), turn))
    pairs = {turn: [(s, s ^ turn) for s in range(shards)] for turn in turns}
    member_at = lax.rem(seq, members)
    member = member_at.reshape(1)
    rate, norm_gain = decay_rate.reshape(1, -1), norm_gain.reshape(1, -1)

    away, earlier, operands = first_part(member, turns, rate, keys, values, gate_logit.T, beta_logit.T)
    others = [lax.ppermute(a, "seq", pairs[turn]) for a, turn in zip(away, turns)]
    own, earlier, mine = second_part(member, operands, earlier)
    groups = shards // members
    order, ending, *total = group_part(member, turns, own, others, groups > 2)

    chips = cores // 2
    chip, core = head // 2, lax.rem(head, 2)
    rows = query.shape[0] // chips
    spots = [jnp.stack([lax.rem(chip + by, chips), core, member_at]) for by in range(chips)]
    apart = rows == CHUNK and chips == 2
    chunks = 1 if apart else query.shape[0] // CHUNK
    spot = spots[1] if apart else jnp.zeros_like(spots[0]).at[2].set(member_at)
    out, gain = third_part(spot, turns, chunks, query, keys, earlier, mine, ending)

    came = []
    for step in range(groups - 1):
        if step:
            start, ending = hop_part(*total, came)
            came = [start]
        along = [(step * members + i, (step + 1) * members + i) for i in range(members)]
        came.append(lax.ppermute(ending, "seq", along))
    if not came:
        came = [jnp.zeros_like(ending)]
    keep, *gives = starts_part(member, turns, order, came, out)
    back = [lax.ppermute(g, "seq", pairs[turn]) for g, turn in zip(gives, turns)]

    swap = [(i, i ^ 1) for i in range(cores)]
    arrived = []
    for by in range(1, chips):
        kept = keep_part(spots[by], turns, rows, gate_z, out_weight, norm_gain, out, gain, keep)
        give, stay = away_part(spots[by], kept, out, gain, back)
        both = (stay + lax.ppermute(give, "head", swap).astype(F32)).astype(BF16)
        arrived.append(lax.ppermute(both, "head", [(i, (i + 2 * by) % cores) for i in range(cores)]))
    spot = spots[0]
    if arrived:
        spot, both = lax.optimization_barrier((spot, both))
    if apart:
        out, gain = third_part(spot, turns, chunks, query, keys, earlier, mine, ending)
    *gives, stay = whole_part(spot, turns, rows, gate_z, out_weight, norm_gain, out, gain, [*back, keep])
    total = stay + jnp.concatenate([lax.ppermute(g, "head", swap) for g in gives], axis=1).astype(F32)
    for part in arrived:
        total = total + part.astype(F32)
    return total.astype(BF16)


def solution(mesh):
    return jax.shard_map(
        on_device,
        mesh=mesh,
        in_specs=(
            P("seq", "head"),
            P("seq", "head"),
            P("seq", "head"),
            P("seq", "head"),
            P("seq", "head"),
            P("head"),
            P(),
            P("seq", "head"),
            P("head", None),
        ),
        out_specs=P(("seq", "head"), None),
        check_vma=False,
    )
```

```python
import jax
import jax.numpy as jnp
from jax import lax
from jax.experimental import pallas as pl
from jax.experimental.pallas import tpu as pltpu
from jax.sharding import PartitionSpec as P

DK = 128
DV = 128
CHUNK = 256
F32 = jnp.float32
BF16 = jnp.bfloat16
NEG = -1e30
SMALL_VMEM = 8 * 1024 * 1024
DELTA_VMEM = 28 * 1024 * 1024
OUTPUT_VMEM = 20 * 1024 * 1024
PROJECT_VMEM = 24 * 1024 * 1024


def mm(left, right):
    return lax.dot_general(left, right, (((1,), (0,)), ((), ())), preferred_element_type=F32)


def mm_nt(left, right):
    return lax.dot_general(left, right, (((1,), (1,)), ((), ())), preferred_element_type=F32)


def iota(shape, dim):
    return lax.broadcasted_iota(jnp.int32, shape, dim)


def split3(x):
    hi = x.astype(BF16).astype(F32)
    mid = (x - hi).astype(BF16).astype(F32)
    return hi, mid, x - hi - mid


def softplus(x):
    small = jnp.exp(-jnp.abs(x))
    one = 1.0 + small
    log1p = jnp.where(one == 1.0, small, jnp.log(one) * (small / jnp.where(one == 1.0, 1.0, one - 1.0)))
    return jnp.maximum(x, 0.0) + log1p


def log_inverse_norm(x, rows):
    square = x.astype(F32) * x.astype(F32)
    high = square.astype(BF16)
    low = (square - high.astype(F32)).astype(BF16)
    ones = jnp.ones((rows, x.shape[1]), BF16)
    return -0.5 * jnp.log(mm_nt(ones, high) + mm_nt(ones, low) + 1e-6)


def odd_rows(x, n):
    return jnp.concatenate([x[i + n : i + 2 * n] for i in range(0, x.shape[0], 2 * n)], axis=0)


def weave(even, odd, n):
    parts = []
    for at in range(0, odd.shape[0], n):
        parts.append(even[2 * at : 2 * at + n])
        parts.append(odd[at : at + n])
    return jnp.concatenate(parts, axis=0)


def as_mask(where):
    return jnp.where(where, 1.0, 0.0).astype(BF16)


def spread(beside):
    half = beside.shape[1] // 2
    zeros = jnp.zeros((half, half), BF16)
    top = jnp.concatenate([beside[:, :half], zeros], axis=1)
    return jnp.concatenate([top, jnp.concatenate([zeros, beside[:, half:]], axis=1)], axis=0)


def unit_lower_inverses(lowers):
    size = lowers[0].shape[0]
    half = size // 2
    row, col = iota((half, size), 0), iota((half, size), 1)
    col = jnp.bitwise_and(col, half - 1)
    crow, ccol = iota((half // 2, size), 0), iota((half // 2, size), 1)
    ccol = jnp.bitwise_and(ccol, half - 1)
    zeros = jnp.zeros((half, size), BF16)
    eye, pair = as_mask(row == col), as_mask(row // 2 == col // 2)
    sides = [jnp.concatenate([lower[:half, :half], lower[half:, half:]], axis=1) for lower in lowers]
    xs = [eye - side * pair for side in sides]
    n = 2
    while n < half:
        if n < 16:
            mask = as_mask((row // n == col // n + 1) & (row // (2 * n) == col // (2 * n)))
            ys = [mm(side * mask, spread(x)).astype(BF16) for side, x in zip(sides, xs)]
            zs = [mm(x, spread(y)).astype(BF16) for x, y in zip(xs, ys)]
            xs = [x - z for x, z in zip(xs, zs)]
        else:
            mask = as_mask(ccol // n == 2 * (crow // n))
            ys = [mm(odd_rows(side, n) * mask, spread(x)).astype(BF16) for side, x in zip(sides, xs)]
            odds = [odd_rows(x, n) for x in xs]
            zs = [mm(odd, spread(weave(zeros, y, n))).astype(BF16) for odd, y in zip(odds, ys)]
            xs = [weave(x, odd - z, n) for x, odd, z in zip(xs, odds, zs)]
        n *= 2
    ys = [mm(lower[half:, :half], x[:, :half]).astype(BF16) for lower, x in zip(lowers, xs)]
    zs = [mm(x[:, half:], y).astype(BF16) for x, y in zip(xs, ys)]
    full = []
    for x, z in zip(xs, zs):
        top = jnp.concatenate([x[:, :half], jnp.zeros((half, half), BF16)], axis=1)
        full.append(jnp.concatenate([top, jnp.concatenate([-z, x[:, half:]], axis=1)], axis=0))
    return full


def decayed(c, b, product, mask):
    h = CHUNK // 2

    def quarter(i, j):
        arg = c[i * h : (i + 1) * h] - b[:, j * h : (j + 1) * h]
        if i == j:
            arg = jnp.where(mask, arg, NEG)
        exact = jnp.exp(arg) * product[i * h : (i + 1) * h, j * h : (j + 1) * h]
        rounded = exact.astype(BF16)
        return rounded, (exact - rounded.astype(F32)).astype(BF16)

    quarters = [quarter(0, 0), quarter(1, 0), quarter(1, 1)]
    results = []
    for a, b, c in zip(*quarters):
        top = jnp.concatenate([a, jnp.zeros((h, h), BF16)], axis=1)
        results.append(jnp.concatenate([top, jnp.concatenate([b, c], axis=1)], axis=0))
    return results


def reordered(x, quarters, first):
    row = iota(x.shape, 0)
    total = jnp.zeros_like(x)
    for j, quarter in enumerate(quarters, first):
        for r in range(2):
            picked = jnp.sum(jnp.where(row == 2 * quarter + r, x, 0.0), axis=0, keepdims=True)
            total = jnp.where(row == 2 * j + r, picked, total)
    return total


def log_norms(refs, heads, first=0):
    tokens = refs[0].shape[0]
    head_row = iota((heads, tokens), 0)
    total = log_inverse_norm(refs[0][...], heads)
    for j, ref in enumerate(refs[1:], first + 1):
        total = jnp.where(head_row < 2 * j, total, log_inverse_norm(ref[...], heads))
    return total


def delta_kernel(waits, rate, gate, beta, quarters, first, k_refs, v_refs, ends_refs, resid_ref, held_ref, cumul_ref, log_ref):
    waited(waits[0])
    tokens = k_refs[0].shape[0]
    heads = gate.shape[0]
    chunks = [slice(at, at + CHUNK) for at in range(0, tokens, CHUNK)]

    diagonal = iota((heads, heads), 0) == iota((heads, heads), 1)
    rate = jnp.sum(jnp.where(diagonal, rate[...], 0.0), axis=1, keepdims=True)
    decay = reordered(-rate * softplus(gate[...]), quarters, first)
    log_beta = reordered(-softplus(-beta[...]), quarters, first)

    row, col = iota((CHUNK, CHUNK), 0), iota((CHUNK, CHUNK), 1)
    upto = jnp.where(row <= col, 1.0, 0.0).astype(BF16)
    sums = mm(
        jnp.concatenate([p for here in chunks for p in split3(decay[:, here])], axis=0).astype(BF16), upto
    )
    square = CHUNK // 2
    strict = iota((square, square), 1) < iota((square, square), 0)

    waited(waits[1])
    log_k = log_norms(k_refs, heads, first)
    waited(waits[2])
    lowers, rests, rights, ended, decays = {}, {}, {}, {}, {}
    for c, here in enumerate(chunks):
        parts = [sums[(3 * c + i) * heads : (3 * c + i + 1) * heads] for i in range(3)]
        cumul = parts[0] + parts[1] + parts[2]
        end = cumul[:, CHUNK - 1 :]
        lb, lk = log_beta[:, here], log_k[:, here]
        col_log = cumul - lk
        row_lower = cumul + lb + lk
        cumul_ref[:, here] = cumul
        log_ref[:, here] = col_log
        key_end = jnp.exp(end - cumul + lk)
        ends = jnp.exp(end)
        columns = jnp.concatenate([row_lower, jnp.exp(lb), jnp.exp(row_lower), key_end], axis=0).T
        for j, (k_ref, v_ref) in enumerate(zip(k_refs, v_refs)):
            k = k_ref[here, :]
            k32 = k.astype(F32)
            turned = k32.T.astype(BF16)
            key_key = mm(k, turned)
            for r in range(2):
                at = 2 * (first + j) + r
                c_lower, c_beta, c_weight, c_end = (
                    columns[:, heads * i + at : heads * i + at + 1] for i in range(4)
                )
                m = (c, 2 * j + r)
                lowers[m], rests[m] = decayed(c_lower, col_log[at : at + 1], key_key, strict)
                v32 = v_ref[here, r * DV : (r + 1) * DV].astype(F32)
                rights[m] = jnp.concatenate([c_beta * v32, c_weight * k32], axis=1).astype(BF16)
                ended[m] = turned, c_end
                decays[m] = ends[at : at + 1]
    names = list(lowers)
    inverses = dict(zip(names, unit_lower_inverses([lowers[m] for m in names])))
    solved = {m: mm(inverses[m], rights[m]) for m in names}
    missed = {m: mm(rests[m], solved[m].astype(BF16)).astype(BF16) for m in names}
    solved = {m: solved[m] - mm(inverses[m], missed[m]) for m in names}
    all_heads = range(2 * len(k_refs))
    state = {}
    for c, here in enumerate(chunks):
        if c == 0:
            resid = {a: jnp.concatenate([solved[c, a][:, :DV], -solved[c, a][:, DV:]], axis=1) for a in all_heads}
            before = iota((DK, DV + DK), 1) == iota((DK, DV + DK), 0) + DV
            before = {a: jnp.where(before, 1.0, 0.0) for a in all_heads}
            for a in all_heads:
                held_ref[a // 2, c, a % 2] = before[a].astype(BF16)
        else:
            held = {a: state[a].astype(BF16) for a in all_heads}
            for a in all_heads:
                held_ref[a // 2, c, a % 2] = held[a]
            moved = {a: mm(solved[c, a][:, DV:].astype(BF16), held[a]) for a in all_heads}
            resid = {
                a: jnp.concatenate([solved[c, a][:, :DV] - moved[a][:, :DV], -moved[a][:, DV:]], axis=1)
                for a in all_heads
            }
            before = state
        for a in all_heads:
            resid_ref[a // 2, c, a % 2] = resid[a].astype(BF16)
        state = {
            a: decays[c, a] * before[a] + mm(ended[c, a][0], (ended[c, a][1] * resid[a]).astype(BF16))
            for a in all_heads
        }
    for a in all_heads:
        ends_refs[a // 2][a % 2] = state[a].astype(BF16)


def local_outputs(q_refs, k_refs, cumul, logs, waits, resid, held, out_ref, gain_ref):
    tokens = q_refs[0].shape[0]
    heads = cumul.shape[0]
    square = CHUNK // 2
    inclusive = iota((square, square), 1) <= iota((square, square), 0)
    row_mix = cumul + log_norms(q_refs, heads)
    mixings, queries = {}, {}
    for c in range(tokens // CHUNK):
        here = slice(c * CHUNK, (c + 1) * CHUNK)
        mix = row_mix[:, here]
        columns = jnp.concatenate([mix, jnp.exp(mix)], axis=0).T
        for j, (q_ref, k_ref) in enumerate(zip(q_refs, k_refs)):
            q, k = q_ref[here, :], k_ref[here, :]
            query_key = mm_nt(q, k)
            q32 = q.astype(F32)
            for a in (2 * j, 2 * j + 1):
                b_row = logs[a : a + 1, here]
                mixings[c, a], _ = decayed(columns[:, a : a + 1], b_row, query_key, inclusive)
                queries[c, a] = (columns[:, heads + a : heads + a + 1] * q32).astype(BF16)
    waited(waits)
    for c, a in mixings:
        here = slice(c * CHUNK, (c + 1) * CHUNK)
        result = mm(queries[c, a], held(c, a)) + mm(mixings[c, a], resid(c, a))
        out_ref[here, a * DV : (a + 1) * DV] = result[:, :DV].astype(BF16)
        gain_ref[here, a * DK : (a + 1) * DK] = result[:, DV:].astype(BF16)


def lanes(source, which, target):
    width = target.shape[1]
    return source.at[:, pl.ds(pl.multiple_of(which * width, 128), width)], target


def started(moves, sems, first=0):
    copies = [pltpu.make_async_copy(a, b, sems.at[first + i]) for i, (a, b) in enumerate(moves)]
    for copy in copies:
        copy.start()
    return copies


def waited(copies):
    for copy in copies:
        copy.wait()


def in_vmem(array):
    return pltpu.with_memory_space_constraint(array, pltpu.VMEM)


def in_hbm(array):
    return pltpu.with_memory_space_constraint(array, pltpu.HBM)


def call(kernel, name, groups, outs, scratch, vmem_bytes, flops):
    specs, args = [], []
    for space, arrays in groups:
        specs += [pl.BlockSpec(memory_space=space)] * len(arrays)
        if space is pltpu.VMEM or space is pltpu.HBM:
            arrays = [pltpu.with_memory_space_constraint(a, space) for a in arrays]
        args += arrays
    return pl.pallas_call(
        kernel,
        in_specs=specs,
        out_specs=[pl.BlockSpec(memory_space=space) for space, _, _ in outs],
        out_shape=[space(shape, kind) for space, shape, kind in outs],
        scratch_shapes=scratch,
        compiler_params=pltpu.CompilerParams(vmem_limit_bytes=vmem_bytes),
        cost_estimate=pl.CostEstimate(flops=flops, bytes_accessed=2**20, transcendentals=0),
        name=name,
    )(*args)


def local_shapes(count, tokens, heads):
    chunks = tokens // CHUNK
    return [
        ((count, chunks, 2, CHUNK, DV + DK), BF16),
        ((count, chunks, 2, DK, DV + DK), BF16),
        ((heads, tokens), F32),
        ((heads, tokens), F32),
    ]


def first_part(member, turns, rate, keys, values, gate_logit, beta_logit):
    heads, tokens = gate_logit.shape
    count = len(turns)
    key_part, value_part = (tokens, DK), (tokens, 2 * DV)

    def kernel(member_ref, rate_hbm, k_hbm, v_hbm, gate_hbm, beta_hbm, *refs):
        ends, (resid, held, cumul, logs, rate, gate, beta, k_own, v_own), refs = (
            refs[:count], refs[count : count + 9], refs[count + 9 :]
        )
        k_refs, v_refs, sems = refs[:count], refs[count : 2 * count], refs[-1]
        quarters = [jnp.bitwise_xor(member_ref[0], turn) for turn in turns]
        moves = [(rate_hbm, rate), (gate_hbm, gate), (beta_hbm, beta)]
        moves += [lanes(k_hbm, q, ref) for q, ref in zip(quarters, k_refs)]
        moves += [lanes(v_hbm, q, ref) for q, ref in zip(quarters, v_refs)]
        moves += [lanes(k_hbm, member_ref[0], k_own), lanes(v_hbm, member_ref[0], v_own)]
        copies = started(moves, sems)
        waits = copies[:3], copies[3 : 3 + count], copies[3 + count : -2]
        delta_kernel(waits, rate, gate, beta, quarters, 0, k_refs, v_refs, ends, resid, held, cumul, logs)
        waited(copies[-2:])

    vmem = pltpu.VMEM
    outs = [(vmem, (2, DK, DV + DK), BF16)] * count
    outs += [(vmem, *shape) for shape in local_shapes(count, tokens, heads)]
    outs += [(vmem, (1, heads), F32), (vmem, (heads, tokens), F32), (vmem, (heads, tokens), F32)]
    outs += [(vmem, key_part, BF16), (vmem, value_part, BF16)]
    outs = [(pltpu.MemorySpace.VMEM, *rest) for _, *rest in outs]
    scratch = [vmem(key_part, BF16)] * count + [vmem(value_part, BF16)] * count
    scratch += [pltpu.SemaphoreType.DMA((5 + 2 * count,))]
    groups = [(pltpu.SMEM, [member]), (pltpu.HBM, [rate, keys, values, gate_logit, beta_logit])]
    result = call(kernel, "first_part", groups, outs, scratch, DELTA_VMEM, 6 * 10**9)
    return result[:count], result[count : count + 4], result[count + 4 :]


def second_part(member, operands, earlier):
    heads, tokens = operands[1].shape

    def kernel(member_ref, rate, gate, beta, k_own, v_own, *refs):
        earlier_refs, (ends,), out_hbm, local, sems = refs[:4], refs[4:5], refs[5:13], refs[13:17], refs[17]
        copies = started(zip(earlier_refs, out_hbm[:4]), sems)
        delta_kernel(
            [[]] * 3, rate, gate, beta, [member_ref[0]], heads // 2 - 1, [k_own], [v_own], [ends], *local
        )
        copies += started(zip(local, out_hbm[4:]), sems, 4)
        waited(copies)

    shapes = local_shapes(1, tokens, heads)
    outs = [(pltpu.MemorySpace.VMEM, (2, DK, DV + DK), BF16)]
    outs += [(pltpu.MemorySpace.HBM, a.shape, a.dtype) for a in earlier]
    outs += [(pltpu.MemorySpace.HBM, *shape) for shape in shapes]
    scratch = [pltpu.VMEM(*shape) for shape in shapes] + [pltpu.SemaphoreType.DMA((8,))]
    groups = [(pltpu.SMEM, [member]), (pltpu.VMEM, [*operands, *earlier])]
    ends, *rest = call(kernel, "second_part", groups, outs, scratch, DELTA_VMEM, 2 * 10**9)
    return ends, rest[:4], rest[4:]


def third_part(place, turns, chunks, query, keys, earlier, own, after):
    count = len(turns) + 1
    tokens = chunks * CHUNK
    heads = 2 * count

    def kernel(place_ref, q_hbm, k_hbm, *refs):
        sources, (_, out, gain), refs = refs[:8], refs[8:11], refs[11:]
        q_refs, k_refs, local, sems = refs[:count], refs[count : 2 * count], refs[2 * count : -1], refs[-1]
        first = place_ref[0] * chunks
        rows = pl.ds(pl.multiple_of(first * CHUNK, CHUNK), tokens)
        quarters = [jnp.bitwise_xor(place_ref[2], turn) for turn in (*turns, 0)]
        moves = []
        for hbm, targets in ((q_hbm, q_refs), (k_hbm, k_refs)):
            for quarter, ref in zip(quarters, targets):
                moves.append((hbm.at[rows, pl.ds(pl.multiple_of(quarter * DK, DK), DK)], ref))
        for i in (2, 3, 6, 7):
            moves.append((sources[i].at[:, rows], local[i]))
        for i in (0, 1, 4, 5):
            moves.append((sources[i].at[:, pl.ds(first, chunks)], local[i]))
        copies = started(moves, sems)
        waited(copies[:-4])
        theirs = iota((heads, tokens), 0) < heads - 2
        cumul = jnp.where(theirs, local[2][...], local[6][...])
        logs = jnp.where(theirs, local[3][...], local[7][...])

        def read(which):
            return lambda c, a: local[which][a // 2, c, a % 2] if a < heads - 2 else local[which + 4][0, c, a % 2]

        local_outputs(q_refs, k_refs, cumul, logs, copies[-4:], read(0), read(1), out, gain)

    outs = [(pltpu.MemorySpace.VMEM, (tokens, heads * DV), BF16)] * 2
    scratch = [pltpu.VMEM((tokens, DK), BF16)] * (2 * count)
    for pairs in (count - 1, 1):
        scratch += [pltpu.VMEM(*shape) for shape in local_shapes(pairs, tokens, heads)]
    scratch += [pltpu.SemaphoreType.DMA((2 * count + 8,))]
    groups = [(pltpu.SMEM, [place]), (pltpu.HBM, [query, keys, *earlier, *own, after])]
    return call(kernel, "third_part", groups, outs, scratch, OUTPUT_VMEM, 3 * 10**9)


def in_order(member_ref, turns, own_ref, other_refs, order_ref):
    order_ref[member_ref[0]] = own_ref[...]
    for turn, ref in zip(turns, other_refs):
        order_ref[jnp.bitwise_xor(member_ref[0], turn)] = ref[...]


def after_shard(ends, state):
    return mm(ends[:, DV:], state.astype(BF16)) + ends[:, :DV].astype(F32)


def group_part(member, turns, own, others, chained):
    count = len(turns) + 1

    def kernel(member_ref, own_ref, *refs):
        other_refs, (order, ending_ref, *total_refs) = refs[: count - 1], refs[count - 1 :]
        in_order(member_ref, turns, own_ref, other_refs, order)
        states = [order[0, h][:, :DV].astype(F32) for h in range(2)]
        for i in range(1, count):
            states = [after_shard(order[i, h], states[h]) for h in range(2)]
        for h in range(2):
            ending_ref[h] = states[h].astype(BF16)
        for total_ref in total_refs:
            for h in range(2):
                transit = order[0, h][:, DV:]
                for i in range(1, count):
                    transit = mm(order[i, h][:, DV:], transit).astype(BF16)
                total_ref[h] = jnp.concatenate([states[h].astype(BF16), transit], axis=1)

    vmem = pltpu.MemorySpace.VMEM
    outs = [(vmem, (count, *own.shape), BF16), (vmem, (2, DK, DV), BF16)]
    if chained:
        outs.append((vmem, own.shape, BF16))
    groups = [(pltpu.SMEM, [member]), (pltpu.VMEM, [own, *others])]
    return call(kernel, "group_part", groups, outs, [], SMALL_VMEM, 10**8)


def hop_part(total, came):
    def kernel(total_ref, *refs):
        sum_ref, out_ref = refs[-2:]
        for h in range(2):
            start = refs[0][h]
            for ref in refs[1:-2]:
                start = start + ref[h]
            sum_ref[h] = start
            out_ref[h] = after_shard(total_ref[h], start).astype(BF16)

    outs = [(pltpu.MemorySpace.VMEM, (2, DK, DV), BF16)] * 2
    return call(kernel, "hop_part", [(pltpu.VMEM, [total, *came])], outs, [], SMALL_VMEM, 10**7)


def starts_part(member, turns, order, came, after):
    count = len(turns) + 1

    def kernel(member_ref, order_ref, *refs):
        came_refs, outs, states_ref = refs[: len(came)], refs[len(came) + 1 : -1], refs[-1]
        states = [came_refs[0][h] for h in range(2)]
        for ref in came_refs[1:]:
            states = [states[h] + ref[h] for h in range(2)]
        for i in range(count):
            for h in range(2):
                states_ref[i, h] = states[h].astype(BF16)
            if i < count - 1:
                states = [after_shard(order_ref[i, h], states[h]) for h in range(2)]
        for turn, ref in zip((0, *turns), outs):
            ref[...] = states_ref[jnp.bitwise_xor(member_ref[0], turn)]

    state = (2, DK, DV)
    outs = [(pltpu.MemorySpace.VMEM, state, BF16)] * count
    groups = [(pltpu.SMEM, [member]), (pltpu.VMEM, [order, *came]), (pltpu.VMEM, [after])]
    return call(kernel, "starts_part", groups, outs, [pltpu.VMEM((count, *state), BF16)], SMALL_VMEM, 10**8)


def gates(z, norm):
    halved = 0.5 * z.astype(F32)
    return halved * (1.0 + jnp.tanh(halved)) * norm


def gated_pairs(out, gain, gate, at, first, start_refs):
    pairs = []
    ones = jnp.full((DV, DV), 1.0 / DV, BF16)
    for j, start_ref in enumerate(start_refs):
        parts = []
        for r in range(2):
            cols = slice((2 * j + r) * DV, (2 * j + r + 1) * DV)
            local = slice((2 * (first + j) + r) * DV, (2 * (first + j) + r + 1) * DV)
            rows = [jnp.concatenate([ref[i, local] for i, _ in at], axis=0) for ref in (out, gain)]
            core = rows[0].astype(F32) + mm(rows[1], start_ref[r])
            mean = mm((core * core).astype(BF16), ones)
            weight = jnp.concatenate([gate[i, cols] for _, i in at], axis=0)
            parts.append((core * lax.rsqrt(mean + 1e-6) * weight).astype(BF16))
        pairs.append(jnp.concatenate(parts, axis=1))
    return pairs


def pair_moves(place_ref, turns, z_hbm, w_hbm, z, w):
    rows, width = z.shape[0], 2 * DV
    here = pl.ds(pl.multiple_of(place_ref[0] * rows, rows), rows)
    gates, bands = [], []
    for j, turn in enumerate(turns):
        at = pl.ds(pl.multiple_of(jnp.bitwise_xor(place_ref[2], turn) * width, width), width)
        part = slice(j * width, (j + 1) * width)
        gates.append((z_hbm.at[here, at], z.at[:, part]))
        bands.append((w_hbm.at[at, :], w.at[part, :]))
    return gates + bands


def pair_buffers(count, rows, wide):
    width = 2 * count * DV
    return [((rows, width), BF16), ((width, wide), BF16)]


def core_rows(place_ref, rows, out):
    half = rows // 2
    slices = []
    for core in (1 - place_ref[1], place_ref[1]):
        chip = 0 if out.shape[0] == rows else place_ref[0] * rows
        slices.append([pl.ds(pl.multiple_of(start + core * half, half), half) for start in (chip, 0)])
    return slices


def projected(pairs, w):
    width = 2 * DV
    total = None
    for j, gated in enumerate(pairs):
        term = mm(gated, w[j * width : (j + 1) * width, :])
        total = term if total is None else total + term
    return total


def keep_part(place, turns, rows, gate_z, weight, norm_gain, out, gain, start):
    wide = weight.shape[1]
    count = len(turns)

    def kernel(place_ref, z_hbm, w_hbm, norm_hbm, out, gain, start_ref, sum_ref, gate_ref, w_away, *refs):
        norm, own_gate, z_away, z_own, w_own, sems = refs
        moves = [(norm_hbm, norm)] + pair_moves(place_ref, [0], z_hbm, w_hbm, z_own, w_own)
        copies = started(moves + pair_moves(place_ref, turns, z_hbm, w_hbm, z_away, w_away), sems)
        waited(copies[:2])
        for h in range(2):
            cols = slice(h * DV, (h + 1) * DV)
            own_gate[:, cols] = gates(z_own[:, cols], norm[...])
        pairs = gated_pairs(out, gain, own_gate, core_rows(place_ref, rows, out), count, [start_ref])
        waited(copies[2 : 3 + count])
        for h in range(2 * count):
            cols = slice(h * DV, (h + 1) * DV)
            gate_ref[:, cols] = gates(z_away[:, cols], norm[...])
        sum_ref[...] = projected(pairs, w_own)
        waited(copies[3 + count :])

    vmem = pltpu.MemorySpace.VMEM
    (z_shape, _), (w_shape, _) = pair_buffers(count, rows, wide)
    outs = [(vmem, (rows, wide), F32), (vmem, z_shape, F32), (vmem, w_shape, BF16)]
    scratch = [pltpu.VMEM((1, DV), F32), pltpu.VMEM((rows, 2 * DV), F32), pltpu.VMEM(z_shape, BF16)]
    scratch += [pltpu.VMEM(*shape) for shape in pair_buffers(1, rows, wide)]
    scratch += [pltpu.SemaphoreType.DMA((3 + 2 * count,))]
    groups = [(pltpu.SMEM, [place]), (pltpu.HBM, [gate_z, weight, norm_gain]), (pltpu.VMEM, [out, gain, start])]
    return call(kernel, "keep_part", groups, outs, scratch, PROJECT_VMEM, 4 * rows * DV * wide)


def away_part(place, kept, out, gain, starts):
    rows, wide = kept[0].shape

    def kernel(place_ref, sum_ref, gate, w, out, gain, *refs):
        start_refs, (send_ref, stay_ref) = refs[:-2], refs[-2:]
        pairs = gated_pairs(out, gain, gate, core_rows(place_ref, rows, out), 0, start_refs)
        partial = projected(pairs, w) + sum_ref[...]
        send_ref[...] = partial[: rows // 2].astype(BF16)
        stay_ref[...] = partial[rows // 2 :]

    vmem = pltpu.MemorySpace.VMEM
    outs = [(vmem, (rows // 2, wide), BF16), (vmem, (rows // 2, wide), F32)]
    groups = [(pltpu.SMEM, [place]), (pltpu.VMEM, [*kept, out, gain, *starts])]
    return call(kernel, "away_part", groups, outs, [], PROJECT_VMEM, 2 * rows * kept[-1].size)


def whole_part(place, turns, rows, gate_z, weight, norm_gain, out, gain, starts):
    wide = weight.shape[1]
    count = len(turns) + 1

    def kernel(place_ref, z_hbm, w_hbm, norm_hbm, out, gain, *refs):
        start_refs, sends, (stay_ref, norm, gate, z, w, sems) = refs[:count], refs[count : count + 2], refs[count + 2 :]
        moves = [(norm_hbm, norm)] + pair_moves(place_ref, (*turns, 0), z_hbm, w_hbm, z, w)
        copies = started(moves, sems)
        waited(copies[: 1 + count])
        for h in range(2 * count):
            cols = slice(h * DV, (h + 1) * DV)
            gate[:, cols] = gates(z[:, cols], norm[...])
        pairs = gated_pairs(out, gain, gate, core_rows(place_ref, rows, out), 0, start_refs)
        waited(copies[1 + count :])
        partial = projected(pairs, w)
        for i, ref in enumerate(sends):
            ref[...] = partial[: rows // 2, i * (wide // 2) : (i + 1) * (wide // 2)].astype(BF16)
        stay_ref[...] = partial[rows // 2 :]

    vmem = pltpu.MemorySpace.VMEM
    outs = [(vmem, (rows // 2, wide // 2), BF16)] * 2 + [(vmem, (rows // 2, wide), F32)]
    (z_shape, _), _ = pair_buffers(count, rows, wide)
    scratch = [pltpu.VMEM((1, DV), F32), pltpu.VMEM(z_shape, F32)]
    scratch += [pltpu.VMEM(*shape) for shape in pair_buffers(count, rows, wide)]
    scratch += [pltpu.SemaphoreType.DMA((1 + 2 * count,))]
    groups = [(pltpu.SMEM, [place]), (pltpu.HBM, [gate_z, weight, norm_gain]), (pltpu.VMEM, [out, gain, *starts])]
    return call(kernel, "whole_part", groups, outs, scratch, PROJECT_VMEM, 2 * rows * weight.size)


def on_device(
    query, keys, values, gate_logit, beta_logit, decay_rate, norm_gain, gate_z, out_weight
):
    shards, cores = lax.axis_size("seq"), lax.axis_size("head")
    seq, head = lax.axis_index("seq"), lax.axis_index("head")
    members = query.shape[1] // DK
    turns = sorted(range(1, members), key=lambda turn: (-bin(turn).count("1"), turn))
    pairs = {turn: [(s, s ^ turn) for s in range(shards)] for turn in turns}
    member_at = lax.rem(seq, members)
    member = member_at.reshape(1)
    rate, norm_gain = decay_rate.reshape(1, -1), norm_gain.reshape(1, -1)

    away, earlier, operands = first_part(member, turns, rate, keys, values, gate_logit.T, beta_logit.T)
    others = [lax.ppermute(a, "seq", pairs[turn]) for a, turn in zip(away, turns)]
    own, earlier, mine = second_part(member, operands, earlier)
    groups = shards // members
    order, ending, *total = group_part(member, turns, own, others, groups > 2)

    chips = cores // 2
    chip, core = head // 2, lax.rem(head, 2)
    rows = query.shape[0] // chips
    spots = [jnp.stack([lax.rem(chip + by, chips), core, member_at]) for by in range(chips)]
    apart = rows == CHUNK and chips == 2
    chunks = 1 if apart else query.shape[0] // CHUNK
    spot = spots[1] if apart else jnp.zeros_like(spots[0]).at[2].set(member_at)
    out, gain = third_part(spot, turns, chunks, query, keys, earlier, mine, ending)

    came = []
    for step in range(groups - 1):
        if step:
            start, ending = hop_part(*total, came)
            came = [start]
        along = [(step * members + i, (step + 1) * members + i) for i in range(members)]
        came.append(lax.ppermute(ending, "seq", along))
    if not came:
        came = [jnp.zeros_like(ending)]
    keep, *gives = starts_part(member, turns, order, came, out)
    back = [lax.ppermute(g, "seq", pairs[turn]) for g, turn in zip(gives, turns)]

    swap = [(i, i ^ 1) for i in range(cores)]
    arrived = []
    for by in range(1, chips):
        kept = keep_part(spots[by], turns, rows, gate_z, out_weight, norm_gain, out, gain, keep)
        give, stay = away_part(spots[by], kept, out, gain, back)
        both = (stay + lax.ppermute(give, "head", swap).astype(F32)).astype(BF16)
        arrived.append(lax.ppermute(both, "head", [(i, (i + 2 * by) % cores) for i in range(cores)]))
    spot = spots[0]
    if arrived:
        spot, both = lax.optimization_barrier((spot, both))
    if apart:
        out, gain = third_part(spot, turns, chunks, query, keys, earlier, mine, ending)
    *gives, stay = whole_part(spot, turns, rows, gate_z, out_weight, norm_gain, out, gain, [*back, keep])
    total = stay + jnp.concatenate([lax.ppermute(g, "head", swap) for g in gives], axis=1).astype(F32)
    for part in arrived:
        total = total + part.astype(F32)
    return total.astype(BF16)


def solution(mesh):
    return jax.shard_map(
        on_device,
        mesh=mesh,
        in_specs=(
            P("seq", "head"),
            P("seq", "head"),
            P("seq", "head"),
            P("seq", "head"),
            P("seq", "head"),
            P("head"),
            P(),
            P("seq", "head"),
            P("head", None),
        ),
        out_specs=P(("seq", "head"), None),
        check_vma=False,
    )
```

```python
import jax
import jax.numpy as jnp
from jax import lax
from jax.experimental import pallas as pl
from jax.experimental.pallas import tpu as pltpu
from jax.sharding import PartitionSpec as P

DK = 128
DV = 128
CHUNK = 256
F32 = jnp.float32
BF16 = jnp.bfloat16
NEG = -1e30
SMALL_VMEM = 8 * 1024 * 1024
DELTA_VMEM = 28 * 1024 * 1024
OUTPUT_VMEM = 20 * 1024 * 1024
PROJECT_VMEM = 24 * 1024 * 1024


def mm(left, right):
    return lax.dot_general(left, right, (((1,), (0,)), ((), ())), preferred_element_type=F32)


def mm_nt(left, right):
    return lax.dot_general(left, right, (((1,), (1,)), ((), ())), preferred_element_type=F32)


def iota(shape, dim):
    return lax.broadcasted_iota(jnp.int32, shape, dim)


def split3(x):
    hi = x.astype(BF16).astype(F32)
    mid = (x - hi).astype(BF16).astype(F32)
    return hi, mid, x - hi - mid


def softplus(x):
    small = jnp.exp(-jnp.abs(x))
    one = 1.0 + small
    log1p = jnp.where(one == 1.0, small, jnp.log(one) * (small / jnp.where(one == 1.0, 1.0, one - 1.0)))
    return jnp.maximum(x, 0.0) + log1p


def log_inverse_norm(x, rows):
    square = x.astype(F32) * x.astype(F32)
    high = square.astype(BF16)
    low = (square - high.astype(F32)).astype(BF16)
    ones = jnp.ones((rows, x.shape[1]), BF16)
    return -0.5 * jnp.log(mm_nt(ones, high) + mm_nt(ones, low) + 1e-6)


def odd_rows(x, n):
    return jnp.concatenate([x[i + n : i + 2 * n] for i in range(0, x.shape[0], 2 * n)], axis=0)


def weave(even, odd, n):
    parts = []
    for at in range(0, odd.shape[0], n):
        parts.append(even[2 * at : 2 * at + n])
        parts.append(odd[at : at + n])
    return jnp.concatenate(parts, axis=0)


def as_mask(where):
    return jnp.where(where, 1.0, 0.0).astype(BF16)


def spread(beside):
    half = beside.shape[1] // 2
    zeros = jnp.zeros((half, half), BF16)
    top = jnp.concatenate([beside[:, :half], zeros], axis=1)
    return jnp.concatenate([top, jnp.concatenate([zeros, beside[:, half:]], axis=1)], axis=0)


def unit_lower_inverses(lowers):
    size = lowers[0].shape[0]
    half = size // 2
    row, col = iota((half, size), 0), iota((half, size), 1)
    col = jnp.bitwise_and(col, half - 1)
    crow, ccol = iota((half // 2, size), 0), iota((half // 2, size), 1)
    ccol = jnp.bitwise_and(ccol, half - 1)
    zeros = jnp.zeros((half, size), BF16)
    eye, pair = as_mask(row == col), as_mask(row // 2 == col // 2)
    sides = [jnp.concatenate([lower[:half, :half], lower[half:, half:]], axis=1) for lower in lowers]
    xs = [eye - side * pair for side in sides]
    n = 2
    while n < half:
        if n < 16:
            mask = as_mask((row // n == col // n + 1) & (row // (2 * n) == col // (2 * n)))
            ys = [mm(side * mask, spread(x)).astype(BF16) for side, x in zip(sides, xs)]
            zs = [mm(x, spread(y)).astype(BF16) for x, y in zip(xs, ys)]
            xs = [x - z for x, z in zip(xs, zs)]
        else:
            mask = as_mask(ccol // n == 2 * (crow // n))
            ys = [mm(odd_rows(side, n) * mask, spread(x)).astype(BF16) for side, x in zip(sides, xs)]
            odds = [odd_rows(x, n) for x in xs]
            zs = [mm(odd, spread(weave(zeros, y, n))).astype(BF16) for odd, y in zip(odds, ys)]
            xs = [weave(x, odd - z, n) for x, odd, z in zip(xs, odds, zs)]
        n *= 2
    ys = [mm(lower[half:, :half], x[:, :half]).astype(BF16) for lower, x in zip(lowers, xs)]
    zs = [mm(x[:, half:], y).astype(BF16) for x, y in zip(xs, ys)]
    full = []
    for x, z in zip(xs, zs):
        top = jnp.concatenate([x[:, :half], jnp.zeros((half, half), BF16)], axis=1)
        full.append(jnp.concatenate([top, jnp.concatenate([-z, x[:, half:]], axis=1)], axis=0))
    return full


def decayed(c, b, product, mask):
    h = CHUNK // 2

    def quarter(i, j):
        arg = c[i * h : (i + 1) * h] - b[:, j * h : (j + 1) * h]
        if i == j:
            arg = jnp.where(mask, arg, NEG)
        exact = jnp.exp(arg) * product[i * h : (i + 1) * h, j * h : (j + 1) * h]
        rounded = exact.astype(BF16)
        return rounded, (exact - rounded.astype(F32)).astype(BF16)

    quarters = [quarter(0, 0), quarter(1, 0), quarter(1, 1)]
    results = []
    for a, b, c in zip(*quarters):
        top = jnp.concatenate([a, jnp.zeros((h, h), BF16)], axis=1)
        results.append(jnp.concatenate([top, jnp.concatenate([b, c], axis=1)], axis=0))
    return results


def reordered(x, quarters, first):
    row = iota(x.shape, 0)
    total = jnp.zeros_like(x)
    for j, quarter in enumerate(quarters, first):
        for r in range(2):
            picked = jnp.sum(jnp.where(row == 2 * quarter + r, x, 0.0), axis=0, keepdims=True)
            total = jnp.where(row == 2 * j + r, picked, total)
    return total


def log_norms(refs, heads, first=0):
    tokens = refs[0].shape[0]
    head_row = iota((heads, tokens), 0)
    total = log_inverse_norm(refs[0][...], heads)
    for j, ref in enumerate(refs[1:], first + 1):
        total = jnp.where(head_row < 2 * j, total, log_inverse_norm(ref[...], heads))
    return total


def delta_kernel(waits, rate, gate, beta, quarters, first, k_refs, v_refs, ends_refs, work_ref, marks_ref):
    waited(waits[0])
    tokens = k_refs[0].shape[0]
    heads = gate.shape[0]
    chunks = [slice(at, at + CHUNK) for at in range(0, tokens, CHUNK)]

    diagonal = iota((heads, heads), 0) == iota((heads, heads), 1)
    rate = jnp.sum(jnp.where(diagonal, rate[...], 0.0), axis=1, keepdims=True)
    decay = reordered(-rate * softplus(gate[...]), quarters, first)
    log_beta = reordered(-softplus(-beta[...]), quarters, first)

    row, col = iota((CHUNK, CHUNK), 0), iota((CHUNK, CHUNK), 1)
    upto = jnp.where(row <= col, 1.0, 0.0).astype(BF16)
    sums = mm(
        jnp.concatenate([p for here in chunks for p in split3(decay[:, here])], axis=0).astype(BF16), upto
    )
    square = CHUNK // 2
    strict = iota((square, square), 1) < iota((square, square), 0)

    waited(waits[1])
    log_k = log_norms(k_refs, heads, first)
    waited(waits[2])
    lowers, rests, rights, ended, decays = {}, {}, {}, {}, {}
    for c, here in enumerate(chunks):
        parts = [sums[(3 * c + i) * heads : (3 * c + i + 1) * heads] for i in range(3)]
        cumul = parts[0] + parts[1] + parts[2]
        end = cumul[:, CHUNK - 1 :]
        lb, lk = log_beta[:, here], log_k[:, here]
        col_log = cumul - lk
        row_lower = cumul + lb + lk
        marks_ref[:heads, here] = cumul
        marks_ref[heads:, here] = col_log
        key_end = jnp.exp(end - cumul + lk)
        ends = jnp.exp(end)
        columns = jnp.concatenate([row_lower, jnp.exp(lb), jnp.exp(row_lower), key_end], axis=0).T
        for j, (k_ref, v_ref) in enumerate(zip(k_refs, v_refs)):
            k = k_ref[here, :]
            k32 = k.astype(F32)
            turned = k32.T.astype(BF16)
            key_key = mm(k, turned)
            for r in range(2):
                at = 2 * (first + j) + r
                c_lower, c_beta, c_weight, c_end = (
                    columns[:, heads * i + at : heads * i + at + 1] for i in range(4)
                )
                m = (c, 2 * j + r)
                lowers[m], rests[m] = decayed(c_lower, col_log[at : at + 1], key_key, strict)
                v32 = v_ref[here, r * DV : (r + 1) * DV].astype(F32)
                rights[m] = jnp.concatenate([c_beta * v32, c_weight * k32], axis=1).astype(BF16)
                ended[m] = turned, c_end
                decays[m] = ends[at : at + 1]
    names = list(lowers)
    inverses = dict(zip(names, unit_lower_inverses([lowers[m] for m in names])))
    solved = {m: mm(inverses[m], rights[m]) for m in names}
    missed = {m: mm(rests[m], solved[m].astype(BF16)).astype(BF16) for m in names}
    solved = {m: solved[m] - mm(inverses[m], missed[m]) for m in names}
    all_heads = range(2 * len(k_refs))
    state = {}
    for c, here in enumerate(chunks):
        if c == 0:
            resid = {a: jnp.concatenate([solved[c, a][:, :DV], -solved[c, a][:, DV:]], axis=1) for a in all_heads}
            before = iota((DK, DV + DK), 1) == iota((DK, DV + DK), 0) + DV
            before = {a: jnp.where(before, 1.0, 0.0) for a in all_heads}
            for a in all_heads:
                work_ref[a // 2, c, a % 2, CHUNK:, :] = before[a].astype(BF16)
        else:
            held = {a: state[a].astype(BF16) for a in all_heads}
            for a in all_heads:
                work_ref[a // 2, c, a % 2, CHUNK:, :] = held[a]
            moved = {a: mm(solved[c, a][:, DV:].astype(BF16), held[a]) for a in all_heads}
            resid = {
                a: jnp.concatenate([solved[c, a][:, :DV] - moved[a][:, :DV], -moved[a][:, DV:]], axis=1)
                for a in all_heads
            }
            before = state
        for a in all_heads:
            work_ref[a // 2, c, a % 2, :CHUNK, :] = resid[a].astype(BF16)
        state = {
            a: decays[c, a] * before[a] + mm(ended[c, a][0], (ended[c, a][1] * resid[a]).astype(BF16))
            for a in all_heads
        }
    for a in all_heads:
        ends_refs[a // 2][a % 2] = state[a].astype(BF16)


def local_outputs(q_refs, k_refs, cumul, logs, waits, resid, held, out_ref, gain_ref):
    tokens = q_refs[0].shape[0]
    heads = cumul.shape[0]
    square = CHUNK // 2
    inclusive = iota((square, square), 1) <= iota((square, square), 0)
    row_mix = cumul + log_norms(q_refs, heads)
    mixings, queries = {}, {}
    for c in range(tokens // CHUNK):
        here = slice(c * CHUNK, (c + 1) * CHUNK)
        mix = row_mix[:, here]
        columns = jnp.concatenate([mix, jnp.exp(mix)], axis=0).T
        for j, (q_ref, k_ref) in enumerate(zip(q_refs, k_refs)):
            q, k = q_ref[here, :], k_ref[here, :]
            query_key = mm_nt(q, k)
            q32 = q.astype(F32)
            for a in (2 * j, 2 * j + 1):
                b_row = logs[a : a + 1, here]
                mixings[c, a], _ = decayed(columns[:, a : a + 1], b_row, query_key, inclusive)
                queries[c, a] = (columns[:, heads + a : heads + a + 1] * q32).astype(BF16)
    waited(waits)
    for c, a in mixings:
        here = slice(c * CHUNK, (c + 1) * CHUNK)
        result = mm(queries[c, a], held(c, a)) + mm(mixings[c, a], resid(c, a))
        out_ref[here, a * DV : (a + 1) * DV] = result[:, :DV].astype(BF16)
        gain_ref[here, a * DK : (a + 1) * DK] = result[:, DV:].astype(BF16)


def started(moves, sems, first=0):
    copies = [pltpu.make_async_copy(a, b, sems.at[first + i]) for i, (a, b) in enumerate(moves)]
    for copy in copies:
        copy.start()
    return copies


def waited(copies):
    for copy in copies:
        copy.wait()


def in_vmem(array):
    return pltpu.with_memory_space_constraint(array, pltpu.VMEM)


def in_hbm(array):
    return pltpu.with_memory_space_constraint(array, pltpu.HBM)


def call(kernel, name, groups, outs, scratch, vmem_bytes, flops):
    specs, args = [], []
    for space, arrays in groups:
        specs += [pl.BlockSpec(memory_space=space)] * len(arrays)
        if space is pltpu.VMEM or space is pltpu.HBM:
            arrays = [pltpu.with_memory_space_constraint(a, space) for a in arrays]
        args += arrays
    return pl.pallas_call(
        kernel,
        in_specs=specs,
        out_specs=[pl.BlockSpec(memory_space=space) for space, _, _ in outs],
        out_shape=[space(shape, kind) for space, shape, kind in outs],
        scratch_shapes=scratch,
        compiler_params=pltpu.CompilerParams(vmem_limit_bytes=vmem_bytes),
        cost_estimate=pl.CostEstimate(flops=flops, bytes_accessed=2**20, transcendentals=0),
        name=name,
    )(*args)


def local_shapes(count, tokens, heads):
    chunks = tokens // CHUNK
    return [((count, chunks, 2, CHUNK + DK, DV + DK), BF16), ((2 * heads, tokens), F32)]


def pair_lanes(ref, quarter, width):
    return ref.at[:, pl.ds(pl.multiple_of(quarter * width, width), width)]


def first_part(code, turns, rate, keys, values, gate_logit, beta_logit):
    heads, tokens = gate_logit.shape
    count = len(turns)

    def kernel(code_ref, rate_hbm, gate_hbm, beta_hbm, k_hbm, v_hbm, *refs):
        ends, (work, marks, rate, gate, beta, k_own, v_own), refs = refs[:count], refs[count : count + 7], refs[count + 7 :]
        k_refs, v_refs, sems = refs[:count], refs[count : 2 * count], refs[-1]
        pair = jnp.bitwise_and(code_ref[0], count)
        quarters = [jnp.bitwise_xor(pair, turn) for turn in turns]
        moves = [(rate_hbm, rate), (gate_hbm, gate), (beta_hbm, beta)]
        moves += [(pair_lanes(k_hbm, q, DK), ref) for q, ref in zip(quarters, k_refs)]
        moves += [(pair_lanes(v_hbm, q, 2 * DV), ref) for q, ref in zip(quarters, v_refs)]
        moves += [(pair_lanes(k_hbm, pair, DK), k_own), (pair_lanes(v_hbm, pair, 2 * DV), v_own)]
        copies = started(moves, sems)
        waits = copies[:3], copies[3 : 3 + count], copies[3 + count : -2]
        delta_kernel(waits, rate, gate, beta, quarters, 0, k_refs, v_refs, ends, work, marks)
        waited(copies[-2:])

    vmem = pltpu.MemorySpace.VMEM
    outs = [(vmem, (2, DK, DV + DK), BF16)] * count
    outs += [(vmem, *shape) for shape in local_shapes(count, tokens, heads)]
    outs += [(vmem, a.shape, a.dtype) for a in (rate, gate_logit, beta_logit)]
    outs += [(vmem, (tokens, DK), BF16), (vmem, (tokens, 2 * DV), BF16)]
    groups = [(pltpu.SMEM, [code]), (pltpu.HBM, [rate, gate_logit, beta_logit, keys, values])]
    scratch = [pltpu.VMEM((tokens, DK), BF16)] * count + [pltpu.VMEM((tokens, 2 * DV), BF16)] * count
    scratch += [pltpu.SemaphoreType.DMA((5 + 2 * count,))]
    result = call(kernel, "first_part", groups, outs, scratch, DELTA_VMEM, 6 * 10**9)
    return result[:count], result[count : count + 2], result[count + 2 :]


def chunk_moves(first, chunks, sources, targets):
    (q_hbm, k_hbm, work, marks), (q, k, work_to, marks_to) = sources, targets
    rows = pl.ds(pl.multiple_of(first * CHUNK, CHUNK), chunks * CHUNK)
    return [
        (q_hbm.at[rows, :], q),
        (k_hbm.at[rows, :], k),
        (marks.at[:, rows], marks_to),
        (work.at[:, pl.ds(first, chunks)], work_to),
    ]


def chunk_shapes(chunks, pairs, width):
    tokens = chunks * CHUNK
    return [((tokens, width), BF16)] * 2 + local_shapes(pairs - 1, tokens, 2 * pairs)


def second_part(code, chunks, operands, earlier, query, keys):
    heads, tokens = operands[1].shape
    near = chunk_shapes(chunks, heads // 2, query.shape[1])

    def kernel(code_ref, q_hbm, k_hbm, rate, gate, beta, k_own, v_own, *refs):
        earlier_refs, (ends, *local), out_hbm, targets, sems = refs[:2], refs[2:5], refs[5:7], refs[7:11], refs[11]
        moves = chunk_moves(code_ref[0] // (heads // 2), chunks, (q_hbm, k_hbm, *earlier_refs), targets)
        copies = started([*moves, *zip(earlier_refs, out_hbm)], sems)
        pair = jnp.bitwise_and(code_ref[0], heads // 2 - 1)
        delta_kernel([[]] * 3, rate, gate, beta, [pair], heads // 2 - 1, [k_own], [v_own], [ends], *local)
        waited(copies)

    vmem = pltpu.MemorySpace.VMEM
    outs = [(vmem, (2, DK, DV + DK), BF16)] + [(vmem, *shape) for shape in local_shapes(1, tokens, heads)]
    outs += [(pltpu.MemorySpace.HBM, a.shape, a.dtype) for a in earlier]
    outs += [(vmem, *shape) for shape in near]
    scratch = [pltpu.SemaphoreType.DMA((6,))]
    groups = [(pltpu.SMEM, [code]), (pltpu.HBM, [query, keys]), (pltpu.VMEM, [*operands, *earlier])]
    ends, work, marks, *rest = call(kernel, "second_part", groups, outs, scratch, DELTA_VMEM, 2 * 10**9)
    return ends, [work, marks], rest[:2], rest[2:]


def third_part(place, turns, chunks, sources, near, own, after):
    count = len(turns) + 1
    tokens = chunks * CHUNK
    heads = 2 * count

    def kernel(place_ref, *refs):
        sources, (own_work, own_marks), (out, gain), scratch = refs[:4], refs[4:6], refs[7:9], refs[9:]
        first = place_ref[0] * chunks
        local, copies = sources, []
        if not near:
            local = scratch[:4]
            copies = started(chunk_moves(first, chunks, sources, local), scratch[4])
            waited(copies[:3])
        q, k, work, marks = local
        quarters = [jnp.bitwise_xor(place_ref[2], turn) for turn in (*turns, 0)]
        q_refs = [pair_lanes(q, quarter, DK) for quarter in quarters]
        k_refs = [pair_lanes(k, quarter, DK) for quarter in quarters]
        own_here = own_marks[:, pl.ds(pl.multiple_of(first * CHUNK, CHUNK), tokens)]
        theirs = iota((heads, tokens), 0) < heads - 2
        cumul = jnp.where(theirs, marks[:heads, :], own_here[:heads])
        logs = jnp.where(theirs, marks[heads:, :], own_here[heads:])

        def read(rows):
            def block(c, a):
                if a < heads - 2:
                    return work[a // 2, c, a % 2, rows, :]
                return own_work[0, first + c, a % 2, rows, :]

            return block

        resid, held = read(slice(0, CHUNK)), read(slice(CHUNK, CHUNK + DK))
        local_outputs(q_refs, k_refs, cumul, logs, copies[3:], resid, held, out, gain)

    outs = [(pltpu.MemorySpace.VMEM, (tokens, heads * DV), BF16)] * 2
    scratch = []
    if not near:
        scratch = [pltpu.VMEM(*shape) for shape in chunk_shapes(chunks, count, sources[0].shape[1])]
        scratch += [pltpu.SemaphoreType.DMA((4,))]
    groups = [(pltpu.SMEM, [place]), (pltpu.VMEM if near else pltpu.HBM, sources), (pltpu.VMEM, own)]
    groups += [(pltpu.HBM, [after])]
    return call(kernel, "third_part", groups, outs, scratch, OUTPUT_VMEM, 3 * 10**9)


def in_order(member_ref, turns, own_ref, other_refs, order_ref):
    order_ref[member_ref[0]] = own_ref[...]
    for turn, ref in zip(turns, other_refs):
        order_ref[jnp.bitwise_xor(member_ref[0], turn)] = ref[...]


def after_shard(ends, state):
    return mm(ends[:, DV:], state.astype(BF16)) + ends[:, :DV].astype(F32)


def group_part(member, turns, own, others, chained):
    count = len(turns) + 1

    def kernel(member_ref, own_ref, *refs):
        other_refs, (order, ending_ref, *total_refs) = refs[: count - 1], refs[count - 1 :]
        in_order(member_ref, turns, own_ref, other_refs, order)
        states = [order[0, h][:, :DV].astype(F32) for h in range(2)]
        for i in range(1, count):
            states = [after_shard(order[i, h], states[h]) for h in range(2)]
        for h in range(2):
            ending_ref[h] = states[h].astype(BF16)
        for total_ref in total_refs:
            for h in range(2):
                transit = order[0, h][:, DV:]
                for i in range(1, count):
                    transit = mm(order[i, h][:, DV:], transit).astype(BF16)
                total_ref[h] = jnp.concatenate([states[h].astype(BF16), transit], axis=1)

    vmem = pltpu.MemorySpace.VMEM
    outs = [(vmem, (count, *own.shape), BF16), (vmem, (2, DK, DV), BF16)]
    if chained:
        outs.append((vmem, own.shape, BF16))
    groups = [(pltpu.SMEM, [member]), (pltpu.VMEM, [own, *others])]
    return call(kernel, "group_part", groups, outs, [], SMALL_VMEM, 10**8)


def hop_part(total, came):
    def kernel(total_ref, *refs):
        sum_ref, out_ref = refs[-2:]
        for h in range(2):
            start = refs[0][h]
            for ref in refs[1:-2]:
                start = start + ref[h]
            sum_ref[h] = start
            out_ref[h] = after_shard(total_ref[h], start).astype(BF16)

    outs = [(pltpu.MemorySpace.VMEM, (2, DK, DV), BF16)] * 2
    return call(kernel, "hop_part", [(pltpu.VMEM, [total, *came])], outs, [], SMALL_VMEM, 10**7)


def starts_part(member, turns, order, came, after):
    count = len(turns) + 1

    def kernel(member_ref, order_ref, *refs):
        came_refs, outs, states_ref = refs[: len(came)], refs[len(came) + 1 : -1], refs[-1]
        states = [came_refs[0][h] for h in range(2)]
        for ref in came_refs[1:]:
            states = [states[h] + ref[h] for h in range(2)]
        for i in range(count):
            for h in range(2):
                states_ref[i, h] = states[h].astype(BF16)
            if i < count - 1:
                states = [after_shard(order_ref[i, h], states[h]) for h in range(2)]
        for turn, ref in zip((0, *turns), outs):
            ref[...] = states_ref[jnp.bitwise_xor(member_ref[0], turn)]

    state = (2, DK, DV)
    outs = [(pltpu.MemorySpace.VMEM, state, BF16)] * count
    groups = [(pltpu.SMEM, [member]), (pltpu.VMEM, [order, *came]), (pltpu.VMEM, [after])]
    return call(kernel, "starts_part", groups, outs, [pltpu.VMEM((count, *state), BF16)], SMALL_VMEM, 10**8)


def gates(z, norm):
    halved = 0.5 * z.astype(F32)
    return halved * (1.0 + jnp.tanh(halved)) * norm


def gated_pairs(out, gain, gate, at, first, start_refs):
    pairs = []
    ones = jnp.full((DV, DV), 1.0 / DV, BF16)
    for j, start_ref in enumerate(start_refs):
        parts = []
        for r in range(2):
            cols = slice((2 * j + r) * DV, (2 * j + r + 1) * DV)
            local = slice((2 * (first + j) + r) * DV, (2 * (first + j) + r + 1) * DV)
            rows = [jnp.concatenate([ref[i, local] for i, _ in at], axis=0) for ref in (out, gain)]
            core = rows[0].astype(F32) + mm(rows[1], start_ref[r])
            mean = mm((core * core).astype(BF16), ones)
            weight = jnp.concatenate([gate[i, cols] for _, i in at], axis=0)
            parts.append((core * lax.rsqrt(mean + 1e-6) * weight).astype(BF16))
        pairs.append(jnp.concatenate(parts, axis=1))
    return pairs


def pair_moves(place_ref, turns, z_hbm, w_hbm, z, w):
    rows, width = z.shape[0], 2 * DV
    here = pl.ds(pl.multiple_of(place_ref[0] * rows, rows), rows)
    gates, bands = [], []
    for j, turn in enumerate(turns):
        at = pl.ds(pl.multiple_of(jnp.bitwise_xor(place_ref[2], turn) * width, width), width)
        part = slice(j * width, (j + 1) * width)
        gates.append((z_hbm.at[here, at], z.at[:, part]))
        bands.append((w_hbm.at[at, :], w.at[part, :]))
    return gates + bands


def pair_buffers(count, rows, wide):
    width = 2 * count * DV
    return [((rows, width), BF16), ((width, wide), BF16)]


def core_rows(place_ref, rows, out):
    half = rows // 2
    slices = []
    for core in (1 - place_ref[1], place_ref[1]):
        chip = 0 if out.shape[0] == rows else place_ref[0] * rows
        slices.append([pl.ds(pl.multiple_of(start + core * half, half), half) for start in (chip, 0)])
    return slices


def projected(pairs, w):
    width = 2 * DV
    total = None
    for j, gated in enumerate(pairs):
        term = mm(gated, w[j * width : (j + 1) * width, :])
        total = term if total is None else total + term
    return total


def keep_part(place, turns, rows, gate_z, weight, norm_gain, out, gain, start):
    wide = weight.shape[1]
    count = len(turns)

    def kernel(place_ref, z_hbm, w_hbm, norm_hbm, out, gain, start_ref, sum_ref, gate_ref, w_away, *refs):
        norm, own_gate, z_away, z_own, w_own, sems = refs
        moves = [(norm_hbm, norm)] + pair_moves(place_ref, [0], z_hbm, w_hbm, z_own, w_own)
        copies = started(moves + pair_moves(place_ref, turns, z_hbm, w_hbm, z_away, w_away), sems)
        waited(copies[:2])
        for h in range(2):
            cols = slice(h * DV, (h + 1) * DV)
            own_gate[:, cols] = gates(z_own[:, cols], norm[...])
        pairs = gated_pairs(out, gain, own_gate, core_rows(place_ref, rows, out), count, [start_ref])
        waited(copies[2 : 3 + count])
        for h in range(2 * count):
            cols = slice(h * DV, (h + 1) * DV)
            gate_ref[:, cols] = gates(z_away[:, cols], norm[...])
        sum_ref[...] = projected(pairs, w_own)
        waited(copies[3 + count :])

    vmem = pltpu.MemorySpace.VMEM
    (z_shape, _), (w_shape, _) = pair_buffers(count, rows, wide)
    outs = [(vmem, (rows, wide), F32), (vmem, z_shape, F32), (vmem, w_shape, BF16)]
    scratch = [pltpu.VMEM((1, DV), F32), pltpu.VMEM((rows, 2 * DV), F32), pltpu.VMEM(z_shape, BF16)]
    scratch += [pltpu.VMEM(*shape) for shape in pair_buffers(1, rows, wide)]
    scratch += [pltpu.SemaphoreType.DMA((3 + 2 * count,))]
    groups = [(pltpu.SMEM, [place]), (pltpu.HBM, [gate_z, weight, norm_gain]), (pltpu.VMEM, [out, gain, start])]
    return call(kernel, "keep_part", groups, outs, scratch, PROJECT_VMEM, 4 * rows * DV * wide)


def away_part(place, kept, out, gain, starts):
    rows, wide = kept[0].shape

    def kernel(place_ref, sum_ref, gate, w, out, gain, *refs):
        start_refs, (send_ref, stay_ref) = refs[:-2], refs[-2:]
        pairs = gated_pairs(out, gain, gate, core_rows(place_ref, rows, out), 0, start_refs)
        partial = projected(pairs, w) + sum_ref[...]
        send_ref[...] = partial[: rows // 2].astype(BF16)
        stay_ref[...] = partial[rows // 2 :]

    vmem = pltpu.MemorySpace.VMEM
    outs = [(vmem, (rows // 2, wide), BF16), (vmem, (rows // 2, wide), F32)]
    groups = [(pltpu.SMEM, [place]), (pltpu.VMEM, [*kept, out, gain, *starts])]
    return call(kernel, "away_part", groups, outs, [], PROJECT_VMEM, 2 * rows * kept[-1].size)


def whole_part(place, turns, rows, gate_z, weight, norm_gain, out, gain, starts):
    wide = weight.shape[1]
    count = len(turns) + 1

    def kernel(place_ref, z_hbm, w_hbm, norm_hbm, out, gain, *refs):
        start_refs, sends, (stay_ref, norm, gate, z, w, sems) = refs[:count], refs[count : count + 2], refs[count + 2 :]
        moves = [(norm_hbm, norm)] + pair_moves(place_ref, (*turns, 0), z_hbm, w_hbm, z, w)
        copies = started(moves, sems)
        waited(copies[: 1 + count])
        for h in range(2 * count):
            cols = slice(h * DV, (h + 1) * DV)
            gate[:, cols] = gates(z[:, cols], norm[...])
        pairs = gated_pairs(out, gain, gate, core_rows(place_ref, rows, out), 0, start_refs)
        waited(copies[1 + count :])
        partial = projected(pairs, w)
        for i, ref in enumerate(sends):
            ref[...] = partial[: rows // 2, i * (wide // 2) : (i + 1) * (wide // 2)].astype(BF16)
        stay_ref[...] = partial[rows // 2 :]

    vmem = pltpu.MemorySpace.VMEM
    outs = [(vmem, (rows // 2, wide // 2), BF16)] * 2 + [(vmem, (rows // 2, wide), F32)]
    (z_shape, _), _ = pair_buffers(count, rows, wide)
    scratch = [pltpu.VMEM((1, DV), F32), pltpu.VMEM(z_shape, F32)]
    scratch += [pltpu.VMEM(*shape) for shape in pair_buffers(count, rows, wide)]
    scratch += [pltpu.SemaphoreType.DMA((1 + 2 * count,))]
    groups = [(pltpu.SMEM, [place]), (pltpu.HBM, [gate_z, weight, norm_gain]), (pltpu.VMEM, [out, gain, *starts])]
    return call(kernel, "whole_part", groups, outs, scratch, PROJECT_VMEM, 2 * rows * weight.size)


def on_device(
    query, keys, values, gate_logit, beta_logit, decay_rate, norm_gain, gate_z, out_weight
):
    shards, cores = lax.axis_size("seq"), lax.axis_size("head")
    seq, head = lax.axis_index("seq"), lax.axis_index("head")
    members = query.shape[1] // DK
    turns = sorted(range(1, members), key=lambda turn: (-bin(turn).count("1"), turn))
    pairs = {turn: [(s, s ^ turn) for s in range(shards)] for turn in turns}
    member_at = lax.rem(seq, members)
    member = member_at.reshape(1)
    rate, norm_gain = decay_rate.reshape(1, -1), norm_gain.reshape(1, -1)

    groups = shards // members
    chips = cores // 2
    chip, core = head // 2, lax.rem(head, 2)
    rows = query.shape[0] // chips
    spots = [jnp.stack([lax.rem(chip + by, chips), core, member_at]) for by in range(chips)]
    apart = rows == CHUNK and chips == 2
    chunks = 1 if apart else query.shape[0] // CHUNK
    code = (member_at + members * lax.rem(chip + 1, chips)).reshape(1) if apart else member
    spot = spots[1] if apart else jnp.stack([jnp.zeros_like(core), core, member_at])
    away, earlier, operands = first_part(code, turns, rate, keys, values, gate_logit.T, beta_logit.T)
    others = [lax.ppermute(a, "seq", pairs[turn]) for a, turn in zip(away, turns)]
    own, mine, locals_, near = second_part(code, chunks, operands, earlier, query, keys)
    order, ending, *total = group_part(member, turns, own, others, groups > 2)
    out, gain = third_part(spot, turns, chunks, near, True, mine, ending)

    came = []
    for step in range(groups - 1):
        if step:
            start, ending = hop_part(*total, came)
            came = [start]
        along = [(step * members + i, (step + 1) * members + i) for i in range(members)]
        came.append(lax.ppermute(ending, "seq", along))
    if not came:
        came = [jnp.zeros_like(ending)]
    keep, *gives = starts_part(member, turns, order, came, out)
    back = [lax.ppermute(g, "seq", pairs[turn]) for g, turn in zip(gives, turns)]

    swap = [(i, i ^ 1) for i in range(cores)]
    arrived = []
    for by in range(1, chips):
        kept = keep_part(spots[by], turns, rows, gate_z, out_weight, norm_gain, out, gain, keep)
        give, stay = away_part(spots[by], kept, out, gain, back)
        both = (stay + lax.ppermute(give, "head", swap).astype(F32)).astype(BF16)
        arrived.append(lax.ppermute(both, "head", [(i, (i + 2 * by) % cores) for i in range(cores)]))
    spot = spots[0]
    if arrived:
        spot, both = lax.optimization_barrier((spot, both))
    if apart:
        out, gain = third_part(spot, turns, chunks, [query, keys, *locals_], False, mine, ending)
    *gives, stay = whole_part(spot, turns, rows, gate_z, out_weight, norm_gain, out, gain, [*back, keep])
    total = stay + jnp.concatenate([lax.ppermute(g, "head", swap) for g in gives], axis=1).astype(F32)
    for part in arrived:
        total = total + part.astype(F32)
    return total.astype(BF16)


def solution(mesh):
    return jax.shard_map(
        on_device,
        mesh=mesh,
        in_specs=(
            P("seq", "head"),
            P("seq", "head"),
            P("seq", "head"),
            P("seq", "head"),
            P("seq", "head"),
            P("head"),
            P(),
            P("seq", "head"),
            P("head", None),
        ),
        out_specs=P(("seq", "head"), None),
        check_vma=False,
    )
```

```python
import jax
import jax.numpy as jnp
from jax import lax
from jax.experimental import pallas as pl
from jax.experimental.pallas import tpu as pltpu
from jax.sharding import PartitionSpec as P

DK = 128
DV = 128
CHUNK = 256
F32 = jnp.float32
BF16 = jnp.bfloat16
NEG = -1e30
SMALL_VMEM = 8 * 1024 * 1024
DELTA_VMEM = 28 * 1024 * 1024
OUTPUT_VMEM = 20 * 1024 * 1024
PROJECT_VMEM = 24 * 1024 * 1024


def mm(left, right):
    return lax.dot_general(left, right, (((1,), (0,)), ((), ())), preferred_element_type=F32)


def mm_nt(left, right):
    return lax.dot_general(left, right, (((1,), (1,)), ((), ())), preferred_element_type=F32)


def iota(shape, dim):
    return lax.broadcasted_iota(jnp.int32, shape, dim)


def split3(x):
    hi = x.astype(BF16).astype(F32)
    mid = (x - hi).astype(BF16).astype(F32)
    return hi, mid, x - hi - mid


def softplus(x):
    small = jnp.exp(-jnp.abs(x))
    one = 1.0 + small
    log1p = jnp.where(one == 1.0, small, jnp.log(one) * (small / jnp.where(one == 1.0, 1.0, one - 1.0)))
    return jnp.maximum(x, 0.0) + log1p


def log_inverse_norm(x, rows):
    square = x.astype(F32) * x.astype(F32)
    high = square.astype(BF16)
    low = (square - high.astype(F32)).astype(BF16)
    ones = jnp.ones((rows, x.shape[1]), BF16)
    return -0.5 * jnp.log(mm_nt(ones, high) + mm_nt(ones, low) + 1e-6)


def odd_rows(x, n):
    return jnp.concatenate([x[i + n : i + 2 * n] for i in range(0, x.shape[0], 2 * n)], axis=0)


def weave(even, odd, n):
    parts = []
    for at in range(0, odd.shape[0], n):
        parts.append(even[2 * at : 2 * at + n])
        parts.append(odd[at : at + n])
    return jnp.concatenate(parts, axis=0)


def as_mask(where):
    return jnp.where(where, 1.0, 0.0).astype(BF16)


def spread(beside):
    half = beside.shape[1] // 2
    zeros = jnp.zeros((half, half), BF16)
    top = jnp.concatenate([beside[:, :half], zeros], axis=1)
    return jnp.concatenate([top, jnp.concatenate([zeros, beside[:, half:]], axis=1)], axis=0)


def unit_lower_inverses(lowers):
    size = lowers[0].shape[0]
    half = size // 2
    row, col = iota((half, size), 0), iota((half, size), 1)
    col = jnp.bitwise_and(col, half - 1)
    crow, ccol = iota((half // 2, size), 0), iota((half // 2, size), 1)
    ccol = jnp.bitwise_and(ccol, half - 1)
    zeros = jnp.zeros((half, size), BF16)
    eye, pair = as_mask(row == col), as_mask(row // 2 == col // 2)
    sides = [jnp.concatenate([lower[:half, :half], lower[half:, half:]], axis=1) for lower in lowers]
    xs = [eye - side * pair for side in sides]
    n = 2
    while n < half:
        if n < 16:
            mask = as_mask((row // n == col // n + 1) & (row // (2 * n) == col // (2 * n)))
            ys = [mm(side * mask, spread(x)).astype(BF16) for side, x in zip(sides, xs)]
            zs = [mm(x, spread(y)).astype(BF16) for x, y in zip(xs, ys)]
            xs = [x - z for x, z in zip(xs, zs)]
        else:
            mask = as_mask(ccol // n == 2 * (crow // n))
            ys = [mm(odd_rows(side, n) * mask, spread(x)).astype(BF16) for side, x in zip(sides, xs)]
            odds = [odd_rows(x, n) for x in xs]
            zs = [mm(odd, spread(weave(zeros, y, n))).astype(BF16) for odd, y in zip(odds, ys)]
            xs = [weave(x, odd - z, n) for x, odd, z in zip(xs, odds, zs)]
        n *= 2
    ys = [mm(lower[half:, :half], x[:, :half]).astype(BF16) for lower, x in zip(lowers, xs)]
    zs = [mm(x[:, half:], y).astype(BF16) for x, y in zip(xs, ys)]
    full = []
    for x, z in zip(xs, zs):
        top = jnp.concatenate([x[:, :half], jnp.zeros((half, half), BF16)], axis=1)
        full.append(jnp.concatenate([top, jnp.concatenate([-z, x[:, half:]], axis=1)], axis=0))
    return full


def decayed(c, b, product, mask):
    h = CHUNK // 2

    def quarter(i, j):
        arg = c[i * h : (i + 1) * h] - b[:, j * h : (j + 1) * h]
        if i == j:
            arg = jnp.where(mask, arg, NEG)
        exact = jnp.exp(arg) * product[i * h : (i + 1) * h, j * h : (j + 1) * h]
        rounded = exact.astype(BF16)
        return rounded, (exact - rounded.astype(F32)).astype(BF16)

    quarters = [quarter(0, 0), quarter(1, 0), quarter(1, 1)]
    results = []
    for a, b, c in zip(*quarters):
        top = jnp.concatenate([a, jnp.zeros((h, h), BF16)], axis=1)
        results.append(jnp.concatenate([top, jnp.concatenate([b, c], axis=1)], axis=0))
    return results


def reordered(x, quarters, first):
    row = iota(x.shape, 0)
    total = jnp.zeros_like(x)
    for j, quarter in enumerate(quarters, first):
        for r in range(2):
            picked = jnp.sum(jnp.where(row == 2 * quarter + r, x, 0.0), axis=0, keepdims=True)
            total = jnp.where(row == 2 * j + r, picked, total)
    return total


def log_norms(refs, heads, first=0):
    tokens = refs[0].shape[0]
    head_row = iota((heads, tokens), 0)
    total = log_inverse_norm(refs[0][...], heads)
    for j, ref in enumerate(refs[1:], first + 1):
        total = jnp.where(head_row < 2 * j, total, log_inverse_norm(ref[...], heads))
    return total


def delta_kernel(waits, rate, gate, beta, quarters, first, k_refs, v_refs, ends_refs, work_ref, marks_ref):
    waited(waits[0])
    tokens = k_refs[0].shape[0]
    heads = gate.shape[0]
    chunks = [slice(at, at + CHUNK) for at in range(0, tokens, CHUNK)]

    diagonal = iota((heads, heads), 0) == iota((heads, heads), 1)
    rate = jnp.sum(jnp.where(diagonal, rate[...], 0.0), axis=1, keepdims=True)
    decay = reordered(-rate * softplus(gate[...]), quarters, first)
    log_beta = reordered(-softplus(-beta[...]), quarters, first)

    row, col = iota((CHUNK, CHUNK), 0), iota((CHUNK, CHUNK), 1)
    upto = jnp.where(row <= col, 1.0, 0.0).astype(BF16)
    sums = mm(
        jnp.concatenate([p for here in chunks for p in split3(decay[:, here])], axis=0).astype(BF16), upto
    )
    square = CHUNK // 2
    strict = iota((square, square), 1) < iota((square, square), 0)

    waited(waits[1])
    log_k = log_norms(k_refs, heads, first)
    waited(waits[2])
    lowers, rests, rights, ended, decays = {}, {}, {}, {}, {}
    for c, here in enumerate(chunks):
        parts = [sums[(3 * c + i) * heads : (3 * c + i + 1) * heads] for i in range(3)]
        cumul = parts[0] + parts[1] + parts[2]
        end = cumul[:, CHUNK - 1 :]
        lb, lk = log_beta[:, here], log_k[:, here]
        col_log = cumul - lk
        row_lower = cumul + lb + lk
        marks_ref[:heads, here] = cumul
        marks_ref[heads:, here] = col_log
        key_end = jnp.exp(end - cumul + lk)
        ends = jnp.exp(end)
        columns = jnp.concatenate([row_lower, jnp.exp(lb), jnp.exp(row_lower), key_end], axis=0).T
        for j, (k_ref, v_ref) in enumerate(zip(k_refs, v_refs)):
            k = k_ref[here, :]
            k32 = k.astype(F32)
            turned = k32.T.astype(BF16)
            key_key = mm(k, turned)
            for r in range(2):
                at = 2 * (first + j) + r
                c_lower, c_beta, c_weight, c_end = (
                    columns[:, heads * i + at : heads * i + at + 1] for i in range(4)
                )
                m = (c, 2 * j + r)
                lowers[m], rests[m] = decayed(c_lower, col_log[at : at + 1], key_key, strict)
                v32 = v_ref[here, r * DV : (r + 1) * DV].astype(F32)
                rights[m] = jnp.concatenate([c_beta * v32, c_weight * k32], axis=1).astype(BF16)
                ended[m] = turned, c_end
                decays[m] = ends[at : at + 1]
    names = list(lowers)
    inverses = dict(zip(names, unit_lower_inverses([lowers[m] for m in names])))
    solved = {m: mm(inverses[m], rights[m]) for m in names}
    missed = {m: mm(rests[m], solved[m].astype(BF16)).astype(BF16) for m in names}
    solved = {m: solved[m] - mm(inverses[m], missed[m]) for m in names}
    all_heads = range(2 * len(k_refs))
    state = {}
    for c, here in enumerate(chunks):
        if c == 0:
            resid = {a: jnp.concatenate([solved[c, a][:, :DV], -solved[c, a][:, DV:]], axis=1) for a in all_heads}
            before = iota((DK, DV + DK), 1) == iota((DK, DV + DK), 0) + DV
            before = {a: jnp.where(before, 1.0, 0.0) for a in all_heads}
            for a in all_heads:
                work_ref[a // 2, c, a % 2, CHUNK:, :] = before[a].astype(BF16)
        else:
            held = {a: state[a].astype(BF16) for a in all_heads}
            for a in all_heads:
                work_ref[a // 2, c, a % 2, CHUNK:, :] = held[a]
            moved = {a: mm(solved[c, a][:, DV:].astype(BF16), held[a]) for a in all_heads}
            resid = {
                a: jnp.concatenate([solved[c, a][:, :DV] - moved[a][:, :DV], -moved[a][:, DV:]], axis=1)
                for a in all_heads
            }
            before = state
        for a in all_heads:
            work_ref[a // 2, c, a % 2, :CHUNK, :] = resid[a].astype(BF16)
        state = {
            a: decays[c, a] * before[a] + mm(ended[c, a][0], (ended[c, a][1] * resid[a]).astype(BF16))
            for a in all_heads
        }
    for a in all_heads:
        ends_refs[a // 2][a % 2] = state[a].astype(BF16)


def local_outputs(q_refs, k_refs, cumul, logs, waits, resid, held, out_ref, gain_ref):
    tokens = q_refs[0].shape[0]
    heads = cumul.shape[0]
    square = CHUNK // 2
    inclusive = iota((square, square), 1) <= iota((square, square), 0)
    row_mix = cumul + log_norms(q_refs, heads)
    mixings, queries = {}, {}
    for c in range(tokens // CHUNK):
        here = slice(c * CHUNK, (c + 1) * CHUNK)
        mix = row_mix[:, here]
        columns = jnp.concatenate([mix, jnp.exp(mix)], axis=0).T
        for j, (q_ref, k_ref) in enumerate(zip(q_refs, k_refs)):
            q, k = q_ref[here, :], k_ref[here, :]
            query_key = mm_nt(q, k)
            q32 = q.astype(F32)
            for a in (2 * j, 2 * j + 1):
                b_row = logs[a : a + 1, here]
                mixings[c, a], _ = decayed(columns[:, a : a + 1], b_row, query_key, inclusive)
                queries[c, a] = (columns[:, heads + a : heads + a + 1] * q32).astype(BF16)
    waited(waits)
    for c, a in mixings:
        here = slice(c * CHUNK, (c + 1) * CHUNK)
        result = mm(queries[c, a], held(c, a)) + mm(mixings[c, a], resid(c, a))
        out_ref[here, a * DV : (a + 1) * DV] = result[:, :DV].astype(BF16)
        gain_ref[here, a * DK : (a + 1) * DK] = result[:, DV:].astype(BF16)


def started(moves, sems, first=0):
    copies = [pltpu.make_async_copy(a, b, sems.at[first + i]) for i, (a, b) in enumerate(moves)]
    for copy in copies:
        copy.start()
    return copies


def waited(copies):
    for copy in copies:
        copy.wait()


def in_vmem(array):
    return pltpu.with_memory_space_constraint(array, pltpu.VMEM)


def in_hbm(array):
    return pltpu.with_memory_space_constraint(array, pltpu.HBM)


def call(kernel, name, groups, outs, scratch, vmem_bytes, flops):
    specs, args = [], []
    for space, arrays in groups:
        specs += [pl.BlockSpec(memory_space=space)] * len(arrays)
        if space is pltpu.VMEM or space is pltpu.HBM:
            arrays = [pltpu.with_memory_space_constraint(a, space) for a in arrays]
        args += arrays
    return pl.pallas_call(
        kernel,
        in_specs=specs,
        out_specs=[pl.BlockSpec(memory_space=space) for space, _, _ in outs],
        out_shape=[space(shape, kind) for space, shape, kind in outs],
        scratch_shapes=scratch,
        compiler_params=pltpu.CompilerParams(vmem_limit_bytes=vmem_bytes),
        cost_estimate=pl.CostEstimate(flops=flops, bytes_accessed=2**20, transcendentals=0),
        name=name,
    )(*args)


def local_shapes(count, tokens, heads):
    chunks = tokens // CHUNK
    return [((count, chunks, 2, CHUNK + DK, DV + DK), BF16), ((2 * heads, tokens), F32)]


def pair_lanes(ref, quarter, width):
    return ref.at[:, pl.ds(pl.multiple_of(quarter * width, width), width)]


def first_part(code, turns, rate, keys, values, gate_logit, beta_logit):
    heads, tokens = gate_logit.shape
    count = len(turns)

    def kernel(code_ref, rate_hbm, gate_hbm, beta_hbm, k_hbm, v_hbm, *refs):
        ends, (work, marks, rate, gate, beta, k_own, v_own), refs = refs[:count], refs[count : count + 7], refs[count + 7 :]
        k_refs, v_refs, sems = refs[:count], refs[count : 2 * count], refs[-1]
        pair = jnp.bitwise_and(code_ref[0], count)
        quarters = [jnp.bitwise_xor(pair, turn) for turn in turns]
        moves = [(rate_hbm, rate), (gate_hbm, gate), (beta_hbm, beta)]
        moves += [(pair_lanes(k_hbm, q, DK), ref) for q, ref in zip(quarters, k_refs)]
        moves += [(pair_lanes(v_hbm, q, 2 * DV), ref) for q, ref in zip(quarters, v_refs)]
        moves += [(pair_lanes(k_hbm, pair, DK), k_own), (pair_lanes(v_hbm, pair, 2 * DV), v_own)]
        copies = started(moves, sems)
        waits = copies[:3], copies[3 : 3 + count], copies[3 + count : -2]
        delta_kernel(waits, rate, gate, beta, quarters, 0, k_refs, v_refs, ends, work, marks)
        waited(copies[-2:])

    vmem = pltpu.MemorySpace.VMEM
    outs = [(vmem, (2, DK, DV + DK), BF16)] * count
    outs += [(vmem, *shape) for shape in local_shapes(count, tokens, heads)]
    outs += [(vmem, a.shape, a.dtype) for a in (rate, gate_logit, beta_logit)]
    outs += [(vmem, (tokens, DK), BF16), (vmem, (tokens, 2 * DV), BF16)]
    groups = [(pltpu.SMEM, [code]), (pltpu.HBM, [rate, gate_logit, beta_logit, keys, values])]
    scratch = [pltpu.VMEM((tokens, DK), BF16)] * count + [pltpu.VMEM((tokens, 2 * DV), BF16)] * count
    scratch += [pltpu.SemaphoreType.DMA((5 + 2 * count,))]
    result = call(kernel, "first_part", groups, outs, scratch, DELTA_VMEM, 6 * 10**9)
    return result[:count], result[count : count + 2], result[count + 2 :]


def place_code(chip, core, member, members):
    return ((chip * 2 + core) * members + member).reshape(1)


def place_of(code_ref, members):
    code = code_ref[0]
    return code // (2 * members), jnp.bitwise_and(code // members, 1), jnp.bitwise_and(code, members - 1)


def chunk_moves(first, chunks, sources, targets):
    (q_hbm, k_hbm, work, marks), (q, k, work_to, marks_to) = sources, targets
    rows = pl.ds(pl.multiple_of(first * CHUNK, CHUNK), chunks * CHUNK)
    return [
        (q_hbm.at[rows, :], q),
        (k_hbm.at[rows, :], k),
        (marks.at[:, rows], marks_to),
        (work.at[:, pl.ds(first, chunks)], work_to),
    ]


def chunk_shapes(chunks, pairs, width):
    tokens = chunks * CHUNK
    return [((tokens, width), BF16)] * 2 + local_shapes(pairs - 1, tokens, 2 * pairs)


def second_part(code, chunks, operands, earlier, query, keys):
    heads, tokens = operands[1].shape
    near = chunk_shapes(chunks, heads // 2, query.shape[1])

    def kernel(code_ref, q_hbm, k_hbm, rate, gate, beta, k_own, v_own, *refs):
        earlier_refs, (ends, *local), out_hbm, targets, sems = refs[:2], refs[2:5], refs[5:7], refs[7:11], refs[11]
        moves = chunk_moves(code_ref[0] // (heads // 2), chunks, (q_hbm, k_hbm, *earlier_refs), targets)
        copies = started([*moves, *zip(earlier_refs, out_hbm)], sems)
        pair = jnp.bitwise_and(code_ref[0], heads // 2 - 1)
        delta_kernel([[]] * 3, rate, gate, beta, [pair], heads // 2 - 1, [k_own], [v_own], [ends], *local)
        waited(copies)

    vmem = pltpu.MemorySpace.VMEM
    outs = [(vmem, (2, DK, DV + DK), BF16)] + [(vmem, *shape) for shape in local_shapes(1, tokens, heads)]
    outs += [(pltpu.MemorySpace.HBM, a.shape, a.dtype) for a in earlier]
    outs += [(vmem, *shape) for shape in near]
    scratch = [pltpu.SemaphoreType.DMA((6,))]
    groups = [(pltpu.SMEM, [code]), (pltpu.HBM, [query, keys]), (pltpu.VMEM, [*operands, *earlier])]
    ends, work, marks, *rest = call(kernel, "second_part", groups, outs, scratch, DELTA_VMEM, 2 * 10**9)
    return ends, [work, marks], rest[:2], rest[2:]


def third_part(place, turns, chunks, sources, near, own, after):
    count = len(turns) + 1
    tokens = chunks * CHUNK
    heads = 2 * count

    def kernel(code_ref, *refs):
        place_ref = place_of(code_ref, count)
        sources, (own_work, own_marks), (out, gain), scratch = refs[:4], refs[4:6], refs[7:9], refs[9:]
        first = place_ref[0] * chunks
        local, copies = sources, []
        if not near:
            local = scratch[:4]
            copies = started(chunk_moves(first, chunks, sources, local), scratch[4])
            waited(copies[:3])
        q, k, work, marks = local
        quarters = [jnp.bitwise_xor(place_ref[2], turn) for turn in (*turns, 0)]
        q_refs = [pair_lanes(q, quarter, DK) for quarter in quarters]
        k_refs = [pair_lanes(k, quarter, DK) for quarter in quarters]
        own_here = own_marks[:, pl.ds(pl.multiple_of(first * CHUNK, CHUNK), tokens)]
        theirs = iota((heads, tokens), 0) < heads - 2
        cumul = jnp.where(theirs, marks[:heads, :], own_here[:heads])
        logs = jnp.where(theirs, marks[heads:, :], own_here[heads:])

        def read(rows):
            def block(c, a):
                if a < heads - 2:
                    return work[a // 2, c, a % 2, rows, :]
                return own_work[0, first + c, a % 2, rows, :]

            return block

        resid, held = read(slice(0, CHUNK)), read(slice(CHUNK, CHUNK + DK))
        local_outputs(q_refs, k_refs, cumul, logs, copies[3:], resid, held, out, gain)

    outs = [(pltpu.MemorySpace.VMEM, (tokens, heads * DV), BF16)] * 2
    scratch = []
    if not near:
        scratch = [pltpu.VMEM(*shape) for shape in chunk_shapes(chunks, count, sources[0].shape[1])]
        scratch += [pltpu.SemaphoreType.DMA((4,))]
    groups = [(pltpu.SMEM, [place]), (pltpu.VMEM if near else pltpu.HBM, sources), (pltpu.VMEM, own)]
    groups += [(pltpu.HBM, [after])]
    return call(kernel, "third_part", groups, outs, scratch, OUTPUT_VMEM, 3 * 10**9)


def in_order(member_ref, turns, own_ref, other_refs, order_ref):
    order_ref[member_ref[0]] = own_ref[...]
    for turn, ref in zip(turns, other_refs):
        order_ref[jnp.bitwise_xor(member_ref[0], turn)] = ref[...]


def after_shard(ends, state):
    return mm(ends[:, DV:], state.astype(BF16)) + ends[:, :DV].astype(F32)


def group_part(member, turns, own, others, chained):
    count = len(turns) + 1

    def kernel(member_ref, own_ref, *refs):
        other_refs, (order, ending_ref, *total_refs) = refs[: count - 1], refs[count - 1 :]
        in_order(member_ref, turns, own_ref, other_refs, order)
        states = [order[0, h][:, :DV].astype(F32) for h in range(2)]
        for i in range(1, count):
            states = [after_shard(order[i, h], states[h]) for h in range(2)]
        for h in range(2):
            ending_ref[h] = states[h].astype(BF16)
        for total_ref in total_refs:
            for h in range(2):
                transit = order[0, h][:, DV:]
                for i in range(1, count):
                    transit = mm(order[i, h][:, DV:], transit).astype(BF16)
                total_ref[h] = jnp.concatenate([states[h].astype(BF16), transit], axis=1)

    vmem = pltpu.MemorySpace.VMEM
    outs = [(vmem, (count, *own.shape), BF16), (vmem, (2, DK, DV), BF16)]
    if chained:
        outs.append((vmem, own.shape, BF16))
    groups = [(pltpu.SMEM, [member]), (pltpu.VMEM, [own, *others])]
    return call(kernel, "group_part", groups, outs, [], SMALL_VMEM, 10**8)


def hop_part(total, came):
    def kernel(total_ref, *refs):
        sum_ref, out_ref = refs[-2:]
        for h in range(2):
            start = refs[0][h]
            for ref in refs[1:-2]:
                start = start + ref[h]
            sum_ref[h] = start
            out_ref[h] = after_shard(total_ref[h], start).astype(BF16)

    outs = [(pltpu.MemorySpace.VMEM, (2, DK, DV), BF16)] * 2
    return call(kernel, "hop_part", [(pltpu.VMEM, [total, *came])], outs, [], SMALL_VMEM, 10**7)


def starts_part(member, turns, order, came, after):
    count = len(turns) + 1

    def kernel(member_ref, order_ref, *refs):
        came_refs, outs, states_ref = refs[: len(came)], refs[len(came) + 1 : -1], refs[-1]
        states = [came_refs[0][h] for h in range(2)]
        for ref in came_refs[1:]:
            states = [states[h] + ref[h] for h in range(2)]
        for i in range(count):
            for h in range(2):
                states_ref[i, h] = states[h].astype(BF16)
            if i < count - 1:
                states = [after_shard(order_ref[i, h], states[h]) for h in range(2)]
        for turn, ref in zip((0, *turns), outs):
            ref[...] = states_ref[jnp.bitwise_xor(member_ref[0], turn)]

    state = (2, DK, DV)
    outs = [(pltpu.MemorySpace.VMEM, state, BF16)] * count
    groups = [(pltpu.SMEM, [member]), (pltpu.VMEM, [order, *came]), (pltpu.VMEM, [after])]
    return call(kernel, "starts_part", groups, outs, [pltpu.VMEM((count, *state), BF16)], SMALL_VMEM, 10**8)


def gates(z, norm):
    halved = 0.5 * z.astype(F32)
    return halved * (1.0 + jnp.tanh(halved)) * norm


def gated_pairs(out, gain, gate, at, first, start_refs):
    pairs = []
    ones = jnp.full((DV, DV), 1.0 / DV, BF16)
    for j, start_ref in enumerate(start_refs):
        parts = []
        for r in range(2):
            cols = slice((2 * j + r) * DV, (2 * j + r + 1) * DV)
            local = slice((2 * (first + j) + r) * DV, (2 * (first + j) + r + 1) * DV)
            rows = [jnp.concatenate([ref[i, local] for i, _ in at], axis=0) for ref in (out, gain)]
            core = rows[0].astype(F32) + mm(rows[1], start_ref[r])
            mean = mm((core * core).astype(BF16), ones)
            weight = jnp.concatenate([gate[i, cols] for _, i in at], axis=0)
            parts.append((core * lax.rsqrt(mean + 1e-6) * weight).astype(BF16))
        pairs.append(jnp.concatenate(parts, axis=1))
    return pairs


def pair_moves(place_ref, turns, z_hbm, w_hbm, z, w):
    rows, width = z.shape[0], 2 * DV
    here = pl.ds(pl.multiple_of(place_ref[0] * rows, rows), rows)
    gates, bands = [], []
    for j, turn in enumerate(turns):
        at = pl.ds(pl.multiple_of(jnp.bitwise_xor(place_ref[2], turn) * width, width), width)
        part = slice(j * width, (j + 1) * width)
        gates.append((z_hbm.at[here, at], z.at[:, part]))
        bands.append((w_hbm.at[at, :], w.at[part, :]))
    return gates + bands


def pair_buffers(count, rows, wide):
    width = 2 * count * DV
    return [((rows, width), BF16), ((width, wide), BF16)]


def core_rows(place_ref, rows, out):
    half = rows // 2
    slices = []
    for core in (1 - place_ref[1], place_ref[1]):
        chip = 0 if out.shape[0] == rows else place_ref[0] * rows
        slices.append([pl.ds(pl.multiple_of(start + core * half, half), half) for start in (chip, 0)])
    return slices


def projected(pairs, w):
    width = 2 * DV
    total = None
    for j, gated in enumerate(pairs):
        term = mm(gated, w[j * width : (j + 1) * width, :])
        total = term if total is None else total + term
    return total


def keep_part(place, turns, rows, gate_z, weight, norm_gain, out, gain, start):
    wide = weight.shape[1]
    count = len(turns)

    def kernel(code_ref, z_hbm, w_hbm, norm_hbm, out, gain, start_ref, sum_ref, gate_ref, w_away, *refs):
        place_ref = place_of(code_ref, count + 1)
        norm, own_gate, z_away, z_own, w_own, sems = refs
        moves = [(norm_hbm, norm)] + pair_moves(place_ref, [0], z_hbm, w_hbm, z_own, w_own)
        copies = started(moves + pair_moves(place_ref, turns, z_hbm, w_hbm, z_away, w_away), sems)
        waited(copies[:2])
        for h in range(2):
            cols = slice(h * DV, (h + 1) * DV)
            own_gate[:, cols] = gates(z_own[:, cols], norm[...])
        pairs = gated_pairs(out, gain, own_gate, core_rows(place_ref, rows, out), count, [start_ref])
        waited(copies[2 : 3 + count])
        for h in range(2 * count):
            cols = slice(h * DV, (h + 1) * DV)
            gate_ref[:, cols] = gates(z_away[:, cols], norm[...])
        sum_ref[...] = projected(pairs, w_own)
        waited(copies[3 + count :])

    vmem = pltpu.MemorySpace.VMEM
    (z_shape, _), (w_shape, _) = pair_buffers(count, rows, wide)
    outs = [(vmem, (rows, wide), F32), (vmem, z_shape, F32), (vmem, w_shape, BF16)]
    scratch = [pltpu.VMEM((1, DV), F32), pltpu.VMEM((rows, 2 * DV), F32), pltpu.VMEM(z_shape, BF16)]
    scratch += [pltpu.VMEM(*shape) for shape in pair_buffers(1, rows, wide)]
    scratch += [pltpu.SemaphoreType.DMA((3 + 2 * count,))]
    groups = [(pltpu.SMEM, [place]), (pltpu.HBM, [gate_z, weight, norm_gain]), (pltpu.VMEM, [out, gain, start])]
    return call(kernel, "keep_part", groups, outs, scratch, PROJECT_VMEM, 4 * rows * DV * wide)


def away_part(place, kept, out, gain, starts):
    rows, wide = kept[0].shape

    def kernel(code_ref, sum_ref, gate, w, out, gain, *refs):
        place_ref = place_of(code_ref, len(starts) + 1)
        start_refs, (send_ref, stay_ref) = refs[:-2], refs[-2:]
        pairs = gated_pairs(out, gain, gate, core_rows(place_ref, rows, out), 0, start_refs)
        partial = projected(pairs, w) + sum_ref[...]
        send_ref[...] = partial[: rows // 2].astype(BF16)
        stay_ref[...] = partial[rows // 2 :]

    vmem = pltpu.MemorySpace.VMEM
    outs = [(vmem, (rows // 2, wide), BF16), (vmem, (rows // 2, wide), F32)]
    groups = [(pltpu.SMEM, [place]), (pltpu.VMEM, [*kept, out, gain, *starts])]
    return call(kernel, "away_part", groups, outs, [], PROJECT_VMEM, 2 * rows * kept[-1].size)


def whole_part(place, turns, rows, gate_z, weight, norm_gain, out, gain, starts):
    wide = weight.shape[1]
    count = len(turns) + 1

    def kernel(code_ref, z_hbm, w_hbm, norm_hbm, out, gain, *refs):
        place_ref = place_of(code_ref, count)
        start_refs, sends, (stay_ref, norm, gate, z, w, sems) = refs[:count], refs[count : count + 2], refs[count + 2 :]
        moves = [(norm_hbm, norm)] + pair_moves(place_ref, (*turns, 0), z_hbm, w_hbm, z, w)
        copies = started(moves, sems)
        waited(copies[: 1 + count])
        for h in range(2 * count):
            cols = slice(h * DV, (h + 1) * DV)
            gate[:, cols] = gates(z[:, cols], norm[...])
        pairs = gated_pairs(out, gain, gate, core_rows(place_ref, rows, out), 0, start_refs)
        waited(copies[1 + count :])
        partial = projected(pairs, w)
        for i, ref in enumerate(sends):
            ref[...] = partial[: rows // 2, i * (wide // 2) : (i + 1) * (wide // 2)].astype(BF16)
        stay_ref[...] = partial[rows // 2 :]

    vmem = pltpu.MemorySpace.VMEM
    outs = [(vmem, (rows // 2, wide // 2), BF16)] * 2 + [(vmem, (rows // 2, wide), F32)]
    (z_shape, _), _ = pair_buffers(count, rows, wide)
    scratch = [pltpu.VMEM((1, DV), F32), pltpu.VMEM(z_shape, F32)]
    scratch += [pltpu.VMEM(*shape) for shape in pair_buffers(count, rows, wide)]
    scratch += [pltpu.SemaphoreType.DMA((1 + 2 * count,))]
    groups = [(pltpu.SMEM, [place]), (pltpu.HBM, [gate_z, weight, norm_gain]), (pltpu.VMEM, [out, gain, *starts])]
    return call(kernel, "whole_part", groups, outs, scratch, PROJECT_VMEM, 2 * rows * weight.size)


def on_device(
    query, keys, values, gate_logit, beta_logit, decay_rate, norm_gain, gate_z, out_weight
):
    shards, cores = lax.axis_size("seq"), lax.axis_size("head")
    seq, head = lax.axis_index("seq"), lax.axis_index("head")
    members = query.shape[1] // DK
    turns = sorted(range(1, members), key=lambda turn: (-bin(turn).count("1"), turn))
    pairs = {turn: [(s, s ^ turn) for s in range(shards)] for turn in turns}
    member_at = lax.rem(seq, members)
    member = member_at.reshape(1)
    rate, norm_gain = decay_rate.reshape(1, -1), norm_gain.reshape(1, -1)

    groups = shards // members
    chips = cores // 2
    chip, core = head // 2, lax.rem(head, 2)
    rows = query.shape[0] // chips
    spots = [place_code(lax.rem(chip + by, chips), core, member_at, members) for by in range(chips)]
    apart = rows == CHUNK and chips == 2
    chunks = 1 if apart else query.shape[0] // CHUNK
    code = (member_at + members * lax.rem(chip + 1, chips)).reshape(1) if apart else member
    spot = spots[1] if apart else place_code(0, core, member_at, members)
    code, member, spot, *spots = lax.optimization_barrier((code, member, spot, *spots))
    away, earlier, operands = first_part(code, turns, rate, keys, values, gate_logit.T, beta_logit.T)
    others = [lax.ppermute(a, "seq", pairs[turn]) for a, turn in zip(away, turns)]
    own, mine, locals_, near = second_part(code, chunks, operands, earlier, query, keys)
    order, ending, *total = group_part(member, turns, own, others, groups > 2)
    out, gain = third_part(spot, turns, chunks, near, True, mine, ending)

    came = []
    for step in range(groups - 1):
        if step:
            start, ending = hop_part(*total, came)
            came = [start]
        along = [(step * members + i, (step + 1) * members + i) for i in range(members)]
        came.append(lax.ppermute(ending, "seq", along))
    if not came:
        came = [jnp.zeros_like(ending)]
    keep, *gives = starts_part(member, turns, order, came, out)
    back = [lax.ppermute(g, "seq", pairs[turn]) for g, turn in zip(gives, turns)]

    swap = [(i, i ^ 1) for i in range(cores)]
    arrived = []
    for by in range(1, chips):
        kept = keep_part(spots[by], turns, rows, gate_z, out_weight, norm_gain, out, gain, keep)
        give, stay = away_part(spots[by], kept, out, gain, back)
        both = (stay + lax.ppermute(give, "head", swap).astype(F32)).astype(BF16)
        arrived.append(lax.ppermute(both, "head", [(i, (i + 2 * by) % cores) for i in range(cores)]))
    spot = spots[0]
    if arrived:
        spot, both = lax.optimization_barrier((spot, both))
    if apart:
        out, gain = third_part(spot, turns, chunks, [query, keys, *locals_], False, mine, ending)
    *gives, stay = whole_part(spot, turns, rows, gate_z, out_weight, norm_gain, out, gain, [*back, keep])
    total = stay + jnp.concatenate([lax.ppermute(g, "head", swap) for g in gives], axis=1).astype(F32)
    for part in arrived:
        total = total + part.astype(F32)
    return total.astype(BF16)


def solution(mesh):
    return jax.shard_map(
        on_device,
        mesh=mesh,
        in_specs=(
            P("seq", "head"),
            P("seq", "head"),
            P("seq", "head"),
            P("seq", "head"),
            P("seq", "head"),
            P("head"),
            P(),
            P("seq", "head"),
            P("head", None),
        ),
        out_specs=P(("seq", "head"), None),
        check_vma=False,
    )
```

```python
import jax
import jax.numpy as jnp
from jax import lax
from jax.experimental import pallas as pl
from jax.experimental.pallas import tpu as pltpu
from jax.sharding import PartitionSpec as P

DK = 128
DV = 128
CHUNK = 256
F32 = jnp.float32
BF16 = jnp.bfloat16
NEG = -1e30
SMALL_VMEM = 8 * 1024 * 1024
DELTA_VMEM = 28 * 1024 * 1024
OUTPUT_VMEM = 20 * 1024 * 1024
PROJECT_VMEM = 24 * 1024 * 1024


def mm(left, right):
    return lax.dot_general(left, right, (((1,), (0,)), ((), ())), preferred_element_type=F32)


def mm_nt(left, right):
    return lax.dot_general(left, right, (((1,), (1,)), ((), ())), preferred_element_type=F32)


def iota(shape, dim):
    return lax.broadcasted_iota(jnp.int32, shape, dim)


def split3(x):
    hi = x.astype(BF16).astype(F32)
    mid = (x - hi).astype(BF16).astype(F32)
    return hi, mid, x - hi - mid


def softplus(x):
    small = jnp.exp(-jnp.abs(x))
    one = 1.0 + small
    log1p = jnp.where(one == 1.0, small, jnp.log(one) * (small / jnp.where(one == 1.0, 1.0, one - 1.0)))
    return jnp.maximum(x, 0.0) + log1p


def log_inverse_norm(x, rows):
    square = x.astype(F32) * x.astype(F32)
    high = square.astype(BF16)
    low = (square - high.astype(F32)).astype(BF16)
    ones = jnp.ones((rows, x.shape[1]), BF16)
    return -0.5 * jnp.log(mm_nt(ones, high) + mm_nt(ones, low) + 1e-6)


def odd_rows(x, n):
    return jnp.concatenate([x[i + n : i + 2 * n] for i in range(0, x.shape[0], 2 * n)], axis=0)


def weave(even, odd, n):
    parts = []
    for at in range(0, odd.shape[0], n):
        parts.append(even[2 * at : 2 * at + n])
        parts.append(odd[at : at + n])
    return jnp.concatenate(parts, axis=0)


def as_mask(where):
    return jnp.where(where, 1.0, 0.0).astype(BF16)


def spread(beside):
    half = beside.shape[1] // 2
    zeros = jnp.zeros((half, half), BF16)
    top = jnp.concatenate([beside[:, :half], zeros], axis=1)
    return jnp.concatenate([top, jnp.concatenate([zeros, beside[:, half:]], axis=1)], axis=0)


def unit_lower_inverses(lowers):
    size = lowers[0].shape[0]
    half = size // 2
    row, col = iota((half, size), 0), iota((half, size), 1)
    col = jnp.bitwise_and(col, half - 1)
    crow, ccol = iota((half // 2, size), 0), iota((half // 2, size), 1)
    ccol = jnp.bitwise_and(ccol, half - 1)
    zeros = jnp.zeros((half, size), BF16)
    eye, pair = as_mask(row == col), as_mask(row // 2 == col // 2)
    sides = [jnp.concatenate([lower[:half, :half], lower[half:, half:]], axis=1) for lower in lowers]
    xs = [eye - side * pair for side in sides]
    n = 2
    while n < half:
        if n < 16:
            mask = as_mask((row // n == col // n + 1) & (row // (2 * n) == col // (2 * n)))
            ys = [mm(side * mask, spread(x)).astype(BF16) for side, x in zip(sides, xs)]
            zs = [mm(x, spread(y)).astype(BF16) for x, y in zip(xs, ys)]
            xs = [x - z for x, z in zip(xs, zs)]
        else:
            mask = as_mask(ccol // n == 2 * (crow // n))
            ys = [mm(odd_rows(side, n) * mask, spread(x)).astype(BF16) for side, x in zip(sides, xs)]
            odds = [odd_rows(x, n) for x in xs]
            zs = [mm(odd, spread(weave(zeros, y, n))).astype(BF16) for odd, y in zip(odds, ys)]
            xs = [weave(x, odd - z, n) for x, odd, z in zip(xs, odds, zs)]
        n *= 2
    ys = [mm(lower[half:, :half], x[:, :half]).astype(BF16) for lower, x in zip(lowers, xs)]
    zs = [mm(x[:, half:], y).astype(BF16) for x, y in zip(xs, ys)]
    full = []
    for x, z in zip(xs, zs):
        top = jnp.concatenate([x[:, :half], jnp.zeros((half, half), BF16)], axis=1)
        full.append(jnp.concatenate([top, jnp.concatenate([-z, x[:, half:]], axis=1)], axis=0))
    return full


def decayed(c, b, product, mask):
    h = CHUNK // 2

    def quarter(i, j):
        arg = c[i * h : (i + 1) * h] - b[:, j * h : (j + 1) * h]
        if i == j:
            arg = jnp.where(mask, arg, NEG)
        exact = jnp.exp(arg) * product[i * h : (i + 1) * h, j * h : (j + 1) * h]
        rounded = exact.astype(BF16)
        return rounded, (exact - rounded.astype(F32)).astype(BF16)

    quarters = [quarter(0, 0), quarter(1, 0), quarter(1, 1)]
    results = []
    for a, b, c in zip(*quarters):
        top = jnp.concatenate([a, jnp.zeros((h, h), BF16)], axis=1)
        results.append(jnp.concatenate([top, jnp.concatenate([b, c], axis=1)], axis=0))
    return results


def reordered(x, quarters, first):
    row = iota(x.shape, 0)
    total = jnp.zeros_like(x)
    for j, quarter in enumerate(quarters, first):
        for r in range(2):
            picked = jnp.sum(jnp.where(row == 2 * quarter + r, x, 0.0), axis=0, keepdims=True)
            total = jnp.where(row == 2 * j + r, picked, total)
    return total


def log_norms(refs, heads, first=0):
    tokens = refs[0].shape[0]
    head_row = iota((heads, tokens), 0)
    total = log_inverse_norm(refs[0][...], heads)
    for j, ref in enumerate(refs[1:], first + 1):
        total = jnp.where(head_row < 2 * j, total, log_inverse_norm(ref[...], heads))
    return total


def delta_kernel(waits, rate, gate, beta, quarters, first, k_refs, v_refs, ends_refs, work_ref, marks_ref):
    waited(waits[0])
    tokens = k_refs[0].shape[0]
    heads = gate.shape[0]
    chunks = [slice(at, at + CHUNK) for at in range(0, tokens, CHUNK)]

    diagonal = iota((heads, heads), 0) == iota((heads, heads), 1)
    rate = jnp.sum(jnp.where(diagonal, rate[...], 0.0), axis=1, keepdims=True)
    decay = reordered(-rate * softplus(gate[...]), quarters, first)
    log_beta = reordered(-softplus(-beta[...]), quarters, first)

    row, col = iota((CHUNK, CHUNK), 0), iota((CHUNK, CHUNK), 1)
    upto = jnp.where(row <= col, 1.0, 0.0).astype(BF16)
    sums = mm(
        jnp.concatenate([p for here in chunks for p in split3(decay[:, here])], axis=0).astype(BF16), upto
    )
    square = CHUNK // 2
    strict = iota((square, square), 1) < iota((square, square), 0)

    waited(waits[1])
    log_k = log_norms(k_refs, heads, first)
    waited(waits[2])
    lowers, rests, rights, ended, decays = {}, {}, {}, {}, {}
    for c, here in enumerate(chunks):
        parts = [sums[(3 * c + i) * heads : (3 * c + i + 1) * heads] for i in range(3)]
        cumul = parts[0] + parts[1] + parts[2]
        end = cumul[:, CHUNK - 1 :]
        lb, lk = log_beta[:, here], log_k[:, here]
        col_log = cumul - lk
        row_lower = cumul + lb + lk
        marks_ref[:heads, here] = cumul
        marks_ref[heads:, here] = col_log
        key_end = jnp.exp(end - cumul + lk)
        ends = jnp.exp(end)
        columns = jnp.concatenate([row_lower, jnp.exp(lb), jnp.exp(row_lower), key_end], axis=0).T
        for j, (k_ref, v_ref) in enumerate(zip(k_refs, v_refs)):
            k = k_ref[here, :]
            k32 = k.astype(F32)
            turned = k32.T.astype(BF16)
            key_key = mm(k, turned)
            for r in range(2):
                at = 2 * (first + j) + r
                c_lower, c_beta, c_weight, c_end = (
                    columns[:, heads * i + at : heads * i + at + 1] for i in range(4)
                )
                m = (c, 2 * j + r)
                lowers[m], rests[m] = decayed(c_lower, col_log[at : at + 1], key_key, strict)
                v32 = v_ref[here, r * DV : (r + 1) * DV].astype(F32)
                rights[m] = jnp.concatenate([c_beta * v32, c_weight * k32], axis=1).astype(BF16)
                ended[m] = turned, c_end
                decays[m] = ends[at : at + 1]
    names = list(lowers)
    inverses = dict(zip(names, unit_lower_inverses([lowers[m] for m in names])))
    solved = {m: mm(inverses[m], rights[m]) for m in names}
    missed = {m: mm(rests[m], solved[m].astype(BF16)).astype(BF16) for m in names}
    solved = {m: solved[m] - mm(inverses[m], missed[m]) for m in names}
    all_heads = range(2 * len(k_refs))
    state = {}
    for c, here in enumerate(chunks):
        if c == 0:
            resid = {a: jnp.concatenate([solved[c, a][:, :DV], -solved[c, a][:, DV:]], axis=1) for a in all_heads}
            before = iota((DK, DV + DK), 1) == iota((DK, DV + DK), 0) + DV
            before = {a: jnp.where(before, 1.0, 0.0) for a in all_heads}
            for a in all_heads:
                work_ref[a // 2, c, a % 2, CHUNK:, :] = before[a].astype(BF16)
        else:
            held = {a: state[a].astype(BF16) for a in all_heads}
            for a in all_heads:
                work_ref[a // 2, c, a % 2, CHUNK:, :] = held[a]
            moved = {a: mm(solved[c, a][:, DV:].astype(BF16), held[a]) for a in all_heads}
            resid = {
                a: jnp.concatenate([solved[c, a][:, :DV] - moved[a][:, :DV], -moved[a][:, DV:]], axis=1)
                for a in all_heads
            }
            before = state
        for a in all_heads:
            work_ref[a // 2, c, a % 2, :CHUNK, :] = resid[a].astype(BF16)
        state = {
            a: decays[c, a] * before[a] + mm(ended[c, a][0], (ended[c, a][1] * resid[a]).astype(BF16))
            for a in all_heads
        }
    for a in all_heads:
        ends_refs[a // 2][a % 2] = state[a].astype(BF16)


def local_outputs(q_refs, k_refs, cumul, logs, waits, resid, held, out_ref, gain_ref):
    tokens = q_refs[0].shape[0]
    heads = cumul.shape[0]
    square = CHUNK // 2
    inclusive = iota((square, square), 1) <= iota((square, square), 0)
    row_mix = cumul + log_norms(q_refs, heads)
    mixings, queries = {}, {}
    for c in range(tokens // CHUNK):
        here = slice(c * CHUNK, (c + 1) * CHUNK)
        mix = row_mix[:, here]
        columns = jnp.concatenate([mix, jnp.exp(mix)], axis=0).T
        for j, (q_ref, k_ref) in enumerate(zip(q_refs, k_refs)):
            q, k = q_ref[here, :], k_ref[here, :]
            query_key = mm_nt(q, k)
            q32 = q.astype(F32)
            for a in (2 * j, 2 * j + 1):
                b_row = logs[a : a + 1, here]
                mixings[c, a], _ = decayed(columns[:, a : a + 1], b_row, query_key, inclusive)
                queries[c, a] = (columns[:, heads + a : heads + a + 1] * q32).astype(BF16)
    waited(waits)
    for c, a in mixings:
        here = slice(c * CHUNK, (c + 1) * CHUNK)
        result = mm(queries[c, a], held(c, a)) + mm(mixings[c, a], resid(c, a))
        out_ref[here, a * DV : (a + 1) * DV] = result[:, :DV].astype(BF16)
        gain_ref[here, a * DK : (a + 1) * DK] = result[:, DV:].astype(BF16)


def started(moves, sems, first=0):
    copies = [pltpu.make_async_copy(a, b, sems.at[first + i]) for i, (a, b) in enumerate(moves)]
    for copy in copies:
        copy.start()
    return copies


def waited(copies):
    for copy in copies:
        copy.wait()


def in_vmem(array):
    return pltpu.with_memory_space_constraint(array, pltpu.VMEM)


def in_hbm(array):
    return pltpu.with_memory_space_constraint(array, pltpu.HBM)


def call(kernel, name, groups, outs, scratch, vmem_bytes, flops):
    specs, args = [], []
    for space, arrays in groups:
        specs += [pl.BlockSpec(memory_space=space)] * len(arrays)
        if space is pltpu.VMEM or space is pltpu.HBM:
            arrays = [pltpu.with_memory_space_constraint(a, space) for a in arrays]
        args += arrays
    return pl.pallas_call(
        kernel,
        in_specs=specs,
        out_specs=[pl.BlockSpec(memory_space=space) for space, _, _ in outs],
        out_shape=[space(shape, kind) for space, shape, kind in outs],
        scratch_shapes=scratch,
        compiler_params=pltpu.CompilerParams(vmem_limit_bytes=vmem_bytes),
        cost_estimate=pl.CostEstimate(flops=flops, bytes_accessed=2**20, transcendentals=0),
        name=name,
    )(*args)


def local_shapes(count, tokens, heads):
    chunks = tokens // CHUNK
    return [((count, chunks, 2, CHUNK + DK, DV + DK), BF16), ((2 * heads, tokens), F32)]


def pair_lanes(ref, quarter, width):
    return ref.at[:, pl.ds(pl.multiple_of(quarter * width, width), width)]


def first_part(code, turns, rate, keys, values, gate_logit, beta_logit):
    heads, tokens = gate_logit.shape
    count = len(turns)

    def kernel(code_ref, rate_hbm, gate_hbm, beta_hbm, k_hbm, v_hbm, *refs):
        ends, (work, marks, rate, gate, beta, k_own, v_own), refs = refs[:count], refs[count : count + 7], refs[count + 7 :]
        k_refs, v_refs, sems = refs[:count], refs[count : 2 * count], refs[-1]
        pair = jnp.bitwise_and(code_ref[0], count)
        quarters = [jnp.bitwise_xor(pair, turn) for turn in turns]
        moves = [(rate_hbm, rate), (gate_hbm, gate), (beta_hbm, beta)]
        moves += [(pair_lanes(k_hbm, q, DK), ref) for q, ref in zip(quarters, k_refs)]
        moves += [(pair_lanes(v_hbm, q, 2 * DV), ref) for q, ref in zip(quarters, v_refs)]
        moves += [(pair_lanes(k_hbm, pair, DK), k_own), (pair_lanes(v_hbm, pair, 2 * DV), v_own)]
        copies = started(moves, sems)
        waits = copies[:3], copies[3 : 3 + count], copies[3 + count : -2]
        delta_kernel(waits, rate, gate, beta, quarters, 0, k_refs, v_refs, ends, work, marks)
        waited(copies[-2:])

    vmem = pltpu.MemorySpace.VMEM
    outs = [(vmem, (2, DK, DV + DK), BF16)] * count
    outs += [(vmem, *shape) for shape in local_shapes(count, tokens, heads)]
    outs += [(vmem, a.shape, a.dtype) for a in (rate, gate_logit, beta_logit)]
    outs += [(vmem, (tokens, DK), BF16), (vmem, (tokens, 2 * DV), BF16)]
    groups = [(pltpu.SMEM, [code]), (pltpu.HBM, [rate, gate_logit, beta_logit, keys, values])]
    scratch = [pltpu.VMEM((tokens, DK), BF16)] * count + [pltpu.VMEM((tokens, 2 * DV), BF16)] * count
    scratch += [pltpu.SemaphoreType.DMA((5 + 2 * count,))]
    result = call(kernel, "first_part", groups, outs, scratch, DELTA_VMEM, 6 * 10**9)
    return result[:count], result[count : count + 2], result[count + 2 :]


def place_code(chip, core, member, members):
    return ((chip * 2 + core) * members + member).reshape(1)


def place_of(code_ref, members):
    code = code_ref[0]
    return code // (2 * members), jnp.bitwise_and(code // members, 1), jnp.bitwise_and(code, members - 1)


def chunk_moves(first, chunks, sources, targets):
    (q_hbm, k_hbm, work, marks), (q, k, work_to, marks_to) = sources, targets
    rows = pl.ds(pl.multiple_of(first * CHUNK, CHUNK), chunks * CHUNK)
    return [
        (q_hbm.at[rows, :], q),
        (k_hbm.at[rows, :], k),
        (marks.at[:, rows], marks_to),
        (work.at[:, pl.ds(first, chunks)], work_to),
    ]


def chunk_shapes(chunks, pairs, width):
    tokens = chunks * CHUNK
    return [((tokens, width), BF16)] * 2 + local_shapes(pairs - 1, tokens, 2 * pairs)


def second_part(code, chunks, operands, earlier, query, keys):
    heads, tokens = operands[1].shape
    near = chunk_shapes(chunks, heads // 2, query.shape[1])

    def kernel(code_ref, q_hbm, k_hbm, rate, gate, beta, k_own, v_own, *refs):
        earlier_refs, (ends, *local), out_hbm, targets, sems = refs[:2], refs[2:5], refs[5:7], refs[7:11], refs[11]
        moves = chunk_moves(code_ref[0] // (heads // 2), chunks, (q_hbm, k_hbm, *earlier_refs), targets)
        copies = started([*moves, *zip(earlier_refs, out_hbm)], sems)
        pair = jnp.bitwise_and(code_ref[0], heads // 2 - 1)
        delta_kernel([[]] * 3, rate, gate, beta, [pair], heads // 2 - 1, [k_own], [v_own], [ends], *local)
        waited(copies)

    vmem = pltpu.MemorySpace.VMEM
    outs = [(vmem, (2, DK, DV + DK), BF16)] + [(vmem, *shape) for shape in local_shapes(1, tokens, heads)]
    outs += [(pltpu.MemorySpace.HBM, a.shape, a.dtype) for a in earlier]
    outs += [(vmem, *shape) for shape in near]
    scratch = [pltpu.SemaphoreType.DMA((6,))]
    groups = [(pltpu.SMEM, [code]), (pltpu.HBM, [query, keys]), (pltpu.VMEM, [*operands, *earlier])]
    ends, work, marks, *rest = call(kernel, "second_part", groups, outs, scratch, DELTA_VMEM, 2 * 10**9)
    return ends, [work, marks], rest[:2], rest[2:]


def third_part(place, turns, chunks, sources, near, own, after):
    count = len(turns) + 1
    tokens = chunks * CHUNK
    heads = 2 * count

    def kernel(code_ref, *refs):
        place_ref = place_of(code_ref, count)
        sources, (own_work, own_marks), (out, gain), scratch = refs[:4], refs[4:6], refs[7:9], refs[9:]
        first = place_ref[0] * chunks
        local, copies = sources, []
        if not near:
            local = scratch[:4]
            copies = started(chunk_moves(first, chunks, sources, local), scratch[4])
            waited(copies[:3])
        q, k, work, marks = local
        quarters = [jnp.bitwise_xor(place_ref[2], turn) for turn in (*turns, 0)]
        q_refs = [pair_lanes(q, quarter, DK) for quarter in quarters]
        k_refs = [pair_lanes(k, quarter, DK) for quarter in quarters]
        own_here = own_marks[:, pl.ds(pl.multiple_of(first * CHUNK, CHUNK), tokens)]
        theirs = iota((heads, tokens), 0) < heads - 2
        cumul = jnp.where(theirs, marks[:heads, :], own_here[:heads])
        logs = jnp.where(theirs, marks[heads:, :], own_here[heads:])

        def read(rows):
            def block(c, a):
                if a < heads - 2:
                    return work[a // 2, c, a % 2, rows, :]
                return own_work[0, first + c, a % 2, rows, :]

            return block

        resid, held = read(slice(0, CHUNK)), read(slice(CHUNK, CHUNK + DK))
        local_outputs(q_refs, k_refs, cumul, logs, copies[3:], resid, held, out, gain)

    outs = [(pltpu.MemorySpace.VMEM, (tokens, heads * DV), BF16)] * 2
    scratch = []
    if not near:
        scratch = [pltpu.VMEM(*shape) for shape in chunk_shapes(chunks, count, sources[0].shape[1])]
        scratch += [pltpu.SemaphoreType.DMA((4,))]
    groups = [(pltpu.SMEM, [place]), (pltpu.VMEM if near else pltpu.HBM, sources), (pltpu.VMEM, own)]
    groups += [(pltpu.HBM, [after])]
    return call(kernel, "third_part", groups, outs, scratch, OUTPUT_VMEM, 3 * 10**9)


def in_order(member, turns, own_ref, other_refs, order_ref):
    order_ref[member] = own_ref[...]
    for turn, ref in zip(turns, other_refs):
        order_ref[jnp.bitwise_xor(member, turn)] = ref[...]


def after_shard(ends, state):
    return mm(ends[:, DV:], state.astype(BF16)) + ends[:, :DV].astype(F32)


def group_part(code, turns, own, others, chained):
    count = len(turns) + 1

    def kernel(code_ref, own_ref, *refs):
        other_refs, (order, ending_ref, *total_refs) = refs[: count - 1], refs[count - 1 :]
        in_order(jnp.bitwise_and(code_ref[0], count - 1), turns, own_ref, other_refs, order)

        @pl.when(code_ref[0] < count)
        def _():
            states = [order[0, h][:, :DV].astype(F32) for h in range(2)]
            for i in range(1, count):
                states = [after_shard(order[i, h], states[h]) for h in range(2)]
            for h in range(2):
                ending_ref[h] = states[h].astype(BF16)
            for total_ref in total_refs:
                for h in range(2):
                    transit = order[0, h][:, DV:]
                    for i in range(1, count):
                        transit = mm(order[i, h][:, DV:], transit).astype(BF16)
                    total_ref[h] = jnp.concatenate([states[h].astype(BF16), transit], axis=1)

        @pl.when(code_ref[0] >= count)
        def _():
            ending_ref[...] = jnp.zeros_like(ending_ref)
            for total_ref in total_refs:
                total_ref[...] = jnp.zeros_like(total_ref)

    vmem = pltpu.MemorySpace.VMEM
    outs = [(vmem, (count, *own.shape), BF16), (vmem, (2, DK, DV), BF16)]
    if chained:
        outs.append((vmem, own.shape, BF16))
    groups = [(pltpu.SMEM, [code]), (pltpu.VMEM, [own, *others])]
    return call(kernel, "group_part", groups, outs, [], SMALL_VMEM, 10**8)


def hop_part(total, came):
    def kernel(total_ref, *refs):
        sum_ref, out_ref = refs[-2:]
        for h in range(2):
            start = refs[0][h]
            for ref in refs[1:-2]:
                start = start + ref[h]
            sum_ref[h] = start
            out_ref[h] = after_shard(total_ref[h], start).astype(BF16)

    outs = [(pltpu.MemorySpace.VMEM, (2, DK, DV), BF16)] * 2
    return call(kernel, "hop_part", [(pltpu.VMEM, [total, *came])], outs, [], SMALL_VMEM, 10**7)


def starts_part(member, turns, order, came, after):
    count = len(turns) + 1

    def kernel(member_ref, order_ref, *refs):
        came_refs, outs, states_ref = refs[: len(came)], refs[len(came) + 1 : -1], refs[-1]
        states = [came_refs[0][h] for h in range(2)]
        for ref in came_refs[1:]:
            states = [states[h] + ref[h] for h in range(2)]
        for i in range(count):
            for h in range(2):
                states_ref[i, h] = states[h].astype(BF16)
            if i < count - 1:
                states = [after_shard(order_ref[i, h], states[h]) for h in range(2)]
        for turn, ref in zip((0, *turns), outs):
            ref[...] = states_ref[jnp.bitwise_xor(member_ref[0], turn)]

    state = (2, DK, DV)
    outs = [(pltpu.MemorySpace.VMEM, state, BF16)] * count
    groups = [(pltpu.SMEM, [member]), (pltpu.VMEM, [order, *came]), (pltpu.VMEM, [after])]
    return call(kernel, "starts_part", groups, outs, [pltpu.VMEM((count, *state), BF16)], SMALL_VMEM, 10**8)


def gates(z, norm):
    halved = 0.5 * z.astype(F32)
    return halved * (1.0 + jnp.tanh(halved)) * norm


def gated_pairs(out, gain, gate, at, first, start_refs):
    pairs = []
    ones = jnp.full((DV, DV), 1.0 / DV, BF16)
    for j, start_ref in enumerate(start_refs):
        parts = []
        for r in range(2):
            cols = slice((2 * j + r) * DV, (2 * j + r + 1) * DV)
            local = slice((2 * (first + j) + r) * DV, (2 * (first + j) + r + 1) * DV)
            rows = [jnp.concatenate([ref[i, local] for i, _ in at], axis=0) for ref in (out, gain)]
            core = rows[0].astype(F32) + mm(rows[1], start_ref[r])
            mean = mm((core * core).astype(BF16), ones)
            weight = jnp.concatenate([gate[i, cols] for _, i in at], axis=0)
            parts.append((core * lax.rsqrt(mean + 1e-6) * weight).astype(BF16))
        pairs.append(jnp.concatenate(parts, axis=1))
    return pairs


def pair_moves(place_ref, turns, z_hbm, w_hbm, z, w):
    rows, width = z.shape[0], 2 * DV
    here = pl.ds(pl.multiple_of(place_ref[0] * rows, rows), rows)
    gates, bands = [], []
    for j, turn in enumerate(turns):
        at = pl.ds(pl.multiple_of(jnp.bitwise_xor(place_ref[2], turn) * width, width), width)
        part = slice(j * width, (j + 1) * width)
        gates.append((z_hbm.at[here, at], z.at[:, part]))
        bands.append((w_hbm.at[at, :], w.at[part, :]))
    return gates + bands


def pair_buffers(count, rows, wide):
    width = 2 * count * DV
    return [((rows, width), BF16), ((width, wide), BF16)]


def core_rows(place_ref, rows, out):
    half = rows // 2
    slices = []
    for core in (1 - place_ref[1], place_ref[1]):
        chip = 0 if out.shape[0] == rows else place_ref[0] * rows
        slices.append([pl.ds(pl.multiple_of(start + core * half, half), half) for start in (chip, 0)])
    return slices


def projected(pairs, w):
    width = 2 * DV
    total = None
    for j, gated in enumerate(pairs):
        term = mm(gated, w[j * width : (j + 1) * width, :])
        total = term if total is None else total + term
    return total


def keep_part(place, turns, rows, gate_z, weight, norm_gain, out, gain, start):
    wide = weight.shape[1]
    count = len(turns)

    def kernel(code_ref, z_hbm, w_hbm, norm_hbm, out, gain, start_ref, sum_ref, gate_ref, w_away, *refs):
        place_ref = place_of(code_ref, count + 1)
        norm, own_gate, z_away, z_own, w_own, sems = refs
        moves = [(norm_hbm, norm)] + pair_moves(place_ref, [0], z_hbm, w_hbm, z_own, w_own)
        copies = started(moves + pair_moves(place_ref, turns, z_hbm, w_hbm, z_away, w_away), sems)
        waited(copies[:2])
        for h in range(2):
            cols = slice(h * DV, (h + 1) * DV)
            own_gate[:, cols] = gates(z_own[:, cols], norm[...])
        pairs = gated_pairs(out, gain, own_gate, core_rows(place_ref, rows, out), count, [start_ref])
        waited(copies[2 : 3 + count])
        for h in range(2 * count):
            cols = slice(h * DV, (h + 1) * DV)
            gate_ref[:, cols] = gates(z_away[:, cols], norm[...])
        sum_ref[...] = projected(pairs, w_own)
        waited(copies[3 + count :])

    vmem = pltpu.MemorySpace.VMEM
    (z_shape, _), (w_shape, _) = pair_buffers(count, rows, wide)
    outs = [(vmem, (rows, wide), F32), (vmem, z_shape, F32), (vmem, w_shape, BF16)]
    scratch = [pltpu.VMEM((1, DV), F32), pltpu.VMEM((rows, 2 * DV), F32), pltpu.VMEM(z_shape, BF16)]
    scratch += [pltpu.VMEM(*shape) for shape in pair_buffers(1, rows, wide)]
    scratch += [pltpu.SemaphoreType.DMA((3 + 2 * count,))]
    groups = [(pltpu.SMEM, [place]), (pltpu.HBM, [gate_z, weight, norm_gain]), (pltpu.VMEM, [out, gain, start])]
    return call(kernel, "keep_part", groups, outs, scratch, PROJECT_VMEM, 4 * rows * DV * wide)


def away_part(place, kept, out, gain, starts):
    rows, wide = kept[0].shape

    def kernel(code_ref, sum_ref, gate, w, out, gain, *refs):
        place_ref = place_of(code_ref, len(starts) + 1)
        start_refs, (send_ref, stay_ref) = refs[:-2], refs[-2:]
        pairs = gated_pairs(out, gain, gate, core_rows(place_ref, rows, out), 0, start_refs)
        partial = projected(pairs, w) + sum_ref[...]
        send_ref[...] = partial[: rows // 2].astype(BF16)
        stay_ref[...] = partial[rows // 2 :]

    vmem = pltpu.MemorySpace.VMEM
    outs = [(vmem, (rows // 2, wide), BF16), (vmem, (rows // 2, wide), F32)]
    groups = [(pltpu.SMEM, [place]), (pltpu.VMEM, [*kept, out, gain, *starts])]
    return call(kernel, "away_part", groups, outs, [], PROJECT_VMEM, 2 * rows * kept[-1].size)


def whole_part(place, turns, rows, gate_z, weight, norm_gain, out, gain, starts):
    wide = weight.shape[1]
    count = len(turns) + 1

    def kernel(code_ref, z_hbm, w_hbm, norm_hbm, out, gain, *refs):
        place_ref = place_of(code_ref, count)
        start_refs, sends, (stay_ref, norm, gate, z, w, sems) = refs[:count], refs[count : count + 2], refs[count + 2 :]
        moves = [(norm_hbm, norm)] + pair_moves(place_ref, (*turns, 0), z_hbm, w_hbm, z, w)
        copies = started(moves, sems)
        waited(copies[: 1 + count])
        for h in range(2 * count):
            cols = slice(h * DV, (h + 1) * DV)
            gate[:, cols] = gates(z[:, cols], norm[...])
        pairs = gated_pairs(out, gain, gate, core_rows(place_ref, rows, out), 0, start_refs)
        waited(copies[1 + count :])
        partial = projected(pairs, w)
        for i, ref in enumerate(sends):
            ref[...] = partial[: rows // 2, i * (wide // 2) : (i + 1) * (wide // 2)].astype(BF16)
        stay_ref[...] = partial[rows // 2 :]

    vmem = pltpu.MemorySpace.VMEM
    outs = [(vmem, (rows // 2, wide // 2), BF16)] * 2 + [(vmem, (rows // 2, wide), F32)]
    (z_shape, _), _ = pair_buffers(count, rows, wide)
    scratch = [pltpu.VMEM((1, DV), F32), pltpu.VMEM(z_shape, F32)]
    scratch += [pltpu.VMEM(*shape) for shape in pair_buffers(count, rows, wide)]
    scratch += [pltpu.SemaphoreType.DMA((1 + 2 * count,))]
    groups = [(pltpu.SMEM, [place]), (pltpu.HBM, [gate_z, weight, norm_gain]), (pltpu.VMEM, [out, gain, *starts])]
    return call(kernel, "whole_part", groups, outs, scratch, PROJECT_VMEM, 2 * rows * weight.size)


def on_device(
    query, keys, values, gate_logit, beta_logit, decay_rate, norm_gain, gate_z, out_weight
):
    shards, cores = lax.axis_size("seq"), lax.axis_size("head")
    seq, head = lax.axis_index("seq"), lax.axis_index("head")
    members = query.shape[1] // DK
    turns = sorted(range(1, members), key=lambda turn: (-bin(turn).count("1"), turn))
    pairs = {turn: [(s, s ^ turn) for s in range(shards)] for turn in turns}
    member_at = lax.rem(seq, members)
    member = member_at.reshape(1)
    rate, norm_gain = decay_rate.reshape(1, -1), norm_gain.reshape(1, -1)

    groups = shards // members
    chips = cores // 2
    chip, core = head // 2, lax.rem(head, 2)
    rows = query.shape[0] // chips
    spots = [place_code(lax.rem(chip + by, chips), core, member_at, members) for by in range(chips)]
    apart = rows == CHUNK and chips == 2
    chunks = 1 if apart else query.shape[0] // CHUNK
    code = (member_at + members * lax.rem(chip + 1, chips)).reshape(1) if apart else member
    spot = spots[1] if apart else place_code(0, core, member_at, members)
    last = (member_at + members * (seq >= shards - members).astype(jnp.int32)).reshape(1)
    code, member, last, spot, *spots = lax.optimization_barrier((code, member, last, spot, *spots))
    away, earlier, operands = first_part(code, turns, rate, keys, values, gate_logit.T, beta_logit.T)
    others = [lax.ppermute(a, "seq", pairs[turn]) for a, turn in zip(away, turns)]
    own, mine, locals_, near = second_part(code, chunks, operands, earlier, query, keys)
    order, ending, *total = group_part(last, turns, own, others, groups > 2)
    out, gain = third_part(spot, turns, chunks, near, True, mine, ending)

    came = []
    for step in range(groups - 1):
        if step:
            start, ending = hop_part(*total, came)
            came = [start]
        along = [(step * members + i, (step + 1) * members + i) for i in range(members)]
        came.append(lax.ppermute(ending, "seq", along))
    if not came:
        came = [jnp.zeros_like(ending)]
    keep, *gives = starts_part(member, turns, order, came, out)
    back = [lax.ppermute(g, "seq", pairs[turn]) for g, turn in zip(gives, turns)]

    swap = [(i, i ^ 1) for i in range(cores)]
    arrived = []
    for by in range(1, chips):
        kept = keep_part(spots[by], turns, rows, gate_z, out_weight, norm_gain, out, gain, keep)
        give, stay = away_part(spots[by], kept, out, gain, back)
        both = (stay + lax.ppermute(give, "head", swap).astype(F32)).astype(BF16)
        arrived.append(lax.ppermute(both, "head", [(i, (i + 2 * by) % cores) for i in range(cores)]))
    spot = spots[0]
    if arrived:
        spot, both = lax.optimization_barrier((spot, both))
    if apart:
        out, gain = third_part(spot, turns, chunks, [query, keys, *locals_], False, mine, ending)
    *gives, stay = whole_part(spot, turns, rows, gate_z, out_weight, norm_gain, out, gain, [*back, keep])
    total = stay + jnp.concatenate([lax.ppermute(g, "head", swap) for g in gives], axis=1).astype(F32)
    for part in arrived:
        total = total + part.astype(F32)
    return total.astype(BF16)


def solution(mesh):
    return jax.shard_map(
        on_device,
        mesh=mesh,
        in_specs=(
            P("seq", "head"),
            P("seq", "head"),
            P("seq", "head"),
            P("seq", "head"),
            P("seq", "head"),
            P("head"),
            P(),
            P("seq", "head"),
            P("head", None),
        ),
        out_specs=P(("seq", "head"), None),
        check_vma=False,
    )
```
